32 devices in a mesh: row: 4 (over y, x), col: 8 (over z, core).
Axes of the slice: x: 2, y: 2, z: 4, core: 2. Of those that a mesh axis runs over, the one named last changes fastest.
Arguments:
- src_cent: float32 [16, 4096], P(None, 'row'), may hold values from -6.5 to 6.5
- tgt_cent: float32 [16, 1024], P(None, 'col'), may hold values from -6.5 to 6.5
- src_mass: float32 [4096], P('row'), may hold values from 6.1035156e-05 to 0.0009765625
- tgt_mass: float32 [1024], P('col'), may hold values from 0.00024414062 to 0.00390625
- src_pts: float32 [16, 65536], P(None, ('row', 'col')), may hold values from -6.5 to 6.5
- tgt_pts: float32 [16, 262144], P(None, ('row', 'col')), may hold values from -6.5 to 6.5
- src_cluster: int32 [65536], P(('row', 'col')), may hold values from 0 to 4095
- tgt_cluster: int32 [262144], P(('row', 'col')), may hold values from 0 to 1023
- support: int32 [256, 16], P(('row', 'col')), may hold values from 0 to 1023, as said below
Outputs:
- coarse_f: float32 [4096], P('row')
- coarse_g: float32 [1024], P('col')
- fine_f: float32 [65536], P(('row', 'col'))
- fine_g: float32 [262144], P(('row', 'col'))
The draws below stay inside these ranges and needn't reach their ends.
Inputs may be any that keep to these rules, and one draw needn't show every extreme that they name: `support`: each row names 16 different target blocks; every target block is named by some row; among the rows of one device (aligned blocks of 8 rows) at most 5 entries fall in any one range k * 32 to (k + 1) * 32 - 1, and exactly 5 in some such range for every device.
All inputs are finite; a program needn't handle non-finite values.
Results may differ from the reference program's by a relative error of at most 0.0003.
Values sent between devices are 32-bit elements; how exact they have to be, the bound alone decides.
No kernel may reach another device: no remote copies, remote signals or barrier semaphores. Data moves between devices by JAX's collectives and lax.ppermute only.
A program may use at most 64 MiB of HBM per device.

```python
import math
import jax
import jax.numpy as jnp
from jax import lax

F = 16
BLK = 256
SUPP = 16
ITERS = 8
SB_DEV = 8
TB_DEV = 32
KS = 4096
KT = 1024
NS = 65536
NT = 262144
DEVICES = 32


def point_cloud(key, rows, cols):
    first = jax.random.fold_in(key, 0)
    base = jnp.clip(jax.random.normal(first, (rows, cols), jnp.float32), -6.0, 6.0)
    return 0.25 * base


def draw_src_cent(key, part):
    return point_cloud(jax.random.fold_in(key, 101), F, KS)


def draw_tgt_cent(key, part):
    return point_cloud(jax.random.fold_in(key, 202), F, KT)


def draw_src_pts(key, part):
    return point_cloud(jax.random.fold_in(key, 303), F, NS)


def draw_tgt_pts(key, part):
    return point_cloud(jax.random.fold_in(key, 404), F, NT)


def draw_support(key, part):
    base_key = jax.random.fold_in(key, 707)
    key_shift, key_score, key_local = jax.random.split(base_key, 3)
    requests_each = SB_DEV * SUPP
    per_owner = requests_each // DEVICES
    slots_each = per_owner + 1
    device_ids = jnp.arange(DEVICES, dtype=jnp.int32)
    offset = jax.random.randint(key_shift, (), 0, DEVICES, dtype=jnp.int32)
    doubled = (device_ids + offset) % DEVICES
    dropped = (doubled + DEVICES // 2) % DEVICES
    counts = per_owner + (device_ids[None, :] == doubled[:, None]).astype(jnp.int32) - (device_ids[None, :] == dropped[:, None]).astype(jnp.int32)
    slot_all = jnp.arange(DEVICES * slots_each, dtype=jnp.int32)
    slot_owner = slot_all // slots_each
    slot_occur = slot_all % slots_each
    valid = slot_occur[None, :] < counts[:, slot_owner]
    scores = jax.random.randint(key_score, (DEVICES, DEVICES * slots_each), 0, 2 ** 19, dtype=jnp.int32) * (DEVICES * slots_each) + slot_all[None, :]
    scores = jnp.where(valid, scores, jnp.int32(2 ** 31 - 1))
    order = jnp.argsort(scores, axis=1, stable=True)[:, :requests_each].astype(jnp.int32)
    owners = order // slots_each
    occurs = order % slots_each
    shifts = jax.random.randint(key_local, (DEVICES,), 0, TB_DEV, dtype=jnp.int32)
    local_ids = (device_ids[:, None] * per_owner + occurs + shifts[owners]) % TB_DEV
    return (owners * TB_DEV + local_ids).reshape(DEVICES * SB_DEV, SUPP)


def place_ends(values, rng, smallest, top_value):
    longest = values.shape.index(max(values.shape))
    spots = []
    for shift in (0, 1):
        where = [jax.random.randint(jax.random.fold_in(rng, axis), (), 0, length) for axis, length in enumerate(values.shape)]
        where[longest] = (where[longest] + shift) % values.shape[longest]
        spots.append(tuple(where))
    return values.at[spots[0]].set(smallest).at[spots[1]].set(top_value)


def levels(stream_key, extent, shards, smallest, largest):
    factor_of, own = 1.0, jax.random.fold_in(stream_key, 6)
    for dim, blocks in shards:
        draws = jnp.exp(jax.random.uniform(jax.random.fold_in(own, dim), (blocks,), jnp.float32, smallest / len(shards), largest / len(shards)))
        factor_of = factor_of * jnp.repeat(draws, extent[dim] // blocks).reshape([-1 if axis == dim else 1 for axis in range(len(extent))])
    return factor_of


def setup_inputs(seed: int = 0) -> dict:
    key_of = jax.random.split(jax.random.key(seed), 10)
    src_cent = draw_src_cent(jax.random.fold_in(key_of[9], 71), 0)
    tgt_cent = draw_tgt_cent(jax.random.fold_in(key_of[9], 71), 0)
    src_mass = jnp.clip(jnp.exp(math.log(0.0009765625) - 2.7725887 * jax.random.uniform(key_of[2], (KS,), jnp.float32) ** levels(key_of[2], (KS,), ((0, 4),), -0.2, 0.2)), 6.103515625e-05, 0.0009765625)
    tgt_mass = jnp.clip(jnp.exp(math.log(0.00390625) - 2.7725887 * jax.random.uniform(key_of[3], (KT,), jnp.float32) ** levels(key_of[3], (KT,), ((0, 8),), -0.2, 0.2)), 0.00024414062, 0.00390625)
    src_pts = draw_src_pts(jax.random.fold_in(key_of[9], 71), 0)
    tgt_pts = draw_tgt_pts(jax.random.fold_in(key_of[9], 71), 0)
    src_cluster = place_ends(jax.random.randint(key_of[6], (NS,), 0, KS), jax.random.fold_in(key_of[6], 1), 0, KS - 1).astype(jnp.int32)
    tgt_cluster = place_ends(jax.random.randint(key_of[7], (NT,), 0, KT), jax.random.fold_in(key_of[7], 1), 0, KT - 1).astype(jnp.int32)
    support = draw_support(jax.random.fold_in(key_of[9], 71), 0)
    return {"src_cent": src_cent, "tgt_cent": tgt_cent, "src_mass": src_mass, "tgt_mass": tgt_mass, "src_pts": src_pts, "tgt_pts": tgt_pts, "src_cluster": src_cluster, "tgt_cluster": tgt_cluster, "support": support}


EPS = 0.1


def pair_cost(left_pts, right_pts):
    cross = jnp.einsum("fi,fj->ij", left_pts, right_pts, precision=lax.Precision.HIGHEST, preferred_element_type=jnp.float32)
    return jnp.sum(left_pts * left_pts, 0)[:, None] + jnp.sum(right_pts * right_pts, 0)[None, :] - 2.0 * cross


def reference(src_cent, tgt_cent, src_mass, tgt_mass, src_pts, tgt_pts, src_cluster, tgt_cluster, support):
    coarse_cost = pair_cost(src_cent, tgt_cent)
    log_src = jnp.log(src_mass)
    log_tgt = jnp.log(tgt_mass)
    coarse_g = jnp.zeros(coarse_cost.shape[1], jnp.float32)
    coarse_f = jnp.zeros(coarse_cost.shape[0], jnp.float32)
    for turn_index in range(ITERS):
        scores = log_tgt[None, :] + (coarse_g[None, :] - coarse_cost) / EPS
        maxima = jnp.max(scores, 1)
        coarse_f = -EPS * (maxima + jnp.log(jnp.sum(jnp.exp(scores - maxima[:, None]), 1)))
        scores = log_src[:, None] + (coarse_f[:, None] - coarse_cost) / EPS
        maxima = jnp.max(scores, 0)
        coarse_g = -EPS * (maxima + jnp.log(jnp.sum(jnp.exp(scores - maxima[None, :]), 0)))
    start_f = coarse_f[src_cluster]
    start_g = coarse_g[tgt_cluster]
    src_count = src_pts.shape[1] // BLK
    tgt_count = tgt_pts.shape[1] // BLK
    src_blocks = src_pts.reshape(F, src_count, BLK).transpose(1, 0, 2)
    tgt_blocks = tgt_pts.reshape(F, tgt_count, BLK).transpose(1, 0, 2)
    start_fb = start_f.reshape(src_count, BLK)
    start_gb = start_g.reshape(tgt_count, BLK)

    def one_block(carry, inputs):
        col_max, col_sum = carry
        src_block, src_dual, block_ids = inputs
        tgt_sel = tgt_blocks[block_ids]
        tgt_dual = start_gb[block_ids]
        cross = jnp.einsum("fi,kfj->ikj", src_block, tgt_sel, precision=lax.Precision.HIGHEST, preferred_element_type=jnp.float32)
        distance = jnp.sum(src_block * src_block, 0)[:, None, None] + jnp.sum(tgt_sel * tgt_sel, 1)[None, :, :] - 2.0 * cross
        scores = (tgt_dual[None, :, :] - distance) / EPS
        row_max = jnp.max(scores, (1, 2))
        row_term = -EPS * (row_max + jnp.log(jnp.sum(jnp.exp(scores - row_max[:, None, None]), (1, 2))) - jnp.log(float(SUPP * BLK)))
        scores = (src_dual[:, None, None] - distance) / EPS
        part_max = jnp.max(scores, 0)
        part_sum = jnp.sum(jnp.exp(scores - part_max[None]), 0)
        old_max = col_max[block_ids]
        new_max = jnp.maximum(old_max, part_max)
        new_sum = col_sum[block_ids] * jnp.exp(old_max - new_max) + part_sum * jnp.exp(part_max - new_max)
        col_max = col_max.at[block_ids].set(new_max)
        col_sum = col_sum.at[block_ids].set(new_sum)
        return (col_max, col_sum), row_term

    init = (jnp.full((tgt_count, BLK), -jnp.inf, jnp.float32), jnp.zeros((tgt_count, BLK), jnp.float32))
    (col_max, col_sum), row_terms = lax.scan(one_block, init, (src_blocks, start_fb, support))
    named = jnp.zeros(tgt_count, jnp.float32).at[support.reshape(-1)].add(jnp.ones(support.size, jnp.float32))
    col_term = -EPS * (col_max + jnp.log(col_sum) - jnp.log(named * BLK)[:, None])
    fine_f = 0.5 * (start_f + row_terms.reshape(-1))
    fine_g = 0.5 * (start_g + col_term.reshape(-1))
    return coarse_f, coarse_g, fine_f, fine_g
```

```python
import functools
import math

import jax
import jax.numpy as jnp
from jax import lax
from jax.experimental import pallas as pl
from jax.experimental.pallas import tpu as pltpu
from jax.sharding import PartitionSpec as P

F = 16
BLK = 256
SUPP = 16
ITERS = 8
SB_DEV = 8
TB_DEV = 32
EPS = 0.1

SCALE = math.log2(math.e) / EPS
KDIM = 7 * F
LANES = 128
ROWS = 256
UNROLL = 2
MIB = 1024 * 1024
AXES = ("row", "col")

VMEM = pl.BlockSpec(memory_space=pltpu.VMEM)
SMEM = pl.BlockSpec(memory_space=pltpu.SMEM)
CONTRACT_FIRST = (((0,), (0,)), ((), ()))


def split3(x):
    first = x.astype(jnp.bfloat16)
    rest = x - first.astype(jnp.float32)
    second = rest.astype(jnp.bfloat16)
    rest = rest - second.astype(jnp.float32)
    return first, second, rest.astype(jnp.bfloat16)


def constant_rows(values, at, ones_at):
    width = values.shape[1]
    parts = split3(jnp.broadcast_to(values, (F, width)))
    row = lax.broadcasted_iota(jnp.int32, (F, width), 0)
    rows = jnp.zeros((F, width), jnp.float32)
    for k, part in enumerate(parts):
        rows = jnp.where(row == at + k, part.astype(jnp.float32), rows)
    if ones_at is not None:
        rows = jnp.where((row >= ones_at) & (row < ones_at + 3), 1.0, rows)
    return rows.astype(jnp.bfloat16)


def pack_left(x, constant):
    a, b, c = split3(x * (2.0 * SCALE))
    return jnp.concatenate([a, a, b, b, a, c, constant_rows(constant, 0, 3)], 0)


def pack_right(y, constant):
    a, b, c = split3(y)
    return jnp.concatenate([a, b, a, b, c, a, constant_rows(constant, 3, 0)], 0)


def contract(left, right):
    return lax.dot_general(left, right, CONTRACT_FIRST, preferred_element_type=jnp.float32)


def square_norm(x):
    return jnp.sum(x * x, 0, keepdims=True)


def fold(values, combine):
    out = values[0:8]
    for k in range(1, values.shape[0] // 8):
        out = combine(out, values[8 * k : 8 * k + 8])
    return out


def coarse_kernel(n_src, n_tgt, stored, *refs):
    src = refs[:n_src]
    tgt = refs[n_src : n_src + n_tgt]
    f_out, g_out, scores, mass, dual = refs[n_src + n_tgt :]
    ks, kt = f_out.shape[1], g_out.shape[1]
    piece = src[0].shape[1]
    tiles = kt // LANES
    y = jnp.concatenate([ref[0:F, :] for ref in tgt], 1)
    log_b = jnp.log2(jnp.concatenate([ref[F : F + 1, :] for ref in tgt], 1))
    right = pack_right(y, log_b - SCALE * square_norm(y))
    ones = jnp.ones((F, LANES), jnp.bfloat16)

    def left_of(s, k):
        span = pl.ds(pl.multiple_of(k * ROWS, ROWS), ROWS)
        x = src[s][0:F, span]
        return pack_left(x, -SCALE * square_norm(x))

    def over_chunks(body, carry):
        for s in range(n_src):

            def chunk(k, carry, s=s):
                base = pl.multiple_of(s * piece + k * ROWS, ROWS)
                return body(s, k, pl.ds(base, ROWS), carry)

            carry = lax.fori_loop(0, piece // ROWS, chunk, carry)
        return carry

    def begin(s, k, rows, largest):
        span = pl.ds(pl.multiple_of(k * ROWS, ROWS), ROWS)
        z = contract(left_of(s, k), right)
        parts = constant_rows(src[s][F : F + 1, span], 0, None)
        mass[rows, :] = contract(parts, ones)
        top = jnp.max(z, 1, keepdims=True)
        f = -(top + jnp.log2(jnp.sum(jnp.exp2(z - top), 1, keepdims=True)))
        z = z + f
        if stored:
            scores[rows, :] = z
        dual[rows, :] = jnp.broadcast_to(f, (ROWS, LANES))
        return jnp.maximum(largest, fold(z, jnp.maximum))

    def read(s, k, rows):
        if stored:
            return scores[rows, :]
        return contract(left_of(s, k), right) + jnp.tile(dual[rows, :], (1, tiles))

    largest = over_chunks(begin, jnp.full((8, kt), -jnp.inf, jnp.float32))
    largest = jnp.max(largest, 0, keepdims=True)
    zero = jnp.zeros((8, kt), jnp.float32)

    def first(s, k, rows, total):
        e = jnp.exp2(read(s, k, rows) - largest)
        return total + fold(e * jnp.tile(mass[rows, :], (1, tiles)), jnp.add)

    total = over_chunks(first, zero)
    g = log_b - (largest + jnp.log2(jnp.sum(total, 0, keepdims=True)))

    def sweep(g, rebase):
        def step(s, k, rows, total):
            z = read(s, k, rows)
            e = jnp.exp2(z + g)
            row_sum = jnp.sum(e, 1, keepdims=True)
            weight = mass[rows, :] / row_sum
            if rebase:
                shift = jnp.log2(row_sum)
                if stored:
                    scores[rows, :] = z - shift
                dual[rows, :] = dual[rows, :] - shift
            return total + fold(e * jnp.tile(weight, (1, tiles)), jnp.add)

        total = over_chunks(step, zero)
        return g + (log_b - jnp.log2(jnp.sum(total, 0, keepdims=True)))

    half = ITERS // 2
    g = lax.fori_loop(0, half - 1, lambda _, g: sweep(g, False), g)
    g = sweep(g, True)
    g = lax.fori_loop(0, ITERS - half - 2, lambda _, g: sweep(g, False), g)
    g = sweep(g, True)
    g_out[...] = g * (1.0 / SCALE)
    diagonal = lax.broadcasted_iota(jnp.int32, (LANES, LANES), 0) == lax.broadcasted_iota(
        jnp.int32, (LANES, LANES), 1
    )

    def to_lanes(k, carry):
        span = pl.ds(pl.multiple_of(k * LANES, LANES), LANES)
        picked = jnp.sum(jnp.where(diagonal, dual[span, :], 0.0), 0, keepdims=True)
        f_out[:, span] = picked * (1.0 / SCALE)
        return carry

    lax.fori_loop(0, ks // LANES, to_lanes, 0)


def coarse_duals(src, tgt):
    ks = sum(part.shape[1] for part in src)
    kt = sum(part.shape[1] for part in tgt)
    stored = ks * kt * 4 <= 16 * MIB
    return pl.pallas_call(
        functools.partial(coarse_kernel, len(src), len(tgt), stored),
        out_shape=(
            jax.ShapeDtypeStruct((1, ks), jnp.float32),
            jax.ShapeDtypeStruct((1, kt), jnp.float32),
        ),
        in_specs=[VMEM] * (len(src) + len(tgt)),
        out_specs=(VMEM, VMEM),
        scratch_shapes=[
            pltpu.VMEM((ks, kt) if stored else (8, LANES), jnp.float32),
            pltpu.VMEM((ks, LANES), jnp.float32),
            pltpu.VMEM((ks, LANES), jnp.float32),
        ],
        compiler_params=pltpu.CompilerParams(vmem_limit_bytes=48 * MIB),
        cost_estimate=pl.CostEstimate(
            flops=40 * ks * kt, bytes_accessed=4 * 24 * (ks + kt), transcendentals=9 * ks * kt
        ),
        name="coarse",
    )(*src, *tgt)


def look_up(table_ref, index):
    low = index & (LANES - 1)
    high = index >> 7
    out = jnp.zeros(index.shape, jnp.float32)
    for h in range(table_ref.shape[1] // LANES):
        row = jnp.broadcast_to(table_ref[0:1, h * LANES : (h + 1) * LANES], index.shape)
        out = jnp.where(high == h, jnp.take_along_axis(row, low, axis=1), out)
    return out


def fine_kernel(
    slots_each,
    slot_ref,
    where_ref,
    bundle,
    tgt_pts,
    tgt_cluster,
    f_table,
    g_table,
    partial_out,
    start_f_out,
    fine_g_out,
    start_f,
    start_g,
    packed,
    col_top,
    col_sum,
    col_count,
    scores_a,
    scores_b,
    order,
):
    devices = bundle.shape[0]
    me, src_flip, tgt_flip = where_ref[0], where_ref[1], where_ref[2]

    def starting_f(d, carry):
        index = bundle[d, 2 * BLK // 2 : 2 * BLK // 2 + F, :].astype(jnp.int32) ^ src_flip
        for half in range(2):
            start_f[d, 8 * half : 8 * half + 8, :] = look_up(f_table, index[8 * half : 8 * half + 8])
        return carry

    lax.fori_loop(0, devices, starting_f, 0)
    start_f_out[...] = start_f[me]
    for k in range(2 * TB_DEV // 8):
        index = tgt_cluster[8 * k : 8 * k + 8, :] ^ tgt_flip
        start_g[8 * k : 8 * k + 8, :] = look_up(g_table, index)

    def pack_target(t, carry):
        y = tgt_pts[:, pl.ds(pl.multiple_of(t * BLK, BLK), BLK)]
        g = jnp.concatenate([start_g[pl.ds(2 * t, 1), :], start_g[pl.ds(2 * t + 1, 1), :]], 1)
        packed[t] = pack_right(y, SCALE * (g - square_norm(y)))
        return carry

    lax.fori_loop(0, TB_DEV, pack_target, 0)
    packed[TB_DEV] = jnp.zeros((KDIM, BLK), jnp.bfloat16)
    col_top[...] = jnp.full(col_top.shape, -jnp.inf, jnp.float32)
    col_sum[...] = jnp.zeros(col_sum.shape, jnp.float32)
    col_count[...] = jnp.zeros(col_count.shape, jnp.float32)

    total = devices * slots_each

    def place(p, carry):
        used, unused = carry
        valid = slot_ref[p] > 0
        order[jnp.where(valid, used, unused)] = p
        step = valid.astype(jnp.int32)
        return used + step, unused - (1 - step)

    used, _ = lax.fori_loop(0, total, place, (jnp.int32(0), jnp.int32(total - 1)))

    def pair(p, scores):
        code = slot_ref[p] - 1
        valid = code >= 0
        block = jnp.where(valid, code // TB_DEV, 0)
        t = jnp.where(valid, code % TB_DEV, TB_DEV)
        d = p // slots_each
        tile = [
            [
                bundle[d, pl.ds(pl.multiple_of(half * 128 + 16 * block + 8 * k, 8), 8), :]
                for k in range(2)
            ]
            for half in range(2)
        ]
        x = jnp.concatenate([jnp.concatenate(row, 1) for row in tile], 0)
        f = jnp.concatenate(
            [start_f[d, pl.ds(2 * block + k, 1), :] for k in range(2)], 1
        )
        left = pack_left(x, SCALE * (f - square_norm(x)))
        right = packed[t]
        scores[0] = contract(left, right)
        scores[1] = contract(right, left)
        z = scores[0]
        top = jnp.max(z, 0, keepdims=True)
        mass = jnp.sum(jnp.exp2(z - top), 0, keepdims=True)
        for k in range(2):
            span = slice(k * LANES, (k + 1) * LANES)
            row = pl.ds(2 * t + k, 1)
            old = col_top[row, :]
            new = jnp.maximum(old, top[:, span])
            col_sum[row, :] = col_sum[row, :] * jnp.exp2(old - new) + mass[:, span] * jnp.exp2(
                top[:, span] - new
            )
            col_top[row, :] = new
            col_count[row, :] = col_count[row, :] + 1.0
        z = scores[1]
        top = jnp.max(z, 0, keepdims=True)
        mass = jnp.sum(jnp.exp2(z - top), 0, keepdims=True)
        partial_out[d, pl.ds(p % slots_each, 1), :] = top + jnp.log2(mass) - SCALE * f

    def pairs(n, carry):
        pair(order[UNROLL * n], scores_a)
        pair(order[UNROLL * n + 1], scores_b)
        return carry

    lax.fori_loop(0, (used + UNROLL - 1) // UNROLL, pairs, 0)
    rows = slice(0, 2 * TB_DEV)
    g = start_g[...]
    lse = (col_top[rows, :] + jnp.log2(col_sum[rows, :])) * (1.0 / SCALE) - g
    term = EPS * jnp.log(col_count[rows, :] * float(BLK)) - lse
    fine_g_out[...] = 0.5 * (g + term)


def fine_update(slots, where, bundle, tgt_pts, tgt_cluster, f_table, g_table, slots_each):
    devices = bundle.shape[0]
    return pl.pallas_call(
        functools.partial(fine_kernel, slots_each),
        out_shape=(
            jax.ShapeDtypeStruct((devices, slots_each, BLK), jnp.float32),
            jax.ShapeDtypeStruct((F, LANES), jnp.float32),
            jax.ShapeDtypeStruct((2 * TB_DEV, LANES), jnp.float32),
        ),
        in_specs=[SMEM, SMEM] + [VMEM] * 5,
        out_specs=(VMEM, VMEM, VMEM),
        scratch_shapes=[
            pltpu.VMEM((devices, F, LANES), jnp.float32),
            pltpu.VMEM((2 * TB_DEV, LANES), jnp.float32),
            pltpu.VMEM((TB_DEV + 1, KDIM, BLK), jnp.bfloat16),
            pltpu.VMEM((2 * TB_DEV + 8, LANES), jnp.float32),
            pltpu.VMEM((2 * TB_DEV + 8, LANES), jnp.float32),
            pltpu.VMEM((2 * TB_DEV + 8, LANES), jnp.float32),
            pltpu.VMEM((2, BLK, BLK), jnp.float32),
            pltpu.VMEM((2, BLK, BLK), jnp.float32),
            pltpu.SMEM((devices * slots_each,), jnp.int32),
        ],
        compiler_params=pltpu.CompilerParams(vmem_limit_bytes=48 * MIB),
        name="fine",
    )(slots, where, bundle, tgt_pts, tgt_cluster, f_table, g_table)


def finish_kernel(slots_each, slot_ref, partial, start_f, fine_f_out, gathered):
    for block in range(SB_DEV):
        for k in range(SUPP):
            slot = slot_ref[block * SUPP + k]
            gathered[k, block : block + 1, :] = partial[
                slot // slots_each, pl.ds(slot % slots_each, 1), :
            ]
    values = gathered[...]
    top = jnp.max(values, 0)
    lse = top + jnp.log2(jnp.sum(jnp.exp2(values - top[None]), 0))
    term = EPS * math.log(float(SUPP * BLK)) - lse * (1.0 / SCALE)
    for block in range(SB_DEV):
        for k in range(2):
            row = slice(2 * block + k, 2 * block + k + 1)
            piece = term[block : block + 1, k * LANES : (k + 1) * LANES]
            fine_f_out[row, :] = 0.5 * (start_f[row, :] + piece)


def finish(slot_ids, partial, start_f, slots_each):
    return pl.pallas_call(
        functools.partial(finish_kernel, slots_each),
        out_shape=jax.ShapeDtypeStruct((F, LANES), jnp.float32),
        in_specs=[SMEM, VMEM, VMEM],
        out_specs=VMEM,
        scratch_shapes=[pltpu.VMEM((SUPP, SB_DEV, BLK), jnp.float32)],
        name="finish",
    )(slot_ids, partial, start_f)


def exchange(x, axis, flip):
    count = lax.axis_size(axis)
    return lax.ppermute(x, axis, [(i, i ^ flip) for i in range(count)])


def on_device(
    src_cent, tgt_cent, src_mass, tgt_mass, src_pts, tgt_pts, src_cluster, tgt_cluster, support
):
    n_row, n_col = lax.axis_size("row"), lax.axis_size("col")
    devices = n_row * n_col
    row, col = lax.axis_index("row"), lax.axis_index("col")
    me = row * n_col + col

    requests_each = SB_DEV * SUPP
    slots_each = requests_each // devices + 1
    wanted = support.reshape(-1)
    owners = wanted // TB_DEV
    positions = jnp.arange(requests_each, dtype=jnp.int32)
    earlier = (owners[None, :] == owners[:, None]) & (positions[None, :] < positions[:, None])
    slot_ids = owners * slots_each + jnp.sum(earlier.astype(jnp.int32), 1)
    codes = (positions // SUPP) * TB_DEV + wanted % TB_DEV + 1
    width = -(-devices * slots_each // LANES) * LANES
    table = jnp.sum(
        jnp.where(slot_ids[None, :] == jnp.arange(width, dtype=jnp.int32)[:, None], codes[None, :], 0), 1
    )
    tiles = src_pts.reshape(2, 8, F, LANES).transpose(0, 2, 1, 3).reshape(2 * BLK // 2, LANES)
    table = jnp.pad(table.reshape(-1, LANES), ((0, -(width // LANES) % 8), (0, 0)))
    bundle = jnp.concatenate(
        [tiles, src_cluster.reshape(F, LANES).astype(jnp.float32), table.astype(jnp.float32)], 0
    )
    bundles = lax.all_gather(bundle, AXES)

    src_own = jnp.concatenate([src_cent, src_mass[None]], 0)
    tgt_own = jnp.concatenate([tgt_cent, tgt_mass[None]], 0)
    tgt_pair = jnp.concatenate([tgt_own, exchange(tgt_own, "col", 1)], 1)
    src_all = [src_own] + [exchange(src_own, "row", k) for k in range(1, n_row)]
    tgt_all = [tgt_pair] + [exchange(tgt_pair, "col", k) for k in range(2, n_col, 2)]
    f_table, g_table = coarse_duals(src_all, tgt_all)
    coarse_f = f_table[0, : src_cent.shape[1]]
    coarse_g = g_table[0, : tgt_cent.shape[1]]

    slots = bundles[:, 2 * BLK // 2 + F :, :].reshape(devices, -1)
    slots = lax.dynamic_slice_in_dim(slots, me * slots_each, slots_each, 1)
    slots = slots.reshape(-1).astype(jnp.int32)
    where = jnp.stack([me, row * src_cent.shape[1], col * tgt_cent.shape[1]]).astype(jnp.int32)
    partial, start_f, fine_g = fine_update(
        slots,
        where,
        bundles,
        tgt_pts,
        tgt_cluster.reshape(2 * TB_DEV, LANES),
        f_table,
        g_table,
        slots_each,
    )
    returned = lax.all_to_all(partial, AXES, split_axis=0, concat_axis=0, tiled=True)
    fine_f = finish(slot_ids, returned, start_f, slots_each)
    return coarse_f, coarse_g, fine_f.reshape(-1), fine_g.reshape(-1)


def solution(mesh):
    in_specs = (
        P(None, "row"),
        P(None, "col"),
        P("row"),
        P("col"),
        P(None, AXES),
        P(None, AXES),
        P(AXES),
        P(AXES),
        P(AXES, None),
    )
    out_specs = (P("row"), P("col"), P(AXES), P(AXES))
    return jax.shard_map(
        on_device, mesh=mesh, in_specs=in_specs, out_specs=out_specs, check_vma=False
    )
```

```python
import functools
import math

import jax
import jax.numpy as jnp
from jax import lax
from jax.experimental import pallas as pl
from jax.experimental.pallas import tpu as pltpu
from jax.sharding import PartitionSpec as P

F = 16
BLK = 256
SUPP = 16
ITERS = 8
SB_DEV = 8
TB_DEV = 32
EPS = 0.1

SCALE = math.log2(math.e) / EPS
KDIM = 7 * F
LANES = 128
ROWS = 256
ROWS_PRODUCT = 1024
ROWS_BEGIN = 1024
ROWS_TURN = 512
PAIRS = 16
BLOCKS = 8
LOW = 2.0**-30
SMALL = 2.0**-80
LARGE = 2.0**100
MIB = 1024 * 1024
AXES = ("row", "col")

VMEM = pl.BlockSpec(memory_space=pltpu.VMEM)
SMEM = pl.BlockSpec(memory_space=pltpu.SMEM)
CONTRACT_FIRST = (((0,), (0,)), ((), ()))


def split3(x):
    first = x.astype(jnp.bfloat16)
    rest = x - first.astype(jnp.float32)
    second = rest.astype(jnp.bfloat16)
    rest = rest - second.astype(jnp.float32)
    return first, second, rest.astype(jnp.bfloat16)


def constant_rows(values, at, ones_at):
    width = values.shape[1]
    parts = split3(jnp.broadcast_to(values, (F, width)))
    row = lax.broadcasted_iota(jnp.int32, (F, width), 0)
    rows = jnp.zeros((F, width), jnp.float32)
    for k, part in enumerate(parts):
        rows = jnp.where(row == at + k, part.astype(jnp.float32), rows)
    if ones_at is not None:
        rows = jnp.where((row >= ones_at) & (row < ones_at + 3), 1.0, rows)
    return rows.astype(jnp.bfloat16)


def pack_left(x, constant):
    a, b, c = split3(x * (2.0 * SCALE))
    return jnp.concatenate([a, a, b, b, a, c, constant_rows(constant, 0, 3)], 0)


def pack_right(y, constant):
    a, b, c = split3(y)
    return jnp.concatenate([a, b, a, b, c, a, constant_rows(constant, 3, 0)], 0)


def contract(left, right):
    return lax.dot_general(left, right, CONTRACT_FIRST, preferred_element_type=jnp.float32)


def square_norm(x):
    return jnp.sum(x * x, 0, keepdims=True)


def fold(values, combine):
    out = values[0:8]
    for k in range(1, values.shape[0] // 8):
        out = combine(out, values[8 * k : 8 * k + 8])
    return out


def coarse_kernel(n_src, n_tgt, stored, *refs):
    src = refs[:n_src]
    tgt = refs[n_src : n_src + n_tgt]
    f_out, g_out, kernel, mass, dual, sums = refs[n_src + n_tgt :]
    ks, kt = f_out.shape[1], g_out.shape[1]
    piece = src[0].shape[1]
    tiles = kt // LANES
    y = jnp.concatenate([ref[0:F, :] for ref in tgt], 1)
    b = jnp.concatenate([ref[F : F + 1, :] for ref in tgt], 1)
    right = pack_right(y, jnp.log2(b) - SCALE * square_norm(y))
    ones = jnp.ones((F, LANES), jnp.bfloat16)
    zero = jnp.zeros((8, kt), jnp.float32)
    high = jnp.full((8, LANES), jnp.inf, jnp.float32)

    def wide(values):
        return jnp.tile(values, (1, tiles))

    def over_sources(size, body, carry):
        for s in range(n_src):

            def chunk(k, carry, s=s):
                span = pl.ds(pl.multiple_of(k * size, size), size)
                rows = pl.ds(pl.multiple_of(s * piece + k * size, size), size)
                x = src[s][0:F, span]
                left = pack_left(x, -SCALE * square_norm(x))
                return body(src[s][F : F + 1, span], rows, left, carry)

            carry = lax.fori_loop(0, piece // size, chunk, carry)
        return carry

    def over_rows(size, body, carry):
        def chunk(k, carry):
            return body(pl.ds(pl.multiple_of(k * size, size), size), carry)

        return lax.fori_loop(0, ks // size, chunk, carry)

    def weigh(e, weighted, rows, carry):
        total, least = carry
        row_sum = jnp.broadcast_to(jnp.sum(weighted, 1, keepdims=True), (e.shape[0], LANES))
        sums[rows, :] = row_sum
        weight = mass[rows, :] / row_sum
        return total + fold(e * wide(weight), jnp.add), jnp.minimum(least, fold(row_sum, jnp.minimum))

    def close(total, least):
        total = jnp.sum(total, 0, keepdims=True)
        small = jnp.minimum(jnp.min(total), jnp.min(least)) < LOW
        return b / total, small.astype(jnp.int32)

    def spread_mass(values, rows, left, carry):
        mass[rows, :] = contract(constant_rows(values, 0, None), ones)
        if stored:
            kernel[rows, :] = contract(left, right)
        return carry

    over_sources(ROWS_PRODUCT, spread_mass, 0)

    def begin_rows(z, rows, carry):
        top = jnp.max(z, 1, keepdims=True)
        dual[rows, :] = jnp.broadcast_to(-top, (z.shape[0], LANES))
        e = jnp.exp2(z - top)
        if stored:
            kernel[rows, :] = e
        return weigh(e, e, rows, carry)

    if stored:
        carry = over_rows(ROWS_BEGIN, lambda rows, c: begin_rows(kernel[rows, :], rows, c), (zero, high))
    else:
        carry = over_sources(ROWS, lambda _, rows, left, c: begin_rows(contract(left, right), rows, c), (zero, high))
    scale, small = close(*carry)
    base = jnp.zeros((1, kt), jnp.float32)

    def rescue(base, scale):
        def rebase(rows, carry):
            dual[rows, :] = dual[rows, :] - jnp.log2(sums[rows, :])
            return carry

        over_rows(ROWS, rebase, 0)

        def tops(_, rows, left, top):
            return jnp.maximum(top, fold(contract(left, right) + wide(dual[rows, :]), jnp.maximum))

        top = jnp.max(over_sources(ROWS, tops, zero - jnp.inf), 0, keepdims=True)

        def step(_, rows, left, total):
            e = jnp.exp2(contract(left, right) + wide(dual[rows, :]) - top)
            return total + fold(e * wide(mass[rows, :]), jnp.add)

        total = jnp.sum(over_sources(ROWS, step, zero), 0, keepdims=True)
        over_rows(ROWS, unit, 0)
        return jnp.log2(b) - (top + jnp.log2(total)), jnp.ones_like(scale)

    def unit(rows, carry):
        sums[rows, :] = jnp.ones((ROWS, LANES), jnp.float32)
        return carry

    base, scale = lax.cond(small > 0, rescue, lambda base, scale: (base, scale), base, scale)

    def renew(base, scale):
        base = base + jnp.log2(scale)

        def step(_, rows, left, carry):
            f = dual[rows, :] - jnp.log2(sums[rows, :])
            dual[rows, :] = f
            e = jnp.exp2(contract(left, right) + wide(f) + base)
            if stored:
                kernel[rows, :] = e
            return weigh(e, e, rows, carry)

        scale, small = close(*over_sources(ROWS, step, (zero, high)))
        return base, scale, small

    def reuse(base, scale):
        def step(rows, carry):
            e = kernel[rows, :]
            return weigh(e, e * scale, rows, carry)

        scale, small = close(*over_rows(ROWS_TURN, step, (zero, high)))
        return base, scale, small

    def turn(_, state):
        base, scale, small = state
        if not stored:
            return renew(base, scale)
        return lax.cond(small > 0, renew, reuse, base, scale)

    base, scale, small = lax.fori_loop(1, ITERS, turn, (base, scale, small))
    g_out[...] = (base + jnp.log2(scale)) * (1.0 / SCALE)
    diagonal = lax.broadcasted_iota(jnp.int32, (LANES, LANES), 0) == lax.broadcasted_iota(
        jnp.int32, (LANES, LANES), 1
    )

    def to_lanes(k, carry):
        span = pl.ds(pl.multiple_of(k * LANES, LANES), LANES)
        f = dual[span, :] - jnp.log2(sums[span, :])
        f_out[:, span] = jnp.sum(jnp.where(diagonal, f, 0.0), 0, keepdims=True) * (1.0 / SCALE)
        return carry

    lax.fori_loop(0, ks // LANES, to_lanes, 0)

def coarse_duals(src, tgt):
    ks = sum(part.shape[1] for part in src)
    kt = sum(part.shape[1] for part in tgt)
    stored = ks * kt * 4 <= 16 * MIB
    return pl.pallas_call(
        functools.partial(coarse_kernel, len(src), len(tgt), stored),
        out_shape=(
            jax.ShapeDtypeStruct((1, ks), jnp.float32),
            jax.ShapeDtypeStruct((1, kt), jnp.float32),
        ),
        in_specs=[VMEM] * (len(src) + len(tgt)),
        out_specs=(VMEM, VMEM),
        scratch_shapes=[
            pltpu.VMEM((ks, kt) if stored else (8, LANES), jnp.float32),
            pltpu.VMEM((ks, LANES), jnp.float32),
            pltpu.VMEM((ks, LANES), jnp.float32),
            pltpu.VMEM((ks, LANES), jnp.float32),
        ],
        compiler_params=pltpu.CompilerParams(vmem_limit_bytes=48 * MIB),
        cost_estimate=pl.CostEstimate(
            flops=40 * ks * kt, bytes_accessed=4 * 24 * (ks + kt), transcendentals=9 * ks * kt
        ),
        name="coarse",
    )(*src, *tgt)


def look_up(table_ref, index):
    low = index & (LANES - 1)
    high = index >> 7
    out = jnp.zeros(index.shape, jnp.float32)
    for h in range(table_ref.shape[1] // LANES):
        row = jnp.broadcast_to(table_ref[0:1, h * LANES : (h + 1) * LANES], index.shape)
        out = jnp.where(high == h, jnp.take_along_axis(row, low, axis=1), out)
    return out


def fine_kernel(slots_each, slot_ref, where_ref, bundle, tgt_pts, tgt_cluster, f_table, g_table,
    partial_out, start_f_out, fine_g_out,
    start_g, packed, col_sum, col_top, order, count):
    devices = bundle.shape[0]
    me, src_flip, tgt_flip = where_ref[0], where_ref[1], where_ref[2]

    index = bundle[me, 2 * LANES : 2 * LANES + F, :].astype(jnp.int32) ^ src_flip
    for half in range(2):
        rows = slice(8 * half, 8 * half + 8)
        start_f_out[rows, :] = look_up(f_table, index[rows])
    for k in range(2 * TB_DEV // 8):
        index = tgt_cluster[8 * k : 8 * k + 8, :] ^ tgt_flip
        start_g[8 * k : 8 * k + 8, :] = look_up(g_table, index)

    def pack_target(t, carry):
        y = tgt_pts[:, pl.ds(pl.multiple_of(t * BLK, BLK), BLK)]
        g = jnp.concatenate([start_g[pl.ds(2 * t, 1), :], start_g[pl.ds(2 * t + 1, 1), :]], 1)
        rows = pack_right(y, SCALE * (g - square_norm(y)))
        rows = jnp.concatenate([rows, jnp.zeros((LANES - KDIM, BLK), jnp.bfloat16)], 0)
        packed[t] = jnp.transpose(rows.astype(jnp.float32)).astype(jnp.bfloat16)
        count[t] = 0
        return carry

    lax.fori_loop(0, TB_DEV, pack_target, 0, unroll=BLOCKS)
    packed[TB_DEV] = jnp.zeros((BLK, LANES), jnp.bfloat16)
    count[TB_DEV] = 0

    total = devices * slots_each
    unroll = math.gcd(PAIRS, total)

    def place(p, carry):
        used, unused = carry
        code = slot_ref[p]
        valid = code > 0
        order[jnp.where(valid, used, unused)] = p
        t = jnp.where(valid, (code - 1) % TB_DEV, TB_DEV)
        count[t] = count[t] + 1
        step = valid.astype(jnp.int32)
        return used + step, unused - (1 - step)

    used, _ = lax.fori_loop(0, total, place, (jnp.int32(0), jnp.int32(total - 1)), unroll=16)

    def cluster_rows(p):
        code = slot_ref[p] - 1
        block = jnp.where(code >= 0, code // TB_DEV, 0)
        d = p // slots_each
        return [bundle[d, pl.ds(2 * LANES + 2 * block + k, 1), :] for k in range(2)]

    def starts(ps):
        out = []
        for n in range(0, len(ps), 4):
            rows = jnp.concatenate([r for p in ps[n:n+4] for r in cluster_rows(p)], 0)
            f = look_up(f_table, rows.astype(jnp.int32) ^ src_flip)
            for m in range(len(ps[n:n+4])):
                out.append(jnp.concatenate([f[2*m:2*m+1], f[2*m+1:2*m+2]], 1))
        return out

    def product(p, f):
        code = slot_ref[p] - 1
        valid = code >= 0
        block = jnp.where(valid, code // TB_DEV, 0)
        t = jnp.where(valid, code % TB_DEV, TB_DEV)
        d = p // slots_each
        tile = [[bundle[d, pl.ds(pl.multiple_of(half * LANES + 16 * block + 8 * k, 8), 8), :] for k in range(2)] for half in range(2)]
        x = jnp.concatenate([jnp.concatenate(row, 1) for row in tile], 0)
        left = pack_left(x, SCALE * (f - square_norm(x)))
        left = jnp.concatenate([left, jnp.zeros((LANES - KDIM, BLK), jnp.bfloat16)], 0)
        z = jnp.dot(packed[t], left, preferred_element_type=jnp.float32)
        return t, d, SCALE * f, z

    def put(p, d, value):
        partial_out[d, pl.ds(p % slots_each, 1), :] = value

    def fill(ref, value):
        def body(t, carry):
            ref[t] = jnp.full(ref.shape[1:], value, jnp.float32)
            return carry
        lax.fori_loop(0, ref.shape[0], body, 0)

    def pair(p, f, least, most):
        t, d, f, z = product(p, f)
        e = jnp.exp2(z)
        row = fold(e, jnp.add)
        col_sum[t] = col_sum[t] + (e[:, :LANES] + e[:, LANES:])
        row = jnp.sum(row, 0, keepdims=True)
        put(p, d, jnp.log2(row) - f)
        return jnp.minimum(least, row), jnp.maximum(most, row)

    def pairs(n, carry):
        ps = [order[unroll * n + u] for u in range(unroll)]
        fs = starts(ps)
        for u in range(unroll):
            carry = pair(ps[u], fs[u], *carry)
        return carry

    def lanes(t, carry):
        least, most = carry
        g = start_g[pl.ds(pl.multiple_of(2 * t, 2), 2), :]
        halves = []
        for k in range(2):
            block = col_sum[t, k * LANES : (k + 1) * LANES, :]
            halves.append(jnp.sum(jnp.transpose(block), 0, keepdims=True))
        s = jnp.concatenate(halves, 0)
        named = jnp.full((2, LANES), count[t].astype(jnp.float32) * float(BLK))
        term = EPS * jnp.log(named) - (jnp.log2(s) * (1.0 / SCALE) - g)
        fine_g_out[pl.ds(pl.multiple_of(2 * t, 2), 2), :] = 0.5 * (g + term)
        return jnp.minimum(least, s), jnp.maximum(most, s)

    fill(col_sum, 0.0)
    least = jnp.full((1, BLK), jnp.inf, jnp.float32)
    least, most = lax.fori_loop(0, (used + unroll - 1) // unroll, pairs, (least, jnp.zeros((1, BLK), jnp.float32)))
    low, high = jnp.full((2, LANES), jnp.inf, jnp.float32), jnp.zeros((2, LANES), jnp.float32)
    low, high = lax.fori_loop(0, TB_DEV, lanes, (low, high), unroll=BLOCKS)
    fits = (jnp.minimum(jnp.min(least), jnp.min(low)) >= SMALL) & (jnp.maximum(jnp.max(most), jnp.max(high)) <= LARGE)

    @pl.when(jnp.logical_not(fits))
    def _():
        fill(col_sum, 0.0)
        fill(col_top, -1e30)

        def pair(n, carry):
            p = order[n]
            t, d, f, z = product(p, starts([p])[0])
            top = jnp.max(z, 0, keepdims=True)
            put(p, d, top + jnp.log2(jnp.sum(jnp.exp2(z - top), 0, keepdims=True)) - f)
            a, b = z[:, :LANES], z[:, LANES:]
            old = col_top[t]
            new = jnp.maximum(old, jnp.maximum(a, b))
            col_sum[t] = col_sum[t] * jnp.exp2(old - new) + (jnp.exp2(a - new) + jnp.exp2(b - new))
            col_top[t] = new
            return carry

        lax.fori_loop(0, used, pair, 0)

        def lanes(t, carry):
            for k in range(2):
                rows = slice(k * LANES, (k + 1) * LANES)
                top = jnp.transpose(col_top[t, rows, :])
                most = jnp.max(top, 0, keepdims=True)
                s = jnp.sum(jnp.transpose(col_sum[t, rows, :]) * jnp.exp2(top - most), 0, keepdims=True)
                g = start_g[pl.ds(2 * t + k, 1), :]
                named = jnp.full((1, LANES), count[t].astype(jnp.float32) * float(BLK))
                term = EPS * jnp.log(named) - ((most + jnp.log2(s)) * (1.0 / SCALE) - g)
                fine_g_out[pl.ds(2 * t + k, 1), :] = 0.5 * (g + term)
            return carry

        lax.fori_loop(0, TB_DEV, lanes, 0)

def fine_update(slots, where, bundle, tgt_pts, tgt_cluster, f_table, g_table, slots_each):
    devices = bundle.shape[0]
    return pl.pallas_call(
        functools.partial(fine_kernel, slots_each),
        out_shape=(
            jax.ShapeDtypeStruct((devices, slots_each, BLK), jnp.float32),
            jax.ShapeDtypeStruct((F, LANES), jnp.float32),
            jax.ShapeDtypeStruct((2 * TB_DEV, LANES), jnp.float32),
        ),
        in_specs=[SMEM, SMEM] + [VMEM] * 5,
        out_specs=(VMEM, VMEM, VMEM),
        scratch_shapes=[
            pltpu.VMEM((2 * TB_DEV, LANES), jnp.float32),
            pltpu.VMEM((TB_DEV + 1, BLK, LANES), jnp.bfloat16),
            pltpu.VMEM((TB_DEV + 1, BLK, LANES), jnp.float32),
            pltpu.VMEM((TB_DEV + 1, BLK, LANES), jnp.float32),
            pltpu.SMEM((devices * slots_each,), jnp.int32),
            pltpu.SMEM((TB_DEV + 1,), jnp.int32),
        ],
        compiler_params=pltpu.CompilerParams(vmem_limit_bytes=48 * MIB),
        name="fine",
    )(slots, where, bundle, tgt_pts, tgt_cluster, f_table, g_table)


def finish_kernel(slots_each, slot_ref, partial, start_f, fine_f_out, gathered):
    for block in range(SB_DEV):
        for k in range(SUPP):
            slot = slot_ref[block * SUPP + k]
            gathered[k, block : block + 1, :] = partial[
                slot // slots_each, pl.ds(slot % slots_each, 1), :
            ]
    values = gathered[...]
    top = jnp.max(values, 0)
    lse = top + jnp.log2(jnp.sum(jnp.exp2(values - top[None]), 0))
    term = EPS * math.log(float(SUPP * BLK)) - lse * (1.0 / SCALE)
    for block in range(SB_DEV):
        for k in range(2):
            row = slice(2 * block + k, 2 * block + k + 1)
            piece = term[block : block + 1, k * LANES : (k + 1) * LANES]
            fine_f_out[row, :] = 0.5 * (start_f[row, :] + piece)


def finish(slot_ids, partial, start_f, slots_each):
    return pl.pallas_call(
        functools.partial(finish_kernel, slots_each),
        out_shape=jax.ShapeDtypeStruct((F, LANES), jnp.float32),
        in_specs=[SMEM, VMEM, VMEM],
        out_specs=VMEM,
        scratch_shapes=[pltpu.VMEM((SUPP, SB_DEV, BLK), jnp.float32)],
        name="finish",
    )(slot_ids, partial, start_f)


def exchange(x, axis, flip):
    count = lax.axis_size(axis)
    return lax.ppermute(x, axis, [(i, i ^ flip) for i in range(count)])


def on_device(
    src_cent, tgt_cent, src_mass, tgt_mass, src_pts, tgt_pts, src_cluster, tgt_cluster, support
):
    n_row, n_col = lax.axis_size("row"), lax.axis_size("col")
    devices = n_row * n_col
    row, col = lax.axis_index("row"), lax.axis_index("col")
    me = row * n_col + col

    requests_each = SB_DEV * SUPP
    slots_each = requests_each // devices + 1
    wanted = support.reshape(-1)
    owners = wanted // TB_DEV
    positions = jnp.arange(requests_each, dtype=jnp.int32)
    earlier = (owners[None, :] == owners[:, None]) & (positions[None, :] < positions[:, None])
    slot_ids = owners * slots_each + jnp.sum(earlier.astype(jnp.int32), 1)
    codes = (positions // SUPP) * TB_DEV + wanted % TB_DEV + 1
    width = -(-devices * slots_each // LANES) * LANES
    table = jnp.sum(
        jnp.where(slot_ids[None, :] == jnp.arange(width, dtype=jnp.int32)[:, None], codes[None, :], 0), 1
    )
    tiles = src_pts.reshape(2, 8, F, LANES).transpose(0, 2, 1, 3).reshape(2 * BLK // 2, LANES)
    table = jnp.pad(table.reshape(-1, LANES), ((0, -(width // LANES) % 8), (0, 0)))
    bundle = jnp.concatenate(
        [tiles, src_cluster.reshape(F, LANES).astype(jnp.float32), table.astype(jnp.float32)], 0
    )
    bundles = lax.all_gather(bundle, AXES)

    src_own = jnp.concatenate([src_cent, src_mass[None]], 0)
    tgt_own = jnp.concatenate([tgt_cent, tgt_mass[None]], 0)
    tgt_pair = jnp.concatenate([tgt_own, exchange(tgt_own, "col", 1)], 1)
    src_all = [src_own] + [exchange(src_own, "row", k) for k in range(1, n_row)]
    tgt_all = [tgt_pair] + [exchange(tgt_pair, "col", k) for k in range(2, n_col, 2)]
    f_table, g_table = coarse_duals(src_all, tgt_all)
    coarse_f = f_table[0, : src_cent.shape[1]]
    coarse_g = g_table[0, : tgt_cent.shape[1]]

    slots = bundles[:, 2 * BLK // 2 + F :, :].reshape(devices, -1)
    slots = lax.dynamic_slice_in_dim(slots, me * slots_each, slots_each, 1)
    slots = slots.reshape(-1).astype(jnp.int32)
    where = jnp.stack([me, row * src_cent.shape[1], col * tgt_cent.shape[1]]).astype(jnp.int32)
    partial, start_f, fine_g = fine_update(
        slots,
        where,
        bundles,
        tgt_pts,
        tgt_cluster.reshape(2 * TB_DEV, LANES),
        f_table,
        g_table,
        slots_each,
    )
    returned = lax.all_to_all(partial, AXES, split_axis=0, concat_axis=0, tiled=True)
    fine_f = finish(slot_ids, returned, start_f, slots_each)
    return coarse_f, coarse_g, fine_f.reshape(-1), fine_g.reshape(-1)


def solution(mesh):
    in_specs = (
        P(None, "row"),
        P(None, "col"),
        P("row"),
        P("col"),
        P(None, AXES),
        P(None, AXES),
        P(AXES),
        P(AXES),
        P(AXES, None),
    )
    out_specs = (P("row"), P("col"), P(AXES), P(AXES))
    return jax.shard_map(
        on_device, mesh=mesh, in_specs=in_specs, out_specs=out_specs, check_vma=False
    )
```

```python
import functools
import math

import jax
import jax.numpy as jnp
from jax import lax
from jax.experimental import pallas as pl
from jax.experimental.pallas import tpu as pltpu
from jax.sharding import PartitionSpec as P

F = 16
BLK = 256
SUPP = 16
ITERS = 8
SB_DEV = 8
TB_DEV = 32
EPS = 0.1

SCALE = math.log2(math.e) / EPS
KDIM = 7 * F
LANES = 128
ROWS = 256
ROWS_PRODUCT = 1024
ROWS_BEGIN = 1024
ROWS_TURN = 512
PAIRS = 16
BLOCKS = 8
LOW = 2.0**-30
SMALL = 2.0**-80
LARGE = 2.0**100
MIB = 1024 * 1024
AXES = ("row", "col")

VMEM = pl.BlockSpec(memory_space=pltpu.VMEM)
SMEM = pl.BlockSpec(memory_space=pltpu.SMEM)
CONTRACT_FIRST = (((0,), (0,)), ((), ()))


def split3(x):
    first = x.astype(jnp.bfloat16)
    rest = x - first.astype(jnp.float32)
    second = rest.astype(jnp.bfloat16)
    rest = rest - second.astype(jnp.float32)
    return first, second, rest.astype(jnp.bfloat16)


def constant_rows(values, at, ones_at):
    width = values.shape[1]
    parts = split3(jnp.broadcast_to(values, (F, width)))
    row = lax.broadcasted_iota(jnp.int32, (F, width), 0)
    rows = jnp.zeros((F, width), jnp.float32)
    for k, part in enumerate(parts):
        rows = jnp.where(row == at + k, part.astype(jnp.float32), rows)
    if ones_at is not None:
        rows = jnp.where((row >= ones_at) & (row < ones_at + 3), 1.0, rows)
    return rows.astype(jnp.bfloat16)


def pack_left(x, constant):
    a, b, c = split3(x * (2.0 * SCALE))
    return jnp.concatenate([a, a, b, b, a, c, constant_rows(constant, 0, 3)], 0)


def pack_right(y, constant):
    a, b, c = split3(y)
    return jnp.concatenate([a, b, a, b, c, a, constant_rows(constant, 3, 0)], 0)


def contract(left, right):
    return lax.dot_general(left, right, CONTRACT_FIRST, preferred_element_type=jnp.float32)


def square_norm(x):
    return jnp.sum(x * x, 0, keepdims=True)


def fold(values, combine):
    out = values[0:8]
    for k in range(1, values.shape[0] // 8):
        out = combine(out, values[8 * k : 8 * k + 8])
    return out


def source_columns(ref, count, k, n):
    halves = [
        jnp.concatenate(
            [
                ref[pl.ds(pl.multiple_of(8 * (half * count + k * n + i), 8), 8), :]
                for i in range(n)
            ],
            1,
        )
        for half in range(2)
    ]
    values = [ref[pl.ds(F * count + k * n + i, 1), :] for i in range(n)]
    return jnp.concatenate(halves, 0), jnp.concatenate(values, 1)


def prepare_kernel(
    src_pts, cluster, table, src_cent, src_mass, tgt_cent, tgt_mass, bundle, src_own, tgt_own
):
    for half in range(2):
        rows = slice(8 * half, 8 * half + 8)
        for ref, out in ((src_pts, bundle), (src_cent, src_own)):
            count = ref.shape[1] // LANES
            for i in range(count):
                at = 8 * (half * count + i)
                out[at : at + 8, :] = ref[rows, i * LANES : (i + 1) * LANES]
    at = 2 * LANES
    bundle[at : at + F, :] = cluster[...].astype(jnp.float32)
    bundle[at + F : at + F + 8, :] = jnp.zeros((8, LANES), jnp.float32)
    bundle[at + F : at + F + table.shape[0], :] = table[...].astype(jnp.float32)
    at = F * src_mass.shape[0]
    src_own[at : at + src_mass.shape[0], :] = src_mass[...]
    tgt_own[0, 0:F, :] = tgt_cent[...]
    tgt_own[0, F : F + 8, :] = jnp.broadcast_to(tgt_mass[...], (8, LANES))


def prepare(src_pts, cluster, table, src_cent, src_mass, tgt_cent, tgt_mass):
    return pl.pallas_call(
        prepare_kernel,
        out_shape=(
            jax.ShapeDtypeStruct((2 * LANES + F + 8, LANES), jnp.float32),
            jax.ShapeDtypeStruct(((F + 1) * src_mass.shape[0], LANES), jnp.float32),
            jax.ShapeDtypeStruct((1, F + 8, LANES), jnp.float32),
        ),
        in_specs=[VMEM] * 7,
        out_specs=(VMEM,) * 3,
        name="prepare",
    )(src_pts, cluster, table, src_cent, src_mass, tgt_cent, tgt_mass)


def coarse_kernel(n_src, n_tgt, stored, *refs):
    src = refs[:n_src]
    tgt = refs[n_src : n_src + n_tgt]
    f_out, g_out, kernel, mass, dual, sums = refs[n_src + n_tgt :]
    ks, kt = f_out.shape[1], g_out.shape[1]
    wide_src = src[0].shape[0] // (F + 1)
    piece = wide_src * LANES
    tiles = kt // LANES
    y = jnp.concatenate([ref[e, 0:F, :] for ref in tgt for e in range(2)], 1)
    b = jnp.concatenate([ref[e, F : F + 1, :] for ref in tgt for e in range(2)], 1)
    right = pack_right(y, jnp.log2(b) - SCALE * square_norm(y))
    ones = jnp.ones((F, LANES), jnp.bfloat16)
    zero = jnp.zeros((8, kt), jnp.float32)
    high = jnp.full((8, LANES), jnp.inf, jnp.float32)

    def wide(values):
        return jnp.tile(values, (1, tiles))

    def over_sources(size, body, carry):
        for s in range(n_src):

            def chunk(k, carry, s=s):
                rows = pl.ds(pl.multiple_of(s * piece + k * size, size), size)
                x, values = source_columns(src[s], wide_src, k, size // LANES)
                left = pack_left(x, -SCALE * square_norm(x))
                return body(values, rows, left, carry)

            carry = lax.fori_loop(0, piece // size, chunk, carry)
        return carry

    def over_rows(size, body, carry):
        def chunk(k, carry):
            return body(pl.ds(pl.multiple_of(k * size, size), size), carry)

        return lax.fori_loop(0, ks // size, chunk, carry)

    def weigh(e, weighted, rows, carry):
        total, least = carry
        row_sum = jnp.broadcast_to(jnp.sum(weighted, 1, keepdims=True), (e.shape[0], LANES))
        sums[rows, :] = row_sum
        weight = mass[rows, :] / row_sum
        return total + fold(e * wide(weight), jnp.add), jnp.minimum(least, fold(row_sum, jnp.minimum))

    def close(total, least):
        total = jnp.sum(total, 0, keepdims=True)
        small = jnp.minimum(jnp.min(total), jnp.min(least)) < LOW
        return b / total, small.astype(jnp.int32)

    def spread_mass(values, rows, left, carry):
        mass[rows, :] = contract(constant_rows(values, 0, None), ones)
        if stored:
            kernel[rows, :] = contract(left, right)
        return carry

    over_sources(ROWS_PRODUCT, spread_mass, 0)

    def begin_rows(z, rows, carry):
        top = jnp.max(z, 1, keepdims=True)
        dual[rows, :] = jnp.broadcast_to(-top, (z.shape[0], LANES))
        e = jnp.exp2(z - top)
        if stored:
            kernel[rows, :] = e
        return weigh(e, e, rows, carry)

    if stored:
        carry = over_rows(ROWS_BEGIN, lambda rows, c: begin_rows(kernel[rows, :], rows, c), (zero, high))
    else:
        carry = over_sources(ROWS, lambda _, rows, left, c: begin_rows(contract(left, right), rows, c), (zero, high))
    scale, small = close(*carry)
    base = jnp.zeros((1, kt), jnp.float32)

    def rescue(base, scale):
        def rebase(rows, carry):
            dual[rows, :] = dual[rows, :] - jnp.log2(sums[rows, :])
            return carry

        over_rows(ROWS, rebase, 0)

        def tops(_, rows, left, top):
            return jnp.maximum(top, fold(contract(left, right) + wide(dual[rows, :]), jnp.maximum))

        top = jnp.max(over_sources(ROWS, tops, zero - jnp.inf), 0, keepdims=True)

        def step(_, rows, left, total):
            e = jnp.exp2(contract(left, right) + wide(dual[rows, :]) - top)
            return total + fold(e * wide(mass[rows, :]), jnp.add)

        total = jnp.sum(over_sources(ROWS, step, zero), 0, keepdims=True)
        over_rows(ROWS, unit, 0)
        return jnp.log2(b) - (top + jnp.log2(total)), jnp.ones_like(scale)

    def unit(rows, carry):
        sums[rows, :] = jnp.ones((ROWS, LANES), jnp.float32)
        return carry

    base, scale = lax.cond(small > 0, rescue, lambda base, scale: (base, scale), base, scale)

    def renew(base, scale):
        base = base + jnp.log2(scale)

        def step(_, rows, left, carry):
            f = dual[rows, :] - jnp.log2(sums[rows, :])
            dual[rows, :] = f
            e = jnp.exp2(contract(left, right) + wide(f) + base)
            if stored:
                kernel[rows, :] = e
            return weigh(e, e, rows, carry)

        scale, small = close(*over_sources(ROWS, step, (zero, high)))
        return base, scale, small

    def reuse(base, scale):
        def step(rows, carry):
            e = kernel[rows, :]
            return weigh(e, e * scale, rows, carry)

        scale, small = close(*over_rows(ROWS_TURN, step, (zero, high)))
        return base, scale, small

    def turn(_, state):
        base, scale, small = state
        if not stored:
            return renew(base, scale)
        return lax.cond(small > 0, renew, reuse, base, scale)

    base, scale, small = lax.fori_loop(1, ITERS, turn, (base, scale, small))
    g_out[...] = (base + jnp.log2(scale)) * (1.0 / SCALE)
    diagonal = lax.broadcasted_iota(jnp.int32, (LANES, LANES), 0) == lax.broadcasted_iota(
        jnp.int32, (LANES, LANES), 1
    )

    def to_lanes(k, carry):
        span = pl.ds(pl.multiple_of(k * LANES, LANES), LANES)
        f = dual[span, :] - jnp.log2(sums[span, :])
        f_out[:, span] = jnp.sum(jnp.where(diagonal, f, 0.0), 0, keepdims=True) * (1.0 / SCALE)
        return carry

    lax.fori_loop(0, ks // LANES, to_lanes, 0)

def coarse_duals(src, tgt):
    ks = sum(part.shape[0] // (F + 1) * LANES for part in src)
    kt = sum(2 * part.shape[2] for part in tgt)
    stored = ks * kt * 4 <= 16 * MIB
    return pl.pallas_call(
        functools.partial(coarse_kernel, len(src), len(tgt), stored),
        out_shape=(
            jax.ShapeDtypeStruct((1, ks), jnp.float32),
            jax.ShapeDtypeStruct((1, kt), jnp.float32),
        ),
        in_specs=[VMEM] * (len(src) + len(tgt)),
        out_specs=(VMEM, VMEM),
        scratch_shapes=[
            pltpu.VMEM((ks, kt) if stored else (8, LANES), jnp.float32),
            pltpu.VMEM((ks, LANES), jnp.float32),
            pltpu.VMEM((ks, LANES), jnp.float32),
            pltpu.VMEM((ks, LANES), jnp.float32),
        ],
        compiler_params=pltpu.CompilerParams(vmem_limit_bytes=48 * MIB),
        cost_estimate=pl.CostEstimate(
            flops=40 * ks * kt, bytes_accessed=4 * 24 * (ks + kt), transcendentals=9 * ks * kt
        ),
        name="coarse",
    )(*src, *tgt)


def look_up(table_ref, index):
    low = index & (LANES - 1)
    high = index >> 7
    out = jnp.zeros(index.shape, jnp.float32)
    for h in range(table_ref.shape[1] // LANES):
        row = jnp.broadcast_to(table_ref[0:1, h * LANES : (h + 1) * LANES], index.shape)
        out = jnp.where(high == h, jnp.take_along_axis(row, low, axis=1), out)
    return out


def fine_kernel(n_stacks, slots_each, stride, where_ref, *refs):
    stacks = refs[:n_stacks]
    tgt_pts, tgt_cluster, f_table, g_table, partial_out, start_f_out, fine_g_out = refs[
        n_stacks : n_stacks + 7
    ]
    bundle, start_g, packed, col_sum, col_top, codes, arrived, slots, order, count = refs[
        n_stacks + 7 :
    ]
    devices = bundle.shape[0]
    depth = devices // n_stacks
    me, src_flip, tgt_flip = where_ref[0], where_ref[1], where_ref[2]

    copies = [
        pltpu.make_async_copy(
            stacks[n], bundle.at[pl.ds(n * depth, depth)], arrived.at[n]
        )
        for n in range(n_stacks)
    ]
    for copy in copies:
        copy.start()

    def sender(place):
        stack = place // depth
        return me ^ (2 * depth * (stack // 2) + 2 * (place % depth) + stack % 2)

    for k in range(2 * TB_DEV // 8):
        index = tgt_cluster[8 * k : 8 * k + 8, :] ^ tgt_flip
        start_g[8 * k : 8 * k + 8, :] = look_up(g_table, index)

    def pack_target(t, carry):
        y = tgt_pts[:, pl.ds(pl.multiple_of(t * BLK, BLK), BLK)]
        g = jnp.concatenate([start_g[pl.ds(2 * t, 1), :], start_g[pl.ds(2 * t + 1, 1), :]], 1)
        rows = pack_right(y, SCALE * (g - square_norm(y)))
        rows = jnp.concatenate([rows, jnp.zeros((LANES - KDIM, BLK), jnp.bfloat16)], 0)
        packed[t] = jnp.transpose(rows.astype(jnp.float32)).astype(jnp.bfloat16)
        count[t] = 0
        return carry

    lax.fori_loop(0, TB_DEV, pack_target, 0, unroll=BLOCKS)
    packed[TB_DEV] = jnp.zeros((BLK, LANES), jnp.bfloat16)
    count[TB_DEV] = 0

    for copy in copies:
        copy.wait()
    index = bundle[0, 2 * LANES : 2 * LANES + F, :].astype(jnp.int32) ^ src_flip
    for half in range(2):
        rows = slice(8 * half, 8 * half + 8)
        start_f_out[rows, :] = look_up(f_table, index[rows])

    at = me * stride

    def slot_row(n, carry):
        codes[pl.ds(n, 1), :] = bundle[n, pl.ds(2 * LANES + F + at // LANES, 1), :].astype(jnp.int32)
        return carry

    lax.fori_loop(0, devices, slot_row, 0, unroll=BLOCKS)
    codes[...] = pltpu.roll(codes[...], (LANES - at % LANES) % LANES, 1)
    copy = pltpu.make_async_copy(codes, slots, arrived.at[0])
    copy.start()
    copy.wait()

    total = devices * slots_each
    unroll = math.gcd(PAIRS, total)

    def place(p, carry):
        used, unused = carry
        code = slots[p // slots_each, p % slots_each]
        valid = code > 0
        order[jnp.where(valid, used, unused)] = p
        t = jnp.where(valid, (code - 1) % TB_DEV, TB_DEV)
        count[t] = count[t] + 1
        step = valid.astype(jnp.int32)
        return used + step, unused - (1 - step)

    used, _ = lax.fori_loop(0, total, place, (jnp.int32(0), jnp.int32(total - 1)), unroll=16)

    def cluster_rows(p):
        code = slots[p // slots_each, p % slots_each] - 1
        block = jnp.where(code >= 0, code // TB_DEV, 0)
        d = p // slots_each
        return [bundle[d, pl.ds(2 * LANES + 2 * block + k, 1), :] for k in range(2)]

    def starts(ps):
        out = []
        for n in range(0, len(ps), 4):
            rows = jnp.concatenate([r for p in ps[n:n+4] for r in cluster_rows(p)], 0)
            f = look_up(f_table, rows.astype(jnp.int32) ^ src_flip)
            for m in range(len(ps[n:n+4])):
                out.append(jnp.concatenate([f[2*m:2*m+1], f[2*m+1:2*m+2]], 1))
        return out

    def product(p, f):
        code = slots[p // slots_each, p % slots_each] - 1
        valid = code >= 0
        block = jnp.where(valid, code // TB_DEV, 0)
        t = jnp.where(valid, code % TB_DEV, TB_DEV)
        d = p // slots_each
        tile = [[bundle[d, pl.ds(pl.multiple_of(half * LANES + 16 * block + 8 * k, 8), 8), :] for k in range(2)] for half in range(2)]
        x = jnp.concatenate([jnp.concatenate(row, 1) for row in tile], 0)
        left = pack_left(x, SCALE * (f - square_norm(x)))
        left = jnp.concatenate([left, jnp.zeros((LANES - KDIM, BLK), jnp.bfloat16)], 0)
        z = jnp.dot(packed[t], left, preferred_element_type=jnp.float32)
        return t, d, SCALE * f, z

    def put(p, d, value):
        span = pl.ds(pl.multiple_of(p % slots_each * BLK, BLK), BLK)
        partial_out[sender(d), :, span] = value

    def fill(ref, value):
        def body(t, carry):
            ref[t] = jnp.full(ref.shape[1:], value, jnp.float32)
            return carry
        lax.fori_loop(0, ref.shape[0], body, 0)

    def pair(p, f, least, most):
        t, d, f, z = product(p, f)
        e = jnp.exp2(z)
        row = fold(e, jnp.add)
        col_sum[t] = col_sum[t] + (e[:, :LANES] + e[:, LANES:])
        row = jnp.sum(row, 0, keepdims=True)
        put(p, d, jnp.log2(row) - f)
        return jnp.minimum(least, row), jnp.maximum(most, row)

    def pairs(n, carry):
        ps = [order[unroll * n + u] for u in range(unroll)]
        fs = starts(ps)
        for u in range(unroll):
            carry = pair(ps[u], fs[u], *carry)
        return carry

    def lanes(t, carry):
        least, most = carry
        g = start_g[pl.ds(pl.multiple_of(2 * t, 2), 2), :]
        halves = []
        for k in range(2):
            block = col_sum[t, k * LANES : (k + 1) * LANES, :]
            halves.append(jnp.sum(jnp.transpose(block), 0, keepdims=True))
        s = jnp.concatenate(halves, 0)
        named = jnp.full((2, LANES), count[t].astype(jnp.float32) * float(BLK))
        term = EPS * jnp.log(named) - (jnp.log2(s) * (1.0 / SCALE) - g)
        fine_g_out[pl.ds(pl.multiple_of(2 * t, 2), 2), :] = 0.5 * (g + term)
        return jnp.minimum(least, s), jnp.maximum(most, s)

    fill(col_sum, 0.0)
    least = jnp.full((1, BLK), jnp.inf, jnp.float32)
    least, most = lax.fori_loop(0, (used + unroll - 1) // unroll, pairs, (least, jnp.zeros((1, BLK), jnp.float32)))
    low, high = jnp.full((2, LANES), jnp.inf, jnp.float32), jnp.zeros((2, LANES), jnp.float32)
    low, high = lax.fori_loop(0, TB_DEV, lanes, (low, high), unroll=BLOCKS)
    fits = (jnp.minimum(jnp.min(least), jnp.min(low)) >= SMALL) & (jnp.maximum(jnp.max(most), jnp.max(high)) <= LARGE)

    @pl.when(jnp.logical_not(fits))
    def _():
        fill(col_sum, 0.0)
        fill(col_top, -1e30)

        def pair(n, carry):
            p = order[n]
            t, d, f, z = product(p, starts([p])[0])
            top = jnp.max(z, 0, keepdims=True)
            put(p, d, top + jnp.log2(jnp.sum(jnp.exp2(z - top), 0, keepdims=True)) - f)
            a, b = z[:, :LANES], z[:, LANES:]
            old = col_top[t]
            new = jnp.maximum(old, jnp.maximum(a, b))
            col_sum[t] = col_sum[t] * jnp.exp2(old - new) + (jnp.exp2(a - new) + jnp.exp2(b - new))
            col_top[t] = new
            return carry

        lax.fori_loop(0, used, pair, 0)

        def lanes(t, carry):
            for k in range(2):
                rows = slice(k * LANES, (k + 1) * LANES)
                top = jnp.transpose(col_top[t, rows, :])
                most = jnp.max(top, 0, keepdims=True)
                s = jnp.sum(jnp.transpose(col_sum[t, rows, :]) * jnp.exp2(top - most), 0, keepdims=True)
                g = start_g[pl.ds(2 * t + k, 1), :]
                named = jnp.full((1, LANES), count[t].astype(jnp.float32) * float(BLK))
                term = EPS * jnp.log(named) - ((most + jnp.log2(s)) * (1.0 / SCALE) - g)
                fine_g_out[pl.ds(2 * t + k, 1), :] = 0.5 * (g + term)
            return carry

        lax.fori_loop(0, TB_DEV, lanes, 0)

def fine_update(where, stacks, tgt_pts, tgt_cluster, f_table, g_table, slots_each, stride):
    devices = sum(stack.shape[0] for stack in stacks)
    return pl.pallas_call(
        functools.partial(fine_kernel, len(stacks), slots_each, stride),
        out_shape=(
            jax.ShapeDtypeStruct((devices, 1, slots_each * BLK), jnp.float32),
            jax.ShapeDtypeStruct((F, LANES), jnp.float32),
            jax.ShapeDtypeStruct((2 * TB_DEV, LANES), jnp.float32),
        ),
        in_specs=[SMEM] + [pl.BlockSpec(memory_space=pl.ANY)] * len(stacks) + [VMEM] * 4,
        out_specs=(VMEM, VMEM, VMEM),
        scratch_shapes=[
            pltpu.VMEM((devices,) + stacks[0].shape[1:], jnp.float32),
            pltpu.VMEM((2 * TB_DEV, LANES), jnp.float32),
            pltpu.VMEM((TB_DEV + 1, BLK, LANES), jnp.bfloat16),
            pltpu.VMEM((TB_DEV + 1, BLK, LANES), jnp.float32),
            pltpu.VMEM((TB_DEV + 1, BLK, LANES), jnp.float32),
            pltpu.VMEM((devices, LANES), jnp.int32),
            pltpu.SemaphoreType.DMA((len(stacks),)),
            pltpu.SMEM((devices, LANES), jnp.int32),
            pltpu.SMEM((devices * slots_each,), jnp.int32),
            pltpu.SMEM((TB_DEV + 1,), jnp.int32),
        ],
        compiler_params=pltpu.CompilerParams(vmem_limit_bytes=48 * MIB),
        name="fine",
    )(where, *stacks, tgt_pts, tgt_cluster, f_table, g_table)


def finish_kernel(slots_each, slot_ref, partial, start_f, fine_f_out, gathered):
    for block in range(SB_DEV):
        for k in range(SUPP):
            slot = slot_ref[block * SUPP + k]
            span = pl.ds(pl.multiple_of(slot % slots_each * BLK, BLK), BLK)
            gathered[k, block : block + 1, :] = partial[slot // slots_each, :, span]
    values = gathered[...]
    top = jnp.max(values, 0)
    lse = top + jnp.log2(jnp.sum(jnp.exp2(values - top[None]), 0))
    term = EPS * math.log(float(SUPP * BLK)) - lse * (1.0 / SCALE)
    for block in range(SB_DEV):
        for k in range(2):
            row = slice(2 * block + k, 2 * block + k + 1)
            piece = term[block : block + 1, k * LANES : (k + 1) * LANES]
            fine_f_out[row, :] = 0.5 * (start_f[row, :] + piece)


def finish(slot_ids, partial, start_f, slots_each):
    return pl.pallas_call(
        functools.partial(finish_kernel, slots_each),
        out_shape=jax.ShapeDtypeStruct((F, LANES), jnp.float32),
        in_specs=[SMEM, VMEM, VMEM],
        out_specs=VMEM,
        scratch_shapes=[pltpu.VMEM((SUPP, SB_DEV, BLK), jnp.float32)],
        name="finish",
    )(slot_ids, partial, start_f)


def exchange(x, axis, flip):
    count = lax.axis_size(axis)
    return lax.ppermute(x, axis, [(i, i ^ flip) for i in range(count)])


def on_device(
    src_cent, tgt_cent, src_mass, tgt_mass, src_pts, tgt_pts, src_cluster, tgt_cluster, support
):
    n_row, n_col = lax.axis_size("row"), lax.axis_size("col")
    devices = n_row * n_col
    row, col = lax.axis_index("row"), lax.axis_index("col")
    me = row * n_col + col

    requests_each = SB_DEV * SUPP
    slots_each = requests_each // devices + 1
    wanted = support.reshape(-1)
    owners = wanted // TB_DEV
    positions = jnp.arange(requests_each, dtype=jnp.int32)
    earlier = (owners[None, :] == owners[:, None]) & (positions[None, :] < positions[:, None])
    slot_ids = owners * slots_each + jnp.sum(earlier.astype(jnp.int32), 1)
    codes = (positions // SUPP) * TB_DEV + wanted % TB_DEV + 1
    stride = 1 << (slots_each - 1).bit_length()
    filled = owners * stride + slot_ids % slots_each
    places = jnp.arange(devices * stride, dtype=jnp.int32)
    table = jnp.sum(jnp.where(filled[None, :] == places[:, None], codes[None, :], 0), 1)
    bundle, src_own, tgt_own = prepare(
        src_pts,
        src_cluster.reshape(F, LANES),
        table.reshape(-1, LANES),
        src_cent,
        src_mass.reshape(-1, LANES),
        tgt_cent,
        tgt_mass.reshape(-1, LANES),
    )

    tgt_pair = jnp.concatenate([tgt_own, exchange(tgt_own, "col", 1)], 0)
    src_all = [src_own] + [exchange(src_own, "row", k) for k in range(1, n_row)]
    tgt_all = [tgt_pair] + [exchange(tgt_pair, "col", k) for k in range(2, n_col, 2)]
    stack = jnp.stack([bundle] + [exchange(bundle, "col", k) for k in range(2, n_col, 2)])
    src_all, tgt_all, stack = lax.optimization_barrier((src_all, tgt_all, stack))
    stacks = [stack] + [exchange(stack, "row", k) for k in range(1, n_row)]
    f_table, g_table = coarse_duals(src_all, tgt_all)
    coarse_f = f_table[0, : src_cent.shape[1]]
    coarse_g = g_table[0, : tgt_cent.shape[1]]

    stacks = [part for own in stacks for part in (own, exchange(own, "col", 1))]
    where = jnp.stack([me, row * src_cent.shape[1], col * tgt_cent.shape[1]]).astype(jnp.int32)
    partial, start_f, fine_g = fine_update(
        where,
        stacks,
        tgt_pts,
        tgt_cluster.reshape(2 * TB_DEV, LANES),
        f_table,
        g_table,
        slots_each,
        stride,
    )
    returned = lax.all_to_all(partial, AXES, split_axis=0, concat_axis=0, tiled=True)
    fine_f = finish(slot_ids, returned, start_f, slots_each)
    return coarse_f, coarse_g, fine_f.reshape(-1), fine_g.reshape(-1)


def solution(mesh):
    in_specs = (
        P(None, "row"),
        P(None, "col"),
        P("row"),
        P("col"),
        P(None, AXES),
        P(None, AXES),
        P(AXES),
        P(AXES),
        P(AXES, None),
    )
    out_specs = (P("row"), P("col"), P(AXES), P(AXES))
    return jax.shard_map(
        on_device, mesh=mesh, in_specs=in_specs, out_specs=out_specs, check_vma=False
    )
```

```python
import functools
import math

import jax
import jax.numpy as jnp
from jax import lax
from jax.experimental import pallas as pl
from jax.experimental.pallas import tpu as pltpu
from jax.sharding import PartitionSpec as P

F = 16
BLK = 256
SUPP = 16
ITERS = 8
SB_DEV = 8
TB_DEV = 32
EPS = 0.1

SCALE = math.log2(math.e) / EPS
KDIM = 7 * F
LANES = 128
ROWS = 256
ROWS_PRODUCT = 1024
ROWS_BEGIN = 1024
ROWS_TURN = 512
PAIRS = 16
BLOCKS = 8
LOW = 2.0**-30
SMALL = 2.0**-80
LARGE = 2.0**100
MIB = 1024 * 1024
AXES = ("row", "col")

VMEM = pl.BlockSpec(memory_space=pltpu.VMEM)
SMEM = pl.BlockSpec(memory_space=pltpu.SMEM)
CONTRACT_FIRST = (((0,), (0,)), ((), ()))


def split3(x):
    first = x.astype(jnp.bfloat16)
    rest = x - first.astype(jnp.float32)
    second = rest.astype(jnp.bfloat16)
    rest = rest - second.astype(jnp.float32)
    return first, second, rest.astype(jnp.bfloat16)


def constant_rows(values, at, ones_at):
    width = values.shape[1]
    parts = split3(jnp.broadcast_to(values, (F, width)))
    row = lax.broadcasted_iota(jnp.int32, (F, width), 0)
    rows = jnp.zeros((F, width), jnp.float32)
    for k, part in enumerate(parts):
        rows = jnp.where(row == at + k, part.astype(jnp.float32), rows)
    if ones_at is not None:
        rows = jnp.where((row >= ones_at) & (row < ones_at + 3), 1.0, rows)
    return rows.astype(jnp.bfloat16)


def pack_left(x, constant):
    a, b, c = split3(x * (2.0 * SCALE))
    return jnp.concatenate([a, a, b, b, a, c, constant_rows(constant, 0, 3)], 0)


def pack_right(y, constant):
    a, b, c = split3(y)
    return jnp.concatenate([a, b, a, b, c, a, constant_rows(constant, 3, 0)], 0)


def contract(left, right):
    return lax.dot_general(left, right, CONTRACT_FIRST, preferred_element_type=jnp.float32)


def square_norm(x):
    return jnp.sum(x * x, 0, keepdims=True)


def fold(values, combine):
    out = values[0:8]
    for k in range(1, values.shape[0] // 8):
        out = combine(out, values[8 * k : 8 * k + 8])
    return out


def source_columns(ref, count, k, n):
    halves = [
        jnp.concatenate(
            [
                ref[pl.ds(pl.multiple_of(8 * (half * count + k * n + i), 8), 8), :]
                for i in range(n)
            ],
            1,
        )
        for half in range(2)
    ]
    values = [ref[pl.ds(F * count + k * n + i, 1), :] for i in range(n)]
    return jnp.concatenate(halves, 0), jnp.concatenate(values, 1)


def prepare_kernel(
    src_pts, cluster, table, src_cent, src_mass, tgt_cent, tgt_mass, bundle, src_own, tgt_own
):
    for half in range(2):
        rows = slice(8 * half, 8 * half + 8)
        for ref, out in ((src_pts, bundle), (src_cent, src_own)):
            count = ref.shape[1] // LANES
            for i in range(count):
                at = 8 * (half * count + i)
                out[at : at + 8, :] = ref[rows, i * LANES : (i + 1) * LANES]
    at = 2 * LANES
    bundle[at : at + F, :] = cluster[...].astype(jnp.float32)
    bundle[at + F : at + F + 8, :] = jnp.zeros((8, LANES), jnp.float32)
    bundle[at + F : at + F + table.shape[0], :] = table[...].astype(jnp.float32)
    at = F * src_mass.shape[0]
    src_own[at : at + src_mass.shape[0], :] = src_mass[...]
    tgt_own[0, 0:F, :] = tgt_cent[...]
    tgt_own[0, F : F + 8, :] = jnp.broadcast_to(tgt_mass[...], (8, LANES))


def prepare(src_pts, cluster, table, src_cent, src_mass, tgt_cent, tgt_mass):
    return pl.pallas_call(
        prepare_kernel,
        out_shape=(
            jax.ShapeDtypeStruct((2 * LANES + F + 8, LANES), jnp.float32),
            jax.ShapeDtypeStruct(((F + 1) * src_mass.shape[0], LANES), jnp.float32),
            jax.ShapeDtypeStruct((1, F + 8, LANES), jnp.float32),
        ),
        in_specs=[VMEM] * 7,
        out_specs=(VMEM,) * 3,
        name="prepare",
    )(src_pts, cluster, table, src_cent, src_mass, tgt_cent, tgt_mass)


def coarse_kernel(n_src, n_tgt, stored, *refs):
    src = refs[:n_src]
    tgt = refs[n_src : n_src + n_tgt]
    f_out, g_out, kernel, mass, dual, sums = refs[n_src + n_tgt :]
    ks, kt = f_out.shape[1], g_out.shape[1]
    wide_src = src[0].shape[0] // (F + 1)
    piece = wide_src * LANES
    tiles = kt // LANES
    y = jnp.concatenate([ref[e, 0:F, :] for ref in tgt for e in range(2)], 1)
    b = jnp.concatenate([ref[e, F : F + 1, :] for ref in tgt for e in range(2)], 1)
    right = pack_right(y, jnp.log2(b) - SCALE * square_norm(y))
    ones = jnp.ones((F, LANES), jnp.bfloat16)
    zero = jnp.zeros((8, kt), jnp.float32)
    high = jnp.full((8, LANES), jnp.inf, jnp.float32)

    def wide(values):
        return jnp.tile(values, (1, tiles))

    def over_sources(size, body, carry):
        for s in range(n_src):

            def chunk(k, carry, s=s):
                rows = pl.ds(pl.multiple_of(s * piece + k * size, size), size)
                x, values = source_columns(src[s], wide_src, k, size // LANES)
                left = pack_left(x, -SCALE * square_norm(x))
                return body(values, rows, left, carry)

            carry = lax.fori_loop(0, piece // size, chunk, carry)
        return carry

    def over_rows(size, body, carry):
        def chunk(k, carry):
            return body(pl.ds(pl.multiple_of(k * size, size), size), carry)

        return lax.fori_loop(0, ks // size, chunk, carry)

    def weigh(e, weighted, rows, carry):
        total, least = carry
        row_sum = jnp.broadcast_to(jnp.sum(weighted, 1, keepdims=True), (e.shape[0], LANES))
        sums[rows, :] = row_sum
        weight = mass[rows, :] / row_sum
        return total + fold(e * wide(weight), jnp.add), jnp.minimum(least, fold(row_sum, jnp.minimum))

    def close(total, least):
        total = jnp.sum(total, 0, keepdims=True)
        small = jnp.minimum(jnp.min(total), jnp.min(least)) < LOW
        return b / total, small.astype(jnp.int32)

    def spread_mass(values, rows, left, carry):
        mass[rows, :] = contract(constant_rows(values, 0, None), ones)
        if stored:
            kernel[rows, :] = contract(left, right)
        return carry

    over_sources(ROWS_PRODUCT, spread_mass, 0)

    def begin_rows(z, rows, carry):
        top = jnp.max(z, 1, keepdims=True)
        dual[rows, :] = jnp.broadcast_to(-top, (z.shape[0], LANES))
        e = jnp.exp2(z - top)
        if stored:
            kernel[rows, :] = e
        return weigh(e, e, rows, carry)

    if stored:
        carry = over_rows(ROWS_BEGIN, lambda rows, c: begin_rows(kernel[rows, :], rows, c), (zero, high))
    else:
        carry = over_sources(ROWS, lambda _, rows, left, c: begin_rows(contract(left, right), rows, c), (zero, high))
    scale, small = close(*carry)
    base = jnp.zeros((1, kt), jnp.float32)

    def rescue(base, scale):
        def rebase(rows, carry):
            dual[rows, :] = dual[rows, :] - jnp.log2(sums[rows, :])
            return carry

        over_rows(ROWS, rebase, 0)

        def tops(_, rows, left, top):
            return jnp.maximum(top, fold(contract(left, right) + wide(dual[rows, :]), jnp.maximum))

        top = jnp.max(over_sources(ROWS, tops, zero - jnp.inf), 0, keepdims=True)

        def step(_, rows, left, total):
            e = jnp.exp2(contract(left, right) + wide(dual[rows, :]) - top)
            return total + fold(e * wide(mass[rows, :]), jnp.add)

        total = jnp.sum(over_sources(ROWS, step, zero), 0, keepdims=True)
        over_rows(ROWS, unit, 0)
        return jnp.log2(b) - (top + jnp.log2(total)), jnp.ones_like(scale)

    def unit(rows, carry):
        sums[rows, :] = jnp.ones((ROWS, LANES), jnp.float32)
        return carry

    base, scale = lax.cond(small > 0, rescue, lambda base, scale: (base, scale), base, scale)

    def renew(base, scale):
        base = base + jnp.log2(scale)

        def step(_, rows, left, carry):
            f = dual[rows, :] - jnp.log2(sums[rows, :])
            dual[rows, :] = f
            e = jnp.exp2(contract(left, right) + wide(f) + base)
            if stored:
                kernel[rows, :] = e
            return weigh(e, e, rows, carry)

        scale, small = close(*over_sources(ROWS, step, (zero, high)))
        return base, scale, small

    def reuse(base, scale):
        def step(rows, carry):
            e = kernel[rows, :]
            return weigh(e, e * scale, rows, carry)

        scale, small = close(*over_rows(ROWS_TURN, step, (zero, high)))
        return base, scale, small

    def turn(_, state):
        base, scale, small = state
        if not stored:
            return renew(base, scale)
        return lax.cond(small > 0, renew, reuse, base, scale)

    base, scale, small = lax.fori_loop(1, ITERS, turn, (base, scale, small))
    g_out[...] = (base + jnp.log2(scale)) * (1.0 / SCALE)
    diagonal = lax.broadcasted_iota(jnp.int32, (LANES, LANES), 0) == lax.broadcasted_iota(
        jnp.int32, (LANES, LANES), 1
    )

    def to_lanes(k, carry):
        span = pl.ds(pl.multiple_of(k * LANES, LANES), LANES)
        f = dual[span, :] - jnp.log2(sums[span, :])
        f_out[:, span] = jnp.sum(jnp.where(diagonal, f, 0.0), 0, keepdims=True) * (1.0 / SCALE)
        return carry

    lax.fori_loop(0, ks // LANES, to_lanes, 0)

def coarse_duals(src, tgt):
    ks = sum(part.shape[0] // (F + 1) * LANES for part in src)
    kt = sum(2 * part.shape[2] for part in tgt)
    stored = ks * kt * 4 <= 16 * MIB
    return pl.pallas_call(
        functools.partial(coarse_kernel, len(src), len(tgt), stored),
        out_shape=(
            jax.ShapeDtypeStruct((1, ks), jnp.float32),
            jax.ShapeDtypeStruct((1, kt), jnp.float32),
        ),
        in_specs=[VMEM] * (len(src) + len(tgt)),
        out_specs=(VMEM, VMEM),
        scratch_shapes=[
            pltpu.VMEM((ks, kt) if stored else (8, LANES), jnp.float32),
            pltpu.VMEM((ks, LANES), jnp.float32),
            pltpu.VMEM((ks, LANES), jnp.float32),
            pltpu.VMEM((ks, LANES), jnp.float32),
        ],
        compiler_params=pltpu.CompilerParams(vmem_limit_bytes=48 * MIB),
        cost_estimate=pl.CostEstimate(
            flops=40 * ks * kt, bytes_accessed=4 * 24 * (ks + kt), transcendentals=9 * ks * kt
        ),
        name="coarse",
    )(*src, *tgt)


def look_up(table_ref, index):
    low = index & (LANES - 1)
    high = index >> 7
    out = jnp.zeros(index.shape, jnp.float32)
    for h in range(table_ref.shape[1] // LANES):
        row = jnp.broadcast_to(table_ref[0:1, h * LANES : (h + 1) * LANES], index.shape)
        out = jnp.where(high == h, jnp.take_along_axis(row, low, axis=1), out)
    return out


def fine_kernel(n_stacks, slots_each, stride, where_ref, *refs):
    stacks = refs[:n_stacks]
    tgt_pts, tgt_cluster, f_table, g_table, partial_out, start_f_out, fine_g_out = refs[
        n_stacks : n_stacks + 7
    ]
    bundle, start_g, packed, col_sum, col_top, codes, arrived, slots, order, count = refs[
        n_stacks + 7 :
    ]
    devices = bundle.shape[0]
    depth = devices // n_stacks
    me, src_flip, tgt_flip = where_ref[0], where_ref[1], where_ref[2]

    copies = [
        pltpu.make_async_copy(
            stacks[n], bundle.at[pl.ds(n * depth, depth)], arrived.at[n]
        )
        for n in range(n_stacks)
    ]
    for copy in copies:
        copy.start()

    def sender(place):
        stack = place // depth
        return me ^ (2 * depth * (stack // 2) + 2 * (place % depth) + stack % 2)

    for k in range(2 * TB_DEV // 8):
        index = tgt_cluster[8 * k : 8 * k + 8, :] ^ tgt_flip
        start_g[8 * k : 8 * k + 8, :] = look_up(g_table, index)

    def pack_target(t, carry):
        y = tgt_pts[:, pl.ds(pl.multiple_of(t * BLK, BLK), BLK)]
        g = jnp.concatenate([start_g[pl.ds(2 * t, 1), :], start_g[pl.ds(2 * t + 1, 1), :]], 1)
        rows = pack_right(y, SCALE * (g - square_norm(y)))
        rows = jnp.concatenate([rows, jnp.zeros((LANES - KDIM, BLK), jnp.bfloat16)], 0)
        packed[t] = jnp.transpose(rows.astype(jnp.float32)).astype(jnp.bfloat16)
        count[t] = 0
        return carry

    lax.fori_loop(0, TB_DEV, pack_target, 0, unroll=BLOCKS)
    packed[TB_DEV] = jnp.zeros((BLK, LANES), jnp.bfloat16)
    count[TB_DEV] = 0

    for copy in copies:
        copy.wait()
    index = bundle[0, 2 * LANES : 2 * LANES + F, :].astype(jnp.int32) ^ src_flip
    for half in range(2):
        rows = slice(8 * half, 8 * half + 8)
        start_f_out[rows, :] = look_up(f_table, index[rows])

    at = me * stride

    def slot_row(n, carry):
        codes[pl.ds(n, 1), :] = bundle[n, pl.ds(2 * LANES + F + at // LANES, 1), :].astype(jnp.int32)
        return carry

    lax.fori_loop(0, devices, slot_row, 0, unroll=BLOCKS)
    codes[...] = pltpu.roll(codes[...], (LANES - at % LANES) % LANES, 1)
    copy = pltpu.make_async_copy(codes, slots, arrived.at[0])
    copy.start()
    copy.wait()

    total = devices * slots_each
    unroll = math.gcd(PAIRS, total)

    def place(p, carry):
        used, unused = carry
        code = slots[p // slots_each, p % slots_each]
        valid = code > 0
        order[jnp.where(valid, used, unused)] = p
        t = jnp.where(valid, (code - 1) % TB_DEV, TB_DEV)
        count[t] = count[t] + 1
        step = valid.astype(jnp.int32)
        return used + step, unused - (1 - step)

    used, _ = lax.fori_loop(0, total, place, (jnp.int32(0), jnp.int32(total - 1)), unroll=16)

    def cluster_rows(p):
        code = slots[p // slots_each, p % slots_each] - 1
        block = jnp.where(code >= 0, code // TB_DEV, 0)
        d = p // slots_each
        return [bundle[d, pl.ds(2 * LANES + 2 * block + k, 1), :] for k in range(2)]

    def starts(ps):
        out = []
        for n in range(0, len(ps), 4):
            rows = jnp.concatenate([r for p in ps[n:n+4] for r in cluster_rows(p)], 0)
            f = look_up(f_table, rows.astype(jnp.int32) ^ src_flip)
            for m in range(len(ps[n:n+4])):
                out.append(jnp.concatenate([f[2*m:2*m+1], f[2*m+1:2*m+2]], 1))
        return out

    def product(p, f):
        code = slots[p // slots_each, p % slots_each] - 1
        valid = code >= 0
        block = jnp.where(valid, code // TB_DEV, 0)
        t = jnp.where(valid, code % TB_DEV, TB_DEV)
        d = p // slots_each
        tile = [[bundle[d, pl.ds(pl.multiple_of(half * LANES + 16 * block + 8 * k, 8), 8), :] for k in range(2)] for half in range(2)]
        x = jnp.concatenate([jnp.concatenate(row, 1) for row in tile], 0)
        left = pack_left(x, SCALE * (f - square_norm(x)))
        left = jnp.concatenate([left, jnp.zeros((LANES - KDIM, BLK), jnp.bfloat16)], 0)
        z = jnp.dot(packed[t], left, preferred_element_type=jnp.float32)
        return t, d, SCALE * f, z

    def put(p, d, value):
        span = pl.ds(pl.multiple_of(p % slots_each * BLK, BLK), BLK)
        partial_out[sender(d), :, span] = value

    def fill(ref, value):
        def body(t, carry):
            ref[t] = jnp.full(ref.shape[1:], value, jnp.float32)
            return carry
        lax.fori_loop(0, ref.shape[0], body, 0)

    def pair(p, f, least, most):
        t, d, f, z = product(p, f)
        e = jnp.exp2(z)
        row = fold(e, jnp.add)
        col_sum[t] = col_sum[t] + (e[:, :LANES] + e[:, LANES:])
        row = jnp.sum(row, 0, keepdims=True)
        put(p, d, jnp.log2(row) - f)
        return jnp.minimum(least, row), jnp.maximum(most, row)

    def pairs(n, carry):
        ps = [order[unroll * n + u] for u in range(unroll)]
        fs = starts(ps)
        for u in range(unroll):
            carry = pair(ps[u], fs[u], *carry)
        return carry

    def lanes(t, carry):
        least, most = carry
        g = start_g[pl.ds(pl.multiple_of(2 * t, 2), 2), :]
        halves = []
        for k in range(2):
            block = col_sum[t, k * LANES : (k + 1) * LANES, :]
            halves.append(jnp.sum(jnp.transpose(block), 0, keepdims=True))
        s = jnp.concatenate(halves, 0)
        named = jnp.full((2, LANES), count[t].astype(jnp.float32) * float(BLK))
        term = EPS * jnp.log(named) - (jnp.log2(s) * (1.0 / SCALE) - g)
        fine_g_out[pl.ds(pl.multiple_of(2 * t, 2), 2), :] = 0.5 * (g + term)
        return jnp.minimum(least, s), jnp.maximum(most, s)

    fill(col_sum, 0.0)
    least = jnp.full((1, BLK), jnp.inf, jnp.float32)
    least, most = lax.fori_loop(0, (used + unroll - 1) // unroll, pairs, (least, jnp.zeros((1, BLK), jnp.float32)))
    low, high = jnp.full((2, LANES), jnp.inf, jnp.float32), jnp.zeros((2, LANES), jnp.float32)
    low, high = lax.fori_loop(0, TB_DEV, lanes, (low, high), unroll=BLOCKS)
    fits = (jnp.minimum(jnp.min(least), jnp.min(low)) >= SMALL) & (jnp.maximum(jnp.max(most), jnp.max(high)) <= LARGE)

    @pl.when(jnp.logical_not(fits))
    def _():
        fill(col_sum, 0.0)
        fill(col_top, -1e30)

        def pair(n, carry):
            p = order[n]
            t, d, f, z = product(p, starts([p])[0])
            top = jnp.max(z, 0, keepdims=True)
            put(p, d, top + jnp.log2(jnp.sum(jnp.exp2(z - top), 0, keepdims=True)) - f)
            a, b = z[:, :LANES], z[:, LANES:]
            old = col_top[t]
            new = jnp.maximum(old, jnp.maximum(a, b))
            col_sum[t] = col_sum[t] * jnp.exp2(old - new) + (jnp.exp2(a - new) + jnp.exp2(b - new))
            col_top[t] = new
            return carry

        lax.fori_loop(0, used, pair, 0)

        def lanes(t, carry):
            for k in range(2):
                rows = slice(k * LANES, (k + 1) * LANES)
                top = jnp.transpose(col_top[t, rows, :])
                most = jnp.max(top, 0, keepdims=True)
                s = jnp.sum(jnp.transpose(col_sum[t, rows, :]) * jnp.exp2(top - most), 0, keepdims=True)
                g = start_g[pl.ds(2 * t + k, 1), :]
                named = jnp.full((1, LANES), count[t].astype(jnp.float32) * float(BLK))
                term = EPS * jnp.log(named) - ((most + jnp.log2(s)) * (1.0 / SCALE) - g)
                fine_g_out[pl.ds(2 * t + k, 1), :] = 0.5 * (g + term)
            return carry

        lax.fori_loop(0, TB_DEV, lanes, 0)

def fine_update(where, stacks, tgt_pts, tgt_cluster, f_table, g_table, slots_each, stride):
    devices = sum(stack.shape[0] for stack in stacks)
    return pl.pallas_call(
        functools.partial(fine_kernel, len(stacks), slots_each, stride),
        out_shape=(
            jax.ShapeDtypeStruct((devices, 1, slots_each * BLK), jnp.float32),
            jax.ShapeDtypeStruct((F, LANES), jnp.float32),
            jax.ShapeDtypeStruct((2 * TB_DEV, LANES), jnp.float32),
        ),
        in_specs=[SMEM] + [pl.BlockSpec(memory_space=pl.ANY)] * len(stacks) + [VMEM] * 4,
        out_specs=(VMEM, VMEM, VMEM),
        scratch_shapes=[
            pltpu.VMEM((devices,) + stacks[0].shape[1:], jnp.float32),
            pltpu.VMEM((2 * TB_DEV, LANES), jnp.float32),
            pltpu.VMEM((TB_DEV + 1, BLK, LANES), jnp.bfloat16),
            pltpu.VMEM((TB_DEV + 1, BLK, LANES), jnp.float32),
            pltpu.VMEM((TB_DEV + 1, BLK, LANES), jnp.float32),
            pltpu.VMEM((devices, LANES), jnp.int32),
            pltpu.SemaphoreType.DMA((len(stacks),)),
            pltpu.SMEM((devices, LANES), jnp.int32),
            pltpu.SMEM((devices * slots_each,), jnp.int32),
            pltpu.SMEM((TB_DEV + 1,), jnp.int32),
        ],
        compiler_params=pltpu.CompilerParams(vmem_limit_bytes=48 * MIB),
        name="fine",
    )(where, *stacks, tgt_pts, tgt_cluster, f_table, g_table)


def finish_kernel(slots_each, slot_ref, partial, start_f, fine_f_out, gathered):
    for block in range(SB_DEV):
        for k in range(SUPP):
            slot = slot_ref[block * SUPP + k]
            span = pl.ds(pl.multiple_of(slot % slots_each * BLK, BLK), BLK)
            gathered[k, block : block + 1, :] = partial[slot // slots_each, :, span]
    values = gathered[...]
    top = jnp.max(values, 0)
    lse = top + jnp.log2(jnp.sum(jnp.exp2(values - top[None]), 0))
    term = EPS * math.log(float(SUPP * BLK)) - lse * (1.0 / SCALE)
    for block in range(SB_DEV):
        for k in range(2):
            row = slice(2 * block + k, 2 * block + k + 1)
            piece = term[block : block + 1, k * LANES : (k + 1) * LANES]
            fine_f_out[row, :] = 0.5 * (start_f[row, :] + piece)


def finish(slot_ids, partial, start_f, slots_each):
    return pl.pallas_call(
        functools.partial(finish_kernel, slots_each),
        out_shape=jax.ShapeDtypeStruct((F, LANES), jnp.float32),
        in_specs=[SMEM, VMEM, VMEM],
        out_specs=VMEM,
        scratch_shapes=[pltpu.VMEM((SUPP, SB_DEV, BLK), jnp.float32)],
        name="finish",
    )(slot_ids, partial, start_f)


def exchange(x, axis, flip):
    count = lax.axis_size(axis)
    return lax.ppermute(x, axis, [(i, i ^ flip) for i in range(count)])


def on_device(
    src_cent, tgt_cent, src_mass, tgt_mass, src_pts, tgt_pts, src_cluster, tgt_cluster, support
):
    n_row, n_col = lax.axis_size("row"), lax.axis_size("col")
    devices = n_row * n_col
    row, col = lax.axis_index("row"), lax.axis_index("col")
    me = row * n_col + col

    requests_each = SB_DEV * SUPP
    slots_each = requests_each // devices + 1
    wanted = support.reshape(-1)
    owners = wanted // TB_DEV
    positions = jnp.arange(requests_each, dtype=jnp.int32)
    earlier = (owners[None, :] == owners[:, None]) & (positions[None, :] < positions[:, None])
    slot_ids = owners * slots_each + jnp.sum(earlier.astype(jnp.int32), 1)
    codes = (positions // SUPP) * TB_DEV + wanted % TB_DEV + 1
    stride = 1 << (slots_each - 1).bit_length()
    filled = owners * stride + slot_ids % slots_each
    places = jnp.arange(devices * stride, dtype=jnp.int32)
    table = jnp.sum(jnp.where(filled[None, :] == places[:, None], codes[None, :], 0), 1)
    bundle, src_own, tgt_own = prepare(
        src_pts,
        src_cluster.reshape(F, LANES),
        table.reshape(-1, LANES),
        src_cent,
        src_mass.reshape(-1, LANES),
        tgt_cent,
        tgt_mass.reshape(-1, LANES),
    )

    tgt_pair = jnp.concatenate([tgt_own, exchange(tgt_own, "col", 1)], 0)
    src_all = [src_own] + [exchange(src_own, "row", k) for k in range(1, n_row)]
    tgt_all = [tgt_pair] + [exchange(tgt_pair, "col", k) for k in range(2, n_col, 2)]
    stack = jnp.stack([bundle] + [exchange(bundle, "col", k) for k in range(2, n_col, 2)])
    src_all, tgt_all, stack = lax.optimization_barrier((src_all, tgt_all, stack))
    stacks = [stack] + [exchange(stack, "row", k) for k in range(1, n_row)]
    f_table, g_table = coarse_duals(src_all, tgt_all)
    coarse_f = f_table[0, : src_cent.shape[1]]
    coarse_g = g_table[0, : tgt_cent.shape[1]]

    stacks, f_table, g_table = lax.optimization_barrier((stacks, f_table, g_table))
    stacks = [part for own in stacks for part in (own, exchange(own, "col", 1))]
    where = jnp.stack([me, row * src_cent.shape[1], col * tgt_cent.shape[1]]).astype(jnp.int32)
    partial, start_f, fine_g = fine_update(
        where,
        stacks,
        tgt_pts,
        tgt_cluster.reshape(2 * TB_DEV, LANES),
        f_table,
        g_table,
        slots_each,
        stride,
    )
    returned = lax.all_to_all(partial, AXES, split_axis=0, concat_axis=0, tiled=True)
    fine_f = finish(slot_ids, returned, start_f, slots_each)
    return coarse_f, coarse_g, fine_f.reshape(-1), fine_g.reshape(-1)


def solution(mesh):
    in_specs = (
        P(None, "row"),
        P(None, "col"),
        P("row"),
        P("col"),
        P(None, AXES),
        P(None, AXES),
        P(AXES),
        P(AXES),
        P(AXES, None),
    )
    out_specs = (P("row"), P("col"), P(AXES), P(AXES))
    return jax.shard_map(
        on_device, mesh=mesh, in_specs=in_specs, out_specs=out_specs, check_vma=False
    )
```

```python
import functools
import math

import jax
import jax.numpy as jnp
from jax import lax
from jax.experimental import pallas as pl
from jax.experimental.pallas import tpu as pltpu
from jax.sharding import PartitionSpec as P

F = 16
BLK = 256
SUPP = 16
ITERS = 8
SB_DEV = 8
TB_DEV = 32
EPS = 0.1

SCALE = math.log2(math.e) / EPS
KDIM = 7 * F
LANES = 128
ROWS = 256
ROWS_PRODUCT = 1024
ROWS_BEGIN = 1024
ROWS_TURN = 512
PAIRS = 16
BLOCKS = 8
LOW = 2.0**-30
SMALL = 2.0**-80
LARGE = 2.0**100
MIB = 1024 * 1024
SLOT_AT = 2 * LANES + F
TGT_AT = SLOT_AT + 8
AXES = ("row", "col")

VMEM = pl.BlockSpec(memory_space=pltpu.VMEM)
SMEM = pl.BlockSpec(memory_space=pltpu.SMEM)
CONTRACT_FIRST = (((0,), (0,)), ((), ()))


def split3(x):
    first = x.astype(jnp.bfloat16)
    rest = x - first.astype(jnp.float32)
    second = rest.astype(jnp.bfloat16)
    rest = rest - second.astype(jnp.float32)
    return first, second, rest.astype(jnp.bfloat16)


def constant_rows(values, at, ones_at):
    width = values.shape[1]
    parts = split3(jnp.broadcast_to(values, (F, width)))
    row = lax.broadcasted_iota(jnp.int32, (F, width), 0)
    rows = jnp.zeros((F, width), jnp.float32)
    for k, part in enumerate(parts):
        rows = jnp.where(row == at + k, part.astype(jnp.float32), rows)
    if ones_at is not None:
        rows = jnp.where((row >= ones_at) & (row < ones_at + 3), 1.0, rows)
    return rows.astype(jnp.bfloat16)


def pack_left(x, constant):
    a, b, c = split3(x * (2.0 * SCALE))
    return jnp.concatenate([a, a, b, b, a, c, constant_rows(constant, 0, 3)], 0)


def pack_right(y, constant):
    a, b, c = split3(y)
    return jnp.concatenate([a, b, a, b, c, a, constant_rows(constant, 3, 0)], 0)


def contract(left, right):
    return lax.dot_general(left, right, CONTRACT_FIRST, preferred_element_type=jnp.float32)


def square_norm(x):
    return jnp.sum(x * x, 0, keepdims=True)


def fold(values, combine):
    out = values[0:8]
    for k in range(1, values.shape[0] // 8):
        out = combine(out, values[8 * k : 8 * k + 8])
    return out


def source_columns(ref, count, k, n):
    halves = [
        jnp.concatenate(
            [
                ref[pl.ds(pl.multiple_of(8 * (half * count + k * n + i), 8), 8), :]
                for i in range(n)
            ],
            1,
        )
        for half in range(2)
    ]
    values = [ref[pl.ds(F * count + k * n + i, 1), :] for i in range(n)]
    return jnp.concatenate(halves, 0), jnp.concatenate(values, 1)


def prepare_kernel(
    src_pts, cluster, table, src_cent, src_mass, tgt_a, mass_a, tgt_b, mass_b, bundle, src_own
):
    for half in range(2):
        rows = slice(8 * half, 8 * half + 8)
        for ref, out in ((src_pts, bundle), (src_cent, src_own)):
            count = ref.shape[1] // LANES
            for i in range(count):
                at = 8 * (half * count + i)
                out[at : at + 8, :] = ref[rows, i * LANES : (i + 1) * LANES]
    at = 2 * LANES
    bundle[at : at + F, :] = cluster[...].astype(jnp.float32)
    bundle[at + F : at + F + 8, :] = jnp.zeros((8, LANES), jnp.float32)
    bundle[at + F : at + F + table.shape[0], :] = table[...].astype(jnp.float32)
    at = F * src_mass.shape[0]
    src_own[at : at + src_mass.shape[0], :] = src_mass[...]
    bundle[TGT_AT : TGT_AT + F, :] = tgt_a[...]
    bundle[TGT_AT + F : TGT_AT + 2 * F, :] = tgt_b[...]
    masses = jnp.concatenate([mass_a[...], mass_b[...], jnp.ones((6, LANES), jnp.float32)], 0)
    bundle[TGT_AT + 2 * F :, :] = masses


def prepare(src_pts, cluster, table, src_cent, src_mass, *tgt):
    return pl.pallas_call(
        prepare_kernel,
        out_shape=(
            jax.ShapeDtypeStruct((TGT_AT + 2 * F + 8, LANES), jnp.float32),
            jax.ShapeDtypeStruct(((F + 1) * src_mass.shape[0], LANES), jnp.float32),
        ),
        in_specs=[VMEM] * 9,
        out_specs=(VMEM,) * 2,
        name="prepare",
    )(src_pts, cluster, table, src_cent, src_mass, *tgt)


def coarse_kernel(n_src, n_tgt, stored, *refs):
    src = refs[:n_src]
    tgt = refs[n_src : n_src + n_tgt]
    f_out, g_out, kernel, mass, dual, sums = refs[n_src + n_tgt :]
    ks, kt = f_out.shape[1], g_out.shape[1]
    wide_src = src[0].shape[0] // (F + 1)
    piece = wide_src * LANES
    tiles = kt // LANES
    y = jnp.concatenate(
        [ref[TGT_AT + F * e : TGT_AT + F * e + F, :] for ref in tgt for e in range(2)], 1
    )
    at = TGT_AT + 2 * F
    b = jnp.concatenate([ref[at + e : at + e + 1, :] for ref in tgt for e in range(2)], 1)
    right = pack_right(y, jnp.log2(b) - SCALE * square_norm(y))
    ones = jnp.ones((F, LANES), jnp.bfloat16)
    zero = jnp.zeros((8, kt), jnp.float32)
    high = jnp.full((8, LANES), jnp.inf, jnp.float32)

    def wide(values):
        return jnp.tile(values, (1, tiles))

    def over_sources(size, body, carry):
        for s in range(n_src):

            def chunk(k, carry, s=s):
                rows = pl.ds(pl.multiple_of(s * piece + k * size, size), size)
                x, values = source_columns(src[s], wide_src, k, size // LANES)
                left = pack_left(x, -SCALE * square_norm(x))
                return body(values, rows, left, carry)

            carry = lax.fori_loop(0, piece // size, chunk, carry)
        return carry

    def over_rows(size, body, carry):
        def chunk(k, carry):
            return body(pl.ds(pl.multiple_of(k * size, size), size), carry)

        return lax.fori_loop(0, ks // size, chunk, carry)

    def weigh(e, weighted, rows, carry):
        total, least = carry
        row_sum = jnp.broadcast_to(jnp.sum(weighted, 1, keepdims=True), (e.shape[0], LANES))
        sums[rows, :] = row_sum
        weight = mass[rows, :] / row_sum
        return total + fold(e * wide(weight), jnp.add), jnp.minimum(least, fold(row_sum, jnp.minimum))

    def close(total, least):
        total = jnp.sum(total, 0, keepdims=True)
        small = jnp.minimum(jnp.min(total), jnp.min(least)) < LOW
        return b / total, small.astype(jnp.int32)

    def spread_mass(values, rows, left, carry):
        mass[rows, :] = contract(constant_rows(values, 0, None), ones)
        if stored:
            kernel[rows, :] = contract(left, right)
        return carry

    over_sources(ROWS_PRODUCT, spread_mass, 0)

    def begin_rows(z, rows, carry):
        top = jnp.max(z, 1, keepdims=True)
        dual[rows, :] = jnp.broadcast_to(-top, (z.shape[0], LANES))
        e = jnp.exp2(z - top)
        if stored:
            kernel[rows, :] = e
        return weigh(e, e, rows, carry)

    if stored:
        carry = over_rows(ROWS_BEGIN, lambda rows, c: begin_rows(kernel[rows, :], rows, c), (zero, high))
    else:
        carry = over_sources(ROWS, lambda _, rows, left, c: begin_rows(contract(left, right), rows, c), (zero, high))
    scale, small = close(*carry)
    base = jnp.zeros((1, kt), jnp.float32)

    def rescue(base, scale):
        def rebase(rows, carry):
            dual[rows, :] = dual[rows, :] - jnp.log2(sums[rows, :])
            return carry

        over_rows(ROWS, rebase, 0)

        def tops(_, rows, left, top):
            return jnp.maximum(top, fold(contract(left, right) + wide(dual[rows, :]), jnp.maximum))

        top = jnp.max(over_sources(ROWS, tops, zero - jnp.inf), 0, keepdims=True)

        def step(_, rows, left, total):
            e = jnp.exp2(contract(left, right) + wide(dual[rows, :]) - top)
            return total + fold(e * wide(mass[rows, :]), jnp.add)

        total = jnp.sum(over_sources(ROWS, step, zero), 0, keepdims=True)
        over_rows(ROWS, unit, 0)
        return jnp.log2(b) - (top + jnp.log2(total)), jnp.ones_like(scale)

    def unit(rows, carry):
        sums[rows, :] = jnp.ones((ROWS, LANES), jnp.float32)
        return carry

    base, scale = lax.cond(small > 0, rescue, lambda base, scale: (base, scale), base, scale)

    def renew(base, scale):
        base = base + jnp.log2(scale)

        def step(_, rows, left, carry):
            f = dual[rows, :] - jnp.log2(sums[rows, :])
            dual[rows, :] = f
            e = jnp.exp2(contract(left, right) + wide(f) + base)
            if stored:
                kernel[rows, :] = e
            return weigh(e, e, rows, carry)

        scale, small = close(*over_sources(ROWS, step, (zero, high)))
        return base, scale, small

    def reuse(base, scale):
        def step(rows, carry):
            e = kernel[rows, :]
            return weigh(e, e * scale, rows, carry)

        scale, small = close(*over_rows(ROWS_TURN, step, (zero, high)))
        return base, scale, small

    def turn(_, state):
        base, scale, small = state
        if not stored:
            return renew(base, scale)
        return lax.cond(small > 0, renew, reuse, base, scale)

    base, scale, small = lax.fori_loop(1, ITERS, turn, (base, scale, small))
    g_out[...] = (base + jnp.log2(scale)) * (1.0 / SCALE)
    diagonal = lax.broadcasted_iota(jnp.int32, (LANES, LANES), 0) == lax.broadcasted_iota(
        jnp.int32, (LANES, LANES), 1
    )

    def to_lanes(k, carry):
        span = pl.ds(pl.multiple_of(k * LANES, LANES), LANES)
        f = dual[span, :] - jnp.log2(sums[span, :])
        f_out[:, span] = jnp.sum(jnp.where(diagonal, f, 0.0), 0, keepdims=True) * (1.0 / SCALE)
        return carry

    lax.fori_loop(0, ks // LANES, to_lanes, 0)

def coarse_duals(src, tgt):
    ks = sum(part.shape[0] // (F + 1) * LANES for part in src)
    kt = sum(2 * part.shape[1] for part in tgt)
    stored = ks * kt * 4 <= 16 * MIB
    return pl.pallas_call(
        functools.partial(coarse_kernel, len(src), len(tgt), stored),
        out_shape=(
            jax.ShapeDtypeStruct((1, ks), jnp.float32),
            jax.ShapeDtypeStruct((1, kt), jnp.float32),
        ),
        in_specs=[VMEM] * (len(src) + len(tgt)),
        out_specs=(VMEM, VMEM),
        scratch_shapes=[
            pltpu.VMEM((ks, kt) if stored else (8, LANES), jnp.float32),
            pltpu.VMEM((ks, LANES), jnp.float32),
            pltpu.VMEM((ks, LANES), jnp.float32),
            pltpu.VMEM((ks, LANES), jnp.float32),
        ],
        compiler_params=pltpu.CompilerParams(vmem_limit_bytes=48 * MIB),
        cost_estimate=pl.CostEstimate(
            flops=40 * ks * kt, bytes_accessed=4 * 24 * (ks + kt), transcendentals=9 * ks * kt
        ),
        name="coarse",
    )(*src, *tgt)


def look_up(table_ref, index):
    low = index & (LANES - 1)
    high = index >> 7
    out = jnp.zeros(index.shape, jnp.float32)
    for h in range(table_ref.shape[1] // LANES):
        row = jnp.broadcast_to(table_ref[0:1, h * LANES : (h + 1) * LANES], index.shape)
        out = jnp.where(high == h, jnp.take_along_axis(row, low, axis=1), out)
    return out


def targets_kernel(flip_ref, tgt_pts, tgt_cluster, g_table, packed, start_g):
    for k in range(2 * TB_DEV // 8):
        index = tgt_cluster[8 * k : 8 * k + 8, :] ^ flip_ref[0]
        start_g[8 * k : 8 * k + 8, :] = look_up(g_table, index)

    def pack_target(t, carry):
        y = tgt_pts[:, pl.ds(pl.multiple_of(t * BLK, BLK), BLK)]
        g = jnp.concatenate([start_g[pl.ds(2 * t, 1), :], start_g[pl.ds(2 * t + 1, 1), :]], 1)
        rows = pack_right(y, SCALE * (g - square_norm(y)))
        rows = jnp.concatenate([rows, jnp.zeros((LANES - KDIM, BLK), jnp.bfloat16)], 0)
        packed[t] = jnp.transpose(rows.astype(jnp.float32)).astype(jnp.bfloat16)
        return carry

    lax.fori_loop(0, TB_DEV, pack_target, 0, unroll=BLOCKS)
    packed[TB_DEV] = jnp.zeros((BLK, LANES), jnp.bfloat16)


def pack_targets(flip, tgt_pts, tgt_cluster, g_table):
    return pl.pallas_call(
        targets_kernel,
        out_shape=(
            jax.ShapeDtypeStruct((TB_DEV + 1, BLK, LANES), jnp.bfloat16),
            jax.ShapeDtypeStruct((2 * TB_DEV, LANES), jnp.float32),
        ),
        in_specs=[SMEM] + [VMEM] * 3,
        out_specs=(VMEM, VMEM),
        compiler_params=pltpu.CompilerParams(vmem_limit_bytes=16 * MIB),
        name="targets",
    )(flip, tgt_pts, tgt_cluster, g_table)


def fine_kernel(n_stacks, slots_each, stride, where_ref, *refs):
    stacks = refs[:n_stacks]
    packed, start_g, f_table, partial_out, start_f_out, fine_g_out = refs[n_stacks : n_stacks + 6]
    bundle, slot_rows, col_sum, col_top, codes, arrived, slots, order, count = refs[n_stacks + 6 :]
    devices = bundle.shape[0]
    depth = devices // n_stacks
    me, src_flip = where_ref[0], where_ref[1]

    def copy_of(n, first, rows, to, sem):
        source = stacks[n].at[:, pl.ds(first, rows), :]
        return pltpu.make_async_copy(source, to.at[pl.ds(n * depth, depth)], arrived.at[sem])

    early = [copy_of(n, SLOT_AT, 8, slot_rows, n) for n in range(n_stacks)]
    late = [copy_of(n, 0, SLOT_AT, bundle, n_stacks + n) for n in range(n_stacks)]
    for copy in early + late:
        copy.start()

    def sender(place):
        stack = place // depth
        return me ^ (2 * depth * (stack // 2) + 2 * (place % depth) + stack % 2)

    for t in range(TB_DEV + 1):
        count[t] = 0
    for copy in early:
        copy.wait()

    at = me * stride

    def slot_row(n, carry):
        codes[pl.ds(n, 1), :] = slot_rows[n, pl.ds(at // LANES, 1), :].astype(jnp.int32)
        return carry

    lax.fori_loop(0, devices, slot_row, 0, unroll=BLOCKS)
    codes[...] = pltpu.roll(codes[...], (LANES - at % LANES) % LANES, 1)
    to_scalars = pltpu.make_async_copy(codes, slots, arrived.at[2 * n_stacks])
    to_scalars.start()

    def fill(ref, value):
        def body(t, carry):
            ref[t] = jnp.full(ref.shape[1:], value, jnp.float32)
            return carry

        lax.fori_loop(0, ref.shape[0], body, 0)

    fill(col_sum, 0.0)
    to_scalars.wait()

    total = devices * slots_each
    unroll = math.gcd(PAIRS, total)

    def place(p, carry):
        used, unused = carry
        code = slots[p // slots_each, p % slots_each]
        valid = code > 0
        order[jnp.where(valid, used, unused)] = p
        t = jnp.where(valid, (code - 1) % TB_DEV, TB_DEV)
        count[t] = count[t] + 1
        step = valid.astype(jnp.int32)
        return used + step, unused - (1 - step)

    used, _ = lax.fori_loop(0, total, place, (jnp.int32(0), jnp.int32(total - 1)), unroll=16)
    for copy in late:
        copy.wait()
    index = bundle[0, 2 * LANES : SLOT_AT, :].astype(jnp.int32) ^ src_flip
    for half in range(2):
        rows = slice(8 * half, 8 * half + 8)
        start_f_out[rows, :] = look_up(f_table, index[rows])

    def cluster_rows(p):
        code = slots[p // slots_each, p % slots_each] - 1
        block = jnp.where(code >= 0, code // TB_DEV, 0)
        d = p // slots_each
        return [bundle[d, pl.ds(2 * LANES + 2 * block + k, 1), :] for k in range(2)]

    def starts(ps):
        out = []
        for n in range(0, len(ps), 4):
            rows = jnp.concatenate([r for p in ps[n:n+4] for r in cluster_rows(p)], 0)
            f = look_up(f_table, rows.astype(jnp.int32) ^ src_flip)
            for m in range(len(ps[n:n+4])):
                out.append(jnp.concatenate([f[2*m:2*m+1], f[2*m+1:2*m+2]], 1))
        return out

    def product(p, f):
        code = slots[p // slots_each, p % slots_each] - 1
        valid = code >= 0
        block = jnp.where(valid, code // TB_DEV, 0)
        t = jnp.where(valid, code % TB_DEV, TB_DEV)
        d = p // slots_each
        tile = [[bundle[d, pl.ds(pl.multiple_of(half * LANES + 16 * block + 8 * k, 8), 8), :] for k in range(2)] for half in range(2)]
        x = jnp.concatenate([jnp.concatenate(row, 1) for row in tile], 0)
        left = pack_left(x, SCALE * (f - square_norm(x)))
        left = jnp.concatenate([left, jnp.zeros((LANES - KDIM, BLK), jnp.bfloat16)], 0)
        z = jnp.dot(packed[t], left, preferred_element_type=jnp.float32)
        return t, d, SCALE * f, z

    def put(p, d, value):
        span = pl.ds(pl.multiple_of(p % slots_each * BLK, BLK), BLK)
        partial_out[sender(d), :, span] = value

    def pair(p, f, least, most):
        t, d, f, z = product(p, f)
        e = jnp.exp2(z)
        row = fold(e, jnp.add)
        col_sum[t] = col_sum[t] + (e[:, :LANES] + e[:, LANES:])
        row = jnp.sum(row, 0, keepdims=True)
        put(p, d, jnp.log2(row) - f)
        return jnp.minimum(least, row), jnp.maximum(most, row)

    def pairs(n, carry):
        ps = [order[unroll * n + u] for u in range(unroll)]
        fs = starts(ps)
        for u in range(unroll):
            carry = pair(ps[u], fs[u], *carry)
        return carry

    def lanes(t, carry):
        least, most = carry
        g = start_g[pl.ds(pl.multiple_of(2 * t, 2), 2), :]
        halves = []
        for k in range(2):
            block = col_sum[t, k * LANES : (k + 1) * LANES, :]
            halves.append(jnp.sum(jnp.transpose(block), 0, keepdims=True))
        s = jnp.concatenate(halves, 0)
        named = jnp.full((2, LANES), count[t].astype(jnp.float32) * float(BLK))
        term = EPS * jnp.log(named) - (jnp.log2(s) * (1.0 / SCALE) - g)
        fine_g_out[pl.ds(pl.multiple_of(2 * t, 2), 2), :] = 0.5 * (g + term)
        return jnp.minimum(least, s), jnp.maximum(most, s)

    least = jnp.full((1, BLK), jnp.inf, jnp.float32)
    least, most = lax.fori_loop(0, (used + unroll - 1) // unroll, pairs, (least, jnp.zeros((1, BLK), jnp.float32)))
    low, high = jnp.full((2, LANES), jnp.inf, jnp.float32), jnp.zeros((2, LANES), jnp.float32)
    low, high = lax.fori_loop(0, TB_DEV, lanes, (low, high), unroll=BLOCKS)
    fits = (jnp.minimum(jnp.min(least), jnp.min(low)) >= SMALL) & (jnp.maximum(jnp.max(most), jnp.max(high)) <= LARGE)

    @pl.when(jnp.logical_not(fits))
    def _():
        fill(col_sum, 0.0)
        fill(col_top, -1e30)

        def pair(n, carry):
            p = order[n]
            t, d, f, z = product(p, starts([p])[0])
            top = jnp.max(z, 0, keepdims=True)
            put(p, d, top + jnp.log2(jnp.sum(jnp.exp2(z - top), 0, keepdims=True)) - f)
            a, b = z[:, :LANES], z[:, LANES:]
            old = col_top[t]
            new = jnp.maximum(old, jnp.maximum(a, b))
            col_sum[t] = col_sum[t] * jnp.exp2(old - new) + (jnp.exp2(a - new) + jnp.exp2(b - new))
            col_top[t] = new
            return carry

        lax.fori_loop(0, used, pair, 0)

        def lanes(t, carry):
            for k in range(2):
                rows = slice(k * LANES, (k + 1) * LANES)
                top = jnp.transpose(col_top[t, rows, :])
                most = jnp.max(top, 0, keepdims=True)
                s = jnp.sum(jnp.transpose(col_sum[t, rows, :]) * jnp.exp2(top - most), 0, keepdims=True)
                g = start_g[pl.ds(2 * t + k, 1), :]
                named = jnp.full((1, LANES), count[t].astype(jnp.float32) * float(BLK))
                term = EPS * jnp.log(named) - ((most + jnp.log2(s)) * (1.0 / SCALE) - g)
                fine_g_out[pl.ds(2 * t + k, 1), :] = 0.5 * (g + term)
            return carry

        lax.fori_loop(0, TB_DEV, lanes, 0)

def fine_update(where, stacks, packed, start_g, f_table, slots_each, stride):
    devices = sum(stack.shape[0] for stack in stacks)
    return pl.pallas_call(
        functools.partial(fine_kernel, len(stacks), slots_each, stride),
        out_shape=(
            jax.ShapeDtypeStruct((devices, 1, slots_each * BLK), jnp.float32),
            jax.ShapeDtypeStruct((F, LANES), jnp.float32),
            jax.ShapeDtypeStruct((2 * TB_DEV, LANES), jnp.float32),
        ),
        in_specs=[SMEM] + [pl.BlockSpec(memory_space=pl.ANY)] * len(stacks) + [VMEM] * 3,
        out_specs=(VMEM, VMEM, VMEM),
        scratch_shapes=[
            pltpu.VMEM((devices, SLOT_AT, LANES), jnp.float32),
            pltpu.VMEM((devices, 8, LANES), jnp.float32),
            pltpu.VMEM((TB_DEV + 1, BLK, LANES), jnp.float32),
            pltpu.VMEM((TB_DEV + 1, BLK, LANES), jnp.float32),
            pltpu.VMEM((devices, LANES), jnp.int32),
            pltpu.SemaphoreType.DMA((2 * len(stacks) + 1,)),
            pltpu.SMEM((devices, LANES), jnp.int32),
            pltpu.SMEM((devices * slots_each,), jnp.int32),
            pltpu.SMEM((TB_DEV + 1,), jnp.int32),
        ],
        compiler_params=pltpu.CompilerParams(vmem_limit_bytes=44 * MIB),
        name="fine",
    )(where, *stacks, packed, start_g, f_table)


def finish_kernel(slots_each, slot_ref, partial, start_f, fine_f_out, gathered):
    for block in range(SB_DEV):
        for k in range(SUPP):
            slot = slot_ref[block * SUPP + k]
            span = pl.ds(pl.multiple_of(slot % slots_each * BLK, BLK), BLK)
            gathered[k, block : block + 1, :] = partial[slot // slots_each, :, span]
    values = gathered[...]
    top = jnp.max(values, 0)
    lse = top + jnp.log2(jnp.sum(jnp.exp2(values - top[None]), 0))
    term = EPS * math.log(float(SUPP * BLK)) - lse * (1.0 / SCALE)
    for block in range(SB_DEV):
        for k in range(2):
            row = slice(2 * block + k, 2 * block + k + 1)
            piece = term[block : block + 1, k * LANES : (k + 1) * LANES]
            fine_f_out[row, :] = 0.5 * (start_f[row, :] + piece)


def finish(slot_ids, partial, start_f, slots_each):
    return pl.pallas_call(
        functools.partial(finish_kernel, slots_each),
        out_shape=jax.ShapeDtypeStruct((F, LANES), jnp.float32),
        in_specs=[SMEM, VMEM, VMEM],
        out_specs=VMEM,
        scratch_shapes=[pltpu.VMEM((SUPP, SB_DEV, BLK), jnp.float32)],
        name="finish",
    )(slot_ids, partial, start_f)


def exchange(x, axis, flip):
    count = lax.axis_size(axis)
    return lax.ppermute(x, axis, [(i, i ^ flip) for i in range(count)])


def on_device(
    src_cent, tgt_cent, src_mass, tgt_mass, src_pts, tgt_pts, src_cluster, tgt_cluster, support
):
    n_row, n_col = lax.axis_size("row"), lax.axis_size("col")
    devices = n_row * n_col
    row, col = lax.axis_index("row"), lax.axis_index("col")
    me = row * n_col + col

    requests_each = SB_DEV * SUPP
    slots_each = requests_each // devices + 1
    wanted = support.reshape(-1)
    owners = wanted // TB_DEV
    positions = jnp.arange(requests_each, dtype=jnp.int32)
    earlier = (owners[None, :] == owners[:, None]) & (positions[None, :] < positions[:, None])
    slot_ids = owners * slots_each + jnp.sum(earlier.astype(jnp.int32), 1)
    codes = (positions // SUPP) * TB_DEV + wanted % TB_DEV + 1
    stride = 1 << (slots_each - 1).bit_length()
    filled = owners * stride + slot_ids % slots_each
    places = jnp.arange(devices * stride, dtype=jnp.int32)
    table = jnp.sum(jnp.where(filled[None, :] == places[:, None], codes[None, :], 0), 1)
    flat_mass = tgt_mass.reshape(-1, LANES)
    bundle, src_own = prepare(
        src_pts,
        src_cluster.reshape(F, LANES),
        table.reshape(-1, LANES),
        src_cent,
        src_mass.reshape(-1, LANES),
        tgt_cent,
        flat_mass,
        exchange(tgt_cent, "col", 1),
        exchange(flat_mass, "col", 1),
    )

    along = [bundle] + [exchange(bundle, "col", k) for k in range(2, n_col, 2)]
    src_all = [src_own] + [exchange(src_own, "row", k) for k in range(1, n_row)]
    stack = jnp.stack([part[:TGT_AT] for part in along])
    src_all, along, stack = lax.optimization_barrier((src_all, along, stack))
    stacks = [stack] + [exchange(stack, "row", k) for k in range(1, n_row)]
    f_table, g_table = coarse_duals(src_all, along)
    coarse_f = f_table[0, : src_cent.shape[1]]
    coarse_g = g_table[0, : tgt_cent.shape[1]]

    stacks, f_table, g_table = lax.optimization_barrier((stacks, f_table, g_table))
    stacks = [part for own in stacks for part in (own, exchange(own, "col", 1))]
    flip = (col * tgt_cent.shape[1]).astype(jnp.int32).reshape(1)
    tgt_cluster = tgt_cluster.reshape(2 * TB_DEV, LANES)
    packed, start_g = pack_targets(flip, tgt_pts, tgt_cluster, g_table)
    where = jnp.stack([me, row * src_cent.shape[1]]).astype(jnp.int32)
    partial, start_f, fine_g = fine_update(
        where, stacks, packed, start_g, f_table, slots_each, stride
    )
    returned = lax.all_to_all(partial, AXES, split_axis=0, concat_axis=0, tiled=True)
    fine_f = finish(slot_ids, returned, start_f, slots_each)
    return coarse_f, coarse_g, fine_f.reshape(-1), fine_g.reshape(-1)


def solution(mesh):
    in_specs = (
        P(None, "row"),
        P(None, "col"),
        P("row"),
        P("col"),
        P(None, AXES),
        P(None, AXES),
        P(AXES),
        P(AXES),
        P(AXES, None),
    )
    out_specs = (P("row"), P("col"), P(AXES), P(AXES))
    return jax.shard_map(
        on_device, mesh=mesh, in_specs=in_specs, out_specs=out_specs, check_vma=False
    )
```

```python
import functools
import math

import jax
import jax.numpy as jnp
from jax import lax
from jax.experimental import pallas as pl
from jax.experimental.pallas import tpu as pltpu
from jax.sharding import PartitionSpec as P

F = 16
BLK = 256
SUPP = 16
ITERS = 8
SB_DEV = 8
TB_DEV = 32
EPS = 0.1

SCALE = math.log2(math.e) / EPS
KDIM = 7 * F
LANES = 128
ROWS = 256
ROWS_PRODUCT = 1024
ROWS_BEGIN = 1024
ROWS_TURN = 512
PAIRS = 16
BLOCKS = 8
LOW = 2.0**-30
SMALL = 2.0**-80
LARGE = 2.0**100
MIB = 1024 * 1024
SLOT_AT = 2 * LANES + F
TGT_AT = SLOT_AT + 8
AXES = ("row", "chip", "core")
CHIPS = ("row", "chip")

VMEM = pl.BlockSpec(memory_space=pltpu.VMEM)
SMEM = pl.BlockSpec(memory_space=pltpu.SMEM)
CONTRACT_FIRST = (((0,), (0,)), ((), ()))


def split3(x):
    first = x.astype(jnp.bfloat16)
    rest = x - first.astype(jnp.float32)
    second = rest.astype(jnp.bfloat16)
    rest = rest - second.astype(jnp.float32)
    return first, second, rest.astype(jnp.bfloat16)


def constant_rows(values, at, ones_at):
    width = values.shape[1]
    parts = split3(jnp.broadcast_to(values, (F, width)))
    row = lax.broadcasted_iota(jnp.int32, (F, width), 0)
    rows = jnp.zeros((F, width), jnp.float32)
    for k, part in enumerate(parts):
        rows = jnp.where(row == at + k, part.astype(jnp.float32), rows)
    if ones_at is not None:
        rows = jnp.where((row >= ones_at) & (row < ones_at + 3), 1.0, rows)
    return rows.astype(jnp.bfloat16)


def pack_left(x, constant):
    a, b, c = split3(x * (2.0 * SCALE))
    return jnp.concatenate([a, a, b, b, a, c, constant_rows(constant, 0, 3)], 0)


def pack_right(y, constant):
    a, b, c = split3(y)
    return jnp.concatenate([a, b, a, b, c, a, constant_rows(constant, 3, 0)], 0)


def contract(left, right):
    return lax.dot_general(left, right, CONTRACT_FIRST, preferred_element_type=jnp.float32)


def square_norm(x):
    return jnp.sum(x * x, 0, keepdims=True)


def fold(values, combine):
    out = values[0:8]
    for k in range(1, values.shape[0] // 8):
        out = combine(out, values[8 * k : 8 * k + 8])
    return out


def source_columns(ref, count, k, n):
    halves = [
        jnp.concatenate(
            [
                ref[pl.ds(pl.multiple_of(8 * (half * count + k * n + i), 8), 8), :]
                for i in range(n)
            ],
            1,
        )
        for half in range(2)
    ]
    values = [ref[pl.ds(F * count + k * n + i, 1), :] for i in range(n)]
    return jnp.concatenate(halves, 0), jnp.concatenate(values, 1)


def to_tiles(ref, out):
    count = ref.shape[1] // LANES
    for half in range(2):
        for i in range(count):
            at = 8 * (half * count + i)
            out[at : at + 8, :] = ref[8 * half : 8 * half + 8, i * LANES : (i + 1) * LANES]


def prepare_kernel(
    src_pts, cluster, table, src_cent, src_mass, tgt_a, mass_a, tgt_b, mass_b, bundle, src_own
):
    to_tiles(src_cent, src_own)
    src_own[F * src_mass.shape[0] :, :] = src_mass[...]
    to_tiles(src_pts, bundle)
    bundle[2 * LANES : SLOT_AT, :] = cluster[...].astype(jnp.float32)
    bundle[SLOT_AT:TGT_AT, :] = jnp.zeros((TGT_AT - SLOT_AT, LANES), jnp.float32)
    bundle[SLOT_AT : SLOT_AT + table.shape[0], :] = table[...].astype(jnp.float32)
    bundle[TGT_AT : TGT_AT + F, :] = tgt_a[...]
    bundle[TGT_AT + F : TGT_AT + 2 * F, :] = tgt_b[...]
    masses = jnp.concatenate([mass_a[...], mass_b[...], jnp.ones((6, LANES), jnp.float32)], 0)
    bundle[TGT_AT + 2 * F :, :] = masses


def prepare(src_pts, cluster, table, src_cent, src_mass, tgt):
    return pl.pallas_call(
        prepare_kernel,
        out_shape=(
            jax.ShapeDtypeStruct((TGT_AT + 2 * F + 8, LANES), jnp.float32),
            jax.ShapeDtypeStruct(((F + 1) * src_mass.shape[0], LANES), jnp.float32),
        ),
        in_specs=[VMEM] * 9,
        out_specs=(VMEM, VMEM),
        name="prepare",
    )(src_pts, cluster, table, src_cent, src_mass, *tgt)


def coarse_kernel(n_src, n_tgt, stored, *refs):
    given_src = refs[:n_src]
    given_tgt = refs[n_src : n_src + n_tgt]
    f_out, g_out, kernel, mass, dual, sums, all_src, all_tgt, arrived, *ahead = refs[n_src + n_tgt :]
    src = [all_src.at[n] for n in range(n_src)]
    tgt = [all_tgt.at[n] for n in range(n_tgt)]
    copies = [
        pltpu.make_async_copy(given.at[pl.ds(TGT_AT, 2 * F + 8)], held, arrived.at[n])
        for n, (given, held) in enumerate(zip(given_tgt, tgt))
    ]
    copies += [
        pltpu.make_async_copy(given, held, arrived.at[n_tgt + n])
        for n, (given, held) in enumerate(zip(given_src, src))
    ]
    for copy in copies:
        copy.start()
    for copy in copies:
        copy.wait()
    ks, kt = f_out.shape[1], g_out.shape[1]
    wide_src = src[0].shape[0] // (F + 1)
    piece = wide_src * LANES
    tiles = kt // LANES
    y = jnp.concatenate(
        [ref[F * e : F * e + F, :] for ref in tgt for e in range(2)], 1
    )
    at = 2 * F
    b = jnp.concatenate([ref[at + e : at + e + 1, :] for ref in tgt for e in range(2)], 1)
    right = pack_right(y, jnp.log2(b) - SCALE * square_norm(y))
    ones = jnp.ones((F, LANES), jnp.bfloat16)
    zero = jnp.zeros((8, kt), jnp.float32)
    high = jnp.full((8, LANES), jnp.inf, jnp.float32)

    def wide(values):
        return jnp.tile(values, (1, tiles))

    def over_sources(size, body, carry):
        for s in range(n_src):

            def chunk(k, carry, s=s):
                rows = pl.ds(pl.multiple_of(s * piece + k * size, size), size)
                x, values = source_columns(src[s], wide_src, k, size // LANES)
                left = pack_left(x, -SCALE * square_norm(x))
                return body(values, rows, left, carry)

            carry = lax.fori_loop(0, piece // size, chunk, carry)
        return carry

    def over_rows(size, body, carry):
        def chunk(k, carry):
            return body(pl.ds(pl.multiple_of(k * size, size), size), carry)

        return lax.fori_loop(0, ks // size, chunk, carry)

    def weigh(e, weighted, rows, carry):
        total, least = carry
        row_sum = jnp.broadcast_to(jnp.sum(weighted, 1, keepdims=True), (e.shape[0], LANES))
        sums[rows, :] = row_sum
        weight = mass[rows, :] / row_sum
        return total + fold(e * wide(weight), jnp.add), jnp.minimum(least, fold(row_sum, jnp.minimum))

    def close(total, least):
        total = jnp.sum(total, 0, keepdims=True)
        small = jnp.minimum(jnp.min(total), jnp.min(least)) < LOW
        return b / total, small.astype(jnp.int32)

    def spread_mass(values, rows):
        mass[rows, :] = contract(constant_rows(values, 0, None), ones)

    def begin_rows(z, rows, carry):
        top = jnp.max(z, 1, keepdims=True)
        dual[rows, :] = jnp.broadcast_to(-top, (z.shape[0], LANES))
        e = jnp.exp2(z - top)
        if stored:
            kernel[rows, :] = e
        return weigh(e, e, rows, carry)

    def begin(values, rows, left, carry):
        spread_mass(values, rows)
        return begin_rows(contract(left, right), rows, carry)

    if stored:
        def products(s, out):
            rows = slice(s * piece, (s + 1) * piece)
            x, values = source_columns(src[s], wide_src, 0, wide_src)
            out[...] = contract(pack_left(x, -SCALE * square_norm(x)), right)
            spread_mass(values, rows)

        products(0, ahead[0])
        carry = (zero, high)
        for s in range(n_src):
            if s + 1 < n_src:
                products(s + 1, ahead[(s + 1) % 2])
            carry = begin_rows(ahead[s % 2][...], slice(s * piece, (s + 1) * piece), carry)
    else:
        carry = over_sources(ROWS, begin, (zero, high))
    scale, small = close(*carry)
    base = jnp.zeros((1, kt), jnp.float32)

    def rescue(base, scale):
        def rebase(rows, carry):
            dual[rows, :] = dual[rows, :] - jnp.log2(sums[rows, :])
            return carry

        over_rows(ROWS, rebase, 0)

        def tops(_, rows, left, top):
            return jnp.maximum(top, fold(contract(left, right) + wide(dual[rows, :]), jnp.maximum))

        top = jnp.max(over_sources(ROWS, tops, zero - jnp.inf), 0, keepdims=True)

        def step(_, rows, left, total):
            e = jnp.exp2(contract(left, right) + wide(dual[rows, :]) - top)
            return total + fold(e * wide(mass[rows, :]), jnp.add)

        total = jnp.sum(over_sources(ROWS, step, zero), 0, keepdims=True)
        over_rows(ROWS, unit, 0)
        return jnp.log2(b) - (top + jnp.log2(total)), jnp.ones_like(scale)

    def unit(rows, carry):
        sums[rows, :] = jnp.ones((ROWS, LANES), jnp.float32)
        return carry

    base, scale = lax.cond(small > 0, rescue, lambda base, scale: (base, scale), base, scale)

    def renew(base, scale):
        base = base + jnp.log2(scale)

        def step(_, rows, left, carry):
            f = dual[rows, :] - jnp.log2(sums[rows, :])
            dual[rows, :] = f
            e = jnp.exp2(contract(left, right) + wide(f) + base)
            if stored:
                kernel[rows, :] = e
            return weigh(e, e, rows, carry)

        scale, small = close(*over_sources(ROWS, step, (zero, high)))
        return base, scale, small

    def reuse(base, scale):
        def step(rows, carry):
            e = kernel[rows, :]
            return weigh(e, e * scale, rows, carry)

        scale, small = close(*over_rows(ROWS_TURN, step, (zero, high)))
        return base, scale, small

    def turn(_, state):
        base, scale, small = state
        if not stored:
            return renew(base, scale)
        return lax.cond(small > 0, renew, reuse, base, scale)

    base, scale, small = lax.fori_loop(1, ITERS, turn, (base, scale, small))
    g_out[...] = (base + jnp.log2(scale)) * (1.0 / SCALE)
    diagonal = lax.broadcasted_iota(jnp.int32, (LANES, LANES), 0) == lax.broadcasted_iota(
        jnp.int32, (LANES, LANES), 1
    )

    def to_lanes(k, carry):
        span = pl.ds(pl.multiple_of(k * LANES, LANES), LANES)
        f = dual[span, :] - jnp.log2(sums[span, :])
        f_out[:, span] = jnp.sum(jnp.where(diagonal, f, 0.0), 0, keepdims=True) * (1.0 / SCALE)
        return carry

    lax.fori_loop(0, ks // LANES, to_lanes, 0)

def coarse_duals(src, tgt):
    ks = sum(part.shape[0] // (F + 1) * LANES for part in src)
    kt = sum(2 * part.shape[1] for part in tgt)
    stored = ks * kt * 4 <= 16 * MIB
    return pl.pallas_call(
        functools.partial(coarse_kernel, len(src), len(tgt), stored),
        out_shape=(
            jax.ShapeDtypeStruct((1, ks), jnp.float32),
            jax.ShapeDtypeStruct((1, kt), jnp.float32),
        ),
        in_specs=[VMEM] * (len(src) + len(tgt)),
        out_specs=(VMEM, VMEM),
        scratch_shapes=[
            pltpu.VMEM((ks, kt) if stored else (8, LANES), jnp.float32),
        ]
        + [pltpu.VMEM((ks, LANES), jnp.float32)] * 3
        + [
            pltpu.VMEM((len(src),) + src[0].shape, jnp.float32),
            pltpu.VMEM((len(tgt), 2 * F + 8, LANES), jnp.float32),
            pltpu.SemaphoreType.DMA((len(src) + len(tgt),)),
        ]
        + [pltpu.VMEM((ks // len(src), kt) if stored else (8, LANES), jnp.float32)] * 2,
        compiler_params=pltpu.CompilerParams(vmem_limit_bytes=36 * MIB),
        cost_estimate=pl.CostEstimate(
            flops=40 * ks * kt, bytes_accessed=4 * 24 * (ks + kt), transcendentals=9 * ks * kt
        ),
        name="coarse",
    )(*src, *tgt)


def look_up(table_ref, index):
    low = index & (LANES - 1)
    high = index >> 7
    out = jnp.zeros(index.shape, jnp.float32)
    for h in range(table_ref.shape[1] // LANES):
        row = jnp.broadcast_to(table_ref[0:1, h * LANES : (h + 1) * LANES], index.shape)
        out = jnp.where(high == h, jnp.take_along_axis(row, low, axis=1), out)
    return out


def fine_kernel(n_stacks, slots_each, stride, where_ref, *refs):
    stacks = refs[:n_stacks]
    points_a, points_b, cluster_a, cluster_b, f_table, g_table = refs[n_stacks : n_stacks + 6]
    partial_out, kept = refs[n_stacks + 6 : n_stacks + 8]
    bundle, slot_rows, start_g, packed, col_sum, col_top, codes, arrived, slots, count = refs[
        n_stacks + 8 : n_stacks + 18
    ]
    order_t, order_block, order_from, order_span = refs[n_stacks + 18 :]
    senders = bundle.shape[0]
    depth = senders // n_stacks
    blocks = 2 * TB_DEV
    sums_out = kept
    start_g_at = 3 * blocks
    start_f_at = start_g_at + 2 * TB_DEV
    me, core, src_flip, tgt_flip = (where_ref[k] for k in range(4))

    def copy_of(n, first, rows, to, sem):
        source = stacks[n].at[:, pl.ds(first, rows), :]
        return pltpu.make_async_copy(source, to.at[pl.ds(n * depth, depth)], arrived.at[sem])

    early = [copy_of(n, SLOT_AT, 8, slot_rows, n) for n in range(n_stacks)]
    late = [copy_of(n, 0, SLOT_AT, bundle, n_stacks + n) for n in range(n_stacks)]
    for copy in early + late:
        copy.start()

    for side, cluster in enumerate((cluster_a, cluster_b)):
        for k in range(2 * TB_DEV // 8):
            index = cluster[8 * k : 8 * k + 8, :] ^ tgt_flip
            at = 2 * TB_DEV * side + 8 * k
            start_g[at : at + 8, :] = look_up(g_table, index)
    kept[start_g_at:start_f_at, :] = start_g[0 : 2 * TB_DEV, :]
    for t in range(blocks + 1):
        count[t] = 0
    for copy in early:
        copy.wait()

    at = me * 2 * stride

    def slot_row(n, carry):
        codes[pl.ds(n, 1), :] = slot_rows[n, pl.ds(at // LANES, 1), :].astype(jnp.int32)
        return carry

    lax.fori_loop(0, senders, slot_row, 0, unroll=BLOCKS)
    codes[...] = pltpu.roll(codes[...], (LANES - at % LANES) % LANES, 1)
    to_scalars = pltpu.make_async_copy(codes, slots, arrived.at[2 * n_stacks])
    to_scalars.start()

    for side, points in enumerate((points_a, points_b)):

        def pack_target(t, carry, side=side, points=points):
            y = points[:, pl.ds(pl.multiple_of(t * BLK, BLK), BLK)]
            row = 2 * (side * TB_DEV + t)
            g = jnp.concatenate([start_g[pl.ds(row, 1), :], start_g[pl.ds(row + 1, 1), :]], 1)
            rows = pack_right(y, SCALE * (g - square_norm(y)))
            rows = jnp.concatenate([rows, jnp.zeros((LANES - KDIM, BLK), jnp.bfloat16)], 0)
            packed[side * TB_DEV + t] = jnp.transpose(rows.astype(jnp.float32)).astype(jnp.bfloat16)
            col_sum[side * TB_DEV + t] = jnp.zeros((BLK, LANES), jnp.float32)
            return carry

        lax.fori_loop(0, TB_DEV, pack_target, 0, unroll=BLOCKS)
    packed[blocks] = jnp.zeros((BLK, LANES), jnp.bfloat16)
    col_sum[blocks] = jnp.zeros((BLK, LANES), jnp.float32)
    to_scalars.wait()

    each = 2 * slots_each
    total = senders * each
    unroll = math.gcd(PAIRS, total)

    def place(d, carry):
        used, unused = carry
        for rest in range(each):
            owner, s = divmod(rest, slots_each)
            code = slots[d, owner * stride + s]
            valid = code > 0
            t = jnp.where(valid, (code - 1) % TB_DEV + TB_DEV * (owner ^ core), blocks)
            n = jnp.where(valid, used, unused)
            order_t[n] = t
            order_block[n] = jnp.where(valid, (code - 1) // TB_DEV, 0)
            order_from[n] = d
            order_span[n] = rest * BLK
            count[t] = count[t] + 1
            step = valid.astype(jnp.int32)
            used, unused = used + step, unused - (1 - step)
        return used, unused

    used, _ = lax.fori_loop(0, senders, place, (jnp.int32(0), jnp.int32(total - 1)))
    for copy in late:
        copy.wait()
    index = bundle[0, 2 * LANES : SLOT_AT, :].astype(jnp.int32) ^ src_flip
    for half in range(2):
        rows = slice(8 * half, 8 * half + 8)
        at = start_f_at + 8 * half
        kept[at : at + 8, :] = look_up(f_table, index[rows])

    def cluster_rows(n):
        at = 2 * LANES + 2 * order_block[n]
        return [bundle[order_from[n], pl.ds(at + k, 1), :] for k in range(2)]

    def starts(ps):
        out = []
        for n in range(0, len(ps), 4):
            rows = jnp.concatenate([r for p in ps[n:n+4] for r in cluster_rows(p)], 0)
            f = look_up(f_table, rows.astype(jnp.int32) ^ src_flip)
            for m in range(len(ps[n:n+4])):
                out.append(jnp.concatenate([f[2*m:2*m+1], f[2*m+1:2*m+2]], 1))
        return out

    def product(p, f):
        t, block, d = order_t[p], order_block[p], order_from[p]
        tile = [[bundle[d, pl.ds(pl.multiple_of(half * LANES + 16 * block + 8 * k, 8), 8), :] for k in range(2)] for half in range(2)]
        x = jnp.concatenate([jnp.concatenate(row, 1) for row in tile], 0)
        left = pack_left(x, SCALE * (f - square_norm(x)))
        left = jnp.concatenate([left, jnp.zeros((LANES - KDIM, BLK), jnp.bfloat16)], 0)
        z = jnp.dot(packed[t], left, preferred_element_type=jnp.float32)
        return t, d, SCALE * f, z

    def put(p, d, value):
        span = pl.ds(pl.multiple_of(order_span[p], BLK), BLK)
        partial_out[me ^ d, :, span] = value

    def pair(p, f, least, most):
        t, d, f, z = product(p, f)
        e = jnp.exp2(z)
        row = fold(e, jnp.add)
        col_sum[t] = col_sum[t] + (e[:, :LANES] + e[:, LANES:])
        row = jnp.sum(row, 0, keepdims=True)
        put(p, d, jnp.log2(row) - f)
        return jnp.minimum(least, row), jnp.maximum(most, row)

    def pairs(n, carry):
        ps = [unroll * n + u for u in range(unroll)]
        fs = starts(ps)
        for u in range(unroll):
            carry = pair(ps[u], fs[u], *carry)
        return carry

    def lanes(t, carry):
        least, most = carry
        halves = []
        for k in range(2):
            block = jnp.transpose(col_sum[t, k * LANES : (k + 1) * LANES, :])
            halves.append(jnp.sum(block, 0, keepdims=True))
        s = jnp.concatenate(halves, 0)
        sums_out[pl.ds(pl.multiple_of(2 * t, 2), 2), :] = jnp.log2(s)
        sums_out[pl.ds(2 * blocks + t, 1), :] = jnp.full((1, LANES), count[t].astype(jnp.float32))
        return jnp.minimum(least, jnp.where(count[t] > 0, s, LARGE)), jnp.maximum(most, s)

    least = jnp.full((1, BLK), LARGE, jnp.float32)
    most = jnp.zeros((1, BLK), jnp.float32)
    least, most = lax.fori_loop(0, (used + unroll - 1) // unroll, pairs, (least, most))
    low = jnp.full((2, LANES), LARGE, jnp.float32)
    high = jnp.zeros((2, LANES), jnp.float32)
    low, high = lax.fori_loop(0, blocks, lanes, (low, high), unroll=BLOCKS)
    smallest = jnp.minimum(jnp.min(least), jnp.min(low))
    largest = jnp.maximum(jnp.max(most), jnp.max(high))
    fits = (smallest >= SMALL) & (largest <= LARGE)

    @pl.when(jnp.logical_not(fits))
    def _():
        def fill(t, carry):
            col_sum[t] = jnp.zeros((BLK, LANES), jnp.float32)
            col_top[t] = jnp.full((BLK, LANES), -1e30, jnp.float32)
            return carry

        lax.fori_loop(0, blocks + 1, fill, 0)

        def pair(n, carry):
            p = n
            t, d, f, z = product(p, starts([p])[0])
            top = jnp.max(z, 0, keepdims=True)
            put(p, d, top + jnp.log2(jnp.sum(jnp.exp2(z - top), 0, keepdims=True)) - f)
            a, b = z[:, :LANES], z[:, LANES:]
            old = col_top[t]
            new = jnp.maximum(old, jnp.maximum(a, b))
            col_sum[t] = col_sum[t] * jnp.exp2(old - new) + (jnp.exp2(a - new) + jnp.exp2(b - new))
            col_top[t] = new
            return carry

        lax.fori_loop(0, used, pair, 0)

        def lanes(t, carry):
            for k in range(2):
                rows = slice(k * LANES, (k + 1) * LANES)
                top = jnp.transpose(col_top[t, rows, :])
                most = jnp.max(top, 0, keepdims=True)
                s = jnp.sum(jnp.transpose(col_sum[t, rows, :]) * jnp.exp2(top - most), 0, keepdims=True)
                sums_out[pl.ds(2 * t + k, 1), :] = most + jnp.log2(s)
            return carry

        lax.fori_loop(0, blocks, lanes, 0)


def fine_update(where, stacks, points, clusters, f_table, g_table, slots_each, stride):
    senders = sum(stack.shape[0] for stack in stacks)
    blocks = 2 * TB_DEV
    return pl.pallas_call(
        functools.partial(fine_kernel, len(stacks), slots_each, stride),
        out_shape=(
            jax.ShapeDtypeStruct((senders, 1, 2 * slots_each * BLK), jnp.float32),
            jax.ShapeDtypeStruct((3 * blocks + 2 * TB_DEV + F, LANES), jnp.float32),
        ),
        in_specs=[SMEM] + [pl.BlockSpec(memory_space=pl.ANY)] * len(stacks) + [VMEM] * 6,
        out_specs=(VMEM, VMEM),
        scratch_shapes=[
            pltpu.VMEM((senders, SLOT_AT, LANES), jnp.float32),
            pltpu.VMEM((senders, 8, LANES), jnp.float32),
            pltpu.VMEM((2 * blocks, LANES), jnp.float32),
            pltpu.VMEM((blocks + 1, BLK, LANES), jnp.bfloat16),
            pltpu.VMEM((blocks + 1, BLK, LANES), jnp.float32),
            pltpu.VMEM((blocks + 1, BLK, LANES), jnp.float32),
            pltpu.VMEM((senders, LANES), jnp.int32),
            pltpu.SemaphoreType.DMA((2 * len(stacks) + 1,)),
            pltpu.SMEM((senders, LANES), jnp.int32),
            pltpu.SMEM((blocks + 1,), jnp.int32),
        ]
        + [pltpu.SMEM((senders * 2 * slots_each,), jnp.int32)] * 4,
        compiler_params=pltpu.CompilerParams(vmem_limit_bytes=(28 + senders // 8) * MIB),
        name="fine",
    )(where, *stacks, *points, *clusters, f_table, g_table)


def finish_kernel(
    from_ref, span_ref, own, other, partial, fine_f_out, fine_g_out, gathered
):
    rows = 2 * TB_DEV
    a, b = own[0:rows, :], other[rows : 2 * rows, :]
    top = jnp.maximum(a, b)
    lse = top + jnp.log2(jnp.exp2(a - top) + jnp.exp2(b - top))
    counts = 2 * rows
    g = own[3 * rows : 4 * rows, :]
    named = own[counts : counts + TB_DEV, :] + other[counts + TB_DEV : counts + 2 * TB_DEV, :]
    logs = EPS * jnp.log(named * float(BLK))
    base = g - (lse * (1.0 / SCALE) - g)
    for t in range(TB_DEV):
        span = slice(2 * t, 2 * t + 2)
        fine_g_out[span, :] = 0.5 * (base[span, :] + logs[t : t + 1, :])
    for block in range(SB_DEV):
        for k in range(SUPP):
            n = block * SUPP + k
            span = pl.ds(pl.multiple_of(span_ref[n], BLK), BLK)
            gathered[k, block : block + 1, :] = partial[from_ref[n], :, span]
    values = gathered[...]
    top = jnp.max(values, 0)
    lse = top + jnp.log2(jnp.sum(jnp.exp2(values - top[None]), 0))
    term = EPS * math.log(float(SUPP * BLK)) - lse * (1.0 / SCALE)
    for block in range(SB_DEV):
        for k in range(2):
            row = slice(2 * block + k, 2 * block + k + 1)
            piece = term[block : block + 1, k * LANES : (k + 1) * LANES]
            start_f = own[4 * rows + 2 * block + k : 4 * rows + 2 * block + k + 1, :]
            fine_f_out[row, :] = 0.5 * (start_f + piece)


def finish(chips, spans, own, other, partial):
    return pl.pallas_call(
        finish_kernel,
        out_shape=(
            jax.ShapeDtypeStruct((F, LANES), jnp.float32),
            jax.ShapeDtypeStruct((2 * TB_DEV, LANES), jnp.float32),
        ),
        in_specs=[SMEM, SMEM] + [VMEM] * 3,
        out_specs=(VMEM, VMEM),
        scratch_shapes=[pltpu.VMEM((SUPP, SB_DEV, BLK), jnp.float32)],
        name="finish",
    )(chips, spans, own, other, partial)


def exchange(x, axis, flip):
    count = lax.axis_size(axis)
    return lax.ppermute(x, axis, [(i, i ^ flip) for i in range(count)])


def on_device(
    src_cent, tgt_cent, src_mass, tgt_mass, src_pts, tgt_pts, src_cluster, tgt_cluster, support
):
    n_row, n_chip, n_core = (lax.axis_size(axis) for axis in AXES)
    devices = n_row * n_chip * n_core
    row, chip, core = (lax.axis_index(axis) for axis in AXES)

    flat_mass = tgt_mass.reshape(-1, LANES)
    tgt = [tgt_cent, flat_mass, exchange(tgt_cent, "core", 1), exchange(flat_mass, "core", 1)]

    tgt_cluster = tgt_cluster.reshape(2 * TB_DEV, LANES)
    requests_each = SB_DEV * SUPP
    slots_each = requests_each // devices + 1
    stride = 1 << (slots_each - 1).bit_length()
    wanted = support.reshape(-1)
    owners = wanted // TB_DEV
    positions = jnp.arange(requests_each, dtype=jnp.int32)
    earlier = (owners[None, :] == owners[:, None]) & (positions[None, :] < positions[:, None])
    occurs = jnp.sum(earlier.astype(jnp.int32), 1)
    codes = (positions // SUPP) * TB_DEV + wanted % TB_DEV + 1
    places = jnp.arange(devices * stride, dtype=jnp.int32)
    filled = owners * stride + occurs
    table = jnp.sum(jnp.where(filled[None, :] == places[:, None], codes[None, :], 0), 1)
    chips = owners // n_core
    spans = (owners % n_core * slots_each + occurs) * BLK
    bundle, src_own = prepare(
        src_pts,
        src_cluster.reshape(F, LANES),
        table.reshape(-1, LANES),
        src_cent,
        src_mass.reshape(-1, LANES),
        tgt,
    )
    along = [bundle] + [exchange(bundle, "chip", k) for k in range(1, n_chip)]
    src_all = [src_own] + [exchange(src_own, "row", k) for k in range(1, 3)]
    src_own, src_all[1] = lax.optimization_barrier((src_own, src_all[1]))
    src_all += [exchange(src_own, "row", k) for k in range(3, n_row)]
    stack = jnp.stack([part[:TGT_AT] for part in along])
    src_all, along, stack = lax.optimization_barrier((src_all, along, stack))
    stacks = [stack] + [exchange(stack, "row", k) for k in range(1, n_row)]
    f_table, g_table = coarse_duals(src_all, along)
    tgt_pts, tgt_cluster, f_table, g_table = lax.optimization_barrier(
        (tgt_pts, tgt_cluster, f_table, g_table)
    )
    points = [tgt_pts, exchange(tgt_pts, "core", 1)]
    clusters = [tgt_cluster, exchange(tgt_cluster, "core", 1)]
    coarse_f = f_table[0, : src_cent.shape[1]]
    coarse_g = g_table[0, : tgt_cent.shape[1]]

    col = chip * n_core + core
    where = [row * n_chip + chip, core, row * src_cent.shape[1], col * tgt_cent.shape[1]]
    partial, kept = fine_update(
        jnp.stack(where).astype(jnp.int32),
        stacks,
        points,
        clusters,
        f_table,
        g_table,
        slots_each,
        stride,
    )
    returned = lax.all_to_all(partial, CHIPS, split_axis=0, concat_axis=0, tiled=True)
    other = exchange(kept, "core", 1)
    fine_f, fine_g = finish(chips, spans, kept, other, returned)
    return coarse_f, coarse_g, fine_f.reshape(-1), fine_g.reshape(-1)


def solution(mesh):
    n_row, n_col = mesh.devices.shape
    cores = jax.sharding.Mesh(mesh.devices.reshape(n_row, n_col // 2, 2), AXES)
    col = CHIPS[1:] + AXES[2:]
    in_specs = (
        P(None, "row"),
        P(None, col),
        P("row"),
        P(col),
        P(None, AXES),
        P(None, AXES),
        P(AXES),
        P(AXES),
        P(AXES, None),
    )
    out_specs = (P("row"), P(col), P(AXES), P(AXES))
    return jax.shard_map(
        on_device, mesh=cores, in_specs=in_specs, out_specs=out_specs, check_vma=False
    )
```

```python
import functools
import math

import jax
import jax.numpy as jnp
from jax import lax
from jax.experimental import pallas as pl
from jax.experimental.pallas import tpu as pltpu
from jax.sharding import PartitionSpec as P

F = 16
BLK = 256
SUPP = 16
ITERS = 8
SB_DEV = 8
TB_DEV = 32
EPS = 0.1

SCALE = math.log2(math.e) / EPS
KDIM = 7 * F
LANES = 128
ROWS = 256
ROWS_PRODUCT = 1024
ROWS_BEGIN = 1024
ROWS_TURN = 512
PAIRS = 32
BLOCKS = 16
LOW = 2.0**-30
SMALL = 2.0**-80
LARGE = 2.0**100
MIB = 1024 * 1024
SLOT_AT = 2 * LANES + F
TGT_AT = SLOT_AT + 8
AXES = ("row", "chip", "core")
CHIPS = ("row", "chip")

VMEM = pl.BlockSpec(memory_space=pltpu.VMEM)
SMEM = pl.BlockSpec(memory_space=pltpu.SMEM)
CONTRACT_FIRST = (((0,), (0,)), ((), ()))


def split3(x):
    first = x.astype(jnp.bfloat16)
    rest = x - first.astype(jnp.float32)
    second = rest.astype(jnp.bfloat16)
    rest = rest - second.astype(jnp.float32)
    return first, second, rest.astype(jnp.bfloat16)


def constant_rows(values, at, ones_at):
    width = values.shape[1]
    parts = split3(jnp.broadcast_to(values, (F, width)))
    row = lax.broadcasted_iota(jnp.int32, (F, width), 0)
    rows = jnp.zeros((F, width), jnp.float32)
    for k, part in enumerate(parts):
        rows = jnp.where(row == at + k, part.astype(jnp.float32), rows)
    if ones_at is not None:
        rows = jnp.where((row >= ones_at) & (row < ones_at + 3), 1.0, rows)
    return rows.astype(jnp.bfloat16)


def pack_left(x, constant):
    a, b, c = split3(x * (2.0 * SCALE))
    return jnp.concatenate([a, a, b, b, a, c, constant_rows(constant, 0, 3)], 0)


def pack_right(y, constant):
    a, b, c = split3(y)
    return jnp.concatenate([a, b, a, b, c, a, constant_rows(constant, 3, 0)], 0)


def contract(left, right):
    return lax.dot_general(left, right, CONTRACT_FIRST, preferred_element_type=jnp.float32)


def square_norm(x):
    return jnp.sum(x * x, 0, keepdims=True)


def fold(values, combine):
    out = values[0:8]
    for k in range(1, values.shape[0] // 8):
        out = combine(out, values[8 * k : 8 * k + 8])
    return out


def source_columns(ref, count, k, n):
    halves = [
        jnp.concatenate(
            [
                ref[pl.ds(pl.multiple_of(8 * (half * count + k * n + i), 8), 8), :]
                for i in range(n)
            ],
            1,
        )
        for half in range(2)
    ]
    values = [ref[pl.ds(F * count + k * n + i, 1), :] for i in range(n)]
    return jnp.concatenate(halves, 0), jnp.concatenate(values, 1)


def to_tiles(ref, out):
    count = ref.shape[1] // LANES
    for half in range(2):
        for i in range(count):
            at = 8 * (half * count + i)
            out[at : at + 8, :] = ref[8 * half : 8 * half + 8, i * LANES : (i + 1) * LANES]


def prepare_kernel(
    rows, slots_each, stride, wanted, src_pts, cluster, src_cent, src_mass, tgt_a, mass_a, tgt_b, mass_b,
    bundle, src_own, places,
):
    shape = (LANES, LANES)
    down = lax.broadcasted_iota(jnp.int32, shape, 0)
    across = lax.broadcasted_iota(jnp.int32, shape, 1)
    block_bits = TB_DEV.bit_length() - 1
    entry = wanted[...]
    owners = entry >> block_bits

    def turned(values):
        return jnp.transpose(jnp.broadcast_to(values.astype(jnp.float32), shape))

    same = turned(owners) == jnp.broadcast_to(owners.astype(jnp.float32), shape)
    earlier = jnp.where(same & (down < across), 1.0, 0.0)
    occurs = jnp.sum(earlier, 0, keepdims=True).astype(jnp.int32)
    number = lax.broadcasted_iota(jnp.int32, entry.shape, 1)
    codes = number // SUPP * TB_DEV + (entry & (TB_DEV - 1)) + 1
    filled, codes = turned(owners * stride + occurs), turned(codes)
    places[0:1, :] = owners >> 1
    places[1:2, :] = ((owners & 1) * slots_each + occurs) * BLK
    bundle[SLOT_AT:TGT_AT, :] = jnp.zeros((TGT_AT - SLOT_AT, LANES), jnp.float32)
    for k in range(rows):
        here = filled == (across + k * LANES).astype(jnp.float32)
        bundle[SLOT_AT + k : SLOT_AT + k + 1, :] = jnp.sum(
            jnp.where(here, codes, 0.0), 0, keepdims=True
        )
    to_tiles(src_cent, src_own)
    src_own[F * src_mass.shape[0] :, :] = src_mass[...]
    to_tiles(src_pts, bundle)
    bundle[2 * LANES : SLOT_AT, :] = cluster[...].astype(jnp.float32)
    bundle[TGT_AT : TGT_AT + F, :] = tgt_a[...]
    bundle[TGT_AT + F : TGT_AT + 2 * F, :] = tgt_b[...]
    masses = jnp.concatenate([mass_a[...], mass_b[...], jnp.ones((6, LANES), jnp.float32)], 0)
    bundle[TGT_AT + 2 * F :, :] = masses


def prepare(wanted, src_pts, cluster, src_cent, src_mass, tgt, devices, slots_each, stride):
    return pl.pallas_call(
        functools.partial(prepare_kernel, devices * stride // LANES, slots_each, stride),
        out_shape=(
            jax.ShapeDtypeStruct((TGT_AT + 2 * F + 8, LANES), jnp.float32),
            jax.ShapeDtypeStruct(((F + 1) * src_mass.shape[0], LANES), jnp.float32),
            jax.ShapeDtypeStruct((2, LANES), jnp.int32),
        ),
        in_specs=[VMEM] * 9,
        out_specs=(VMEM, VMEM, VMEM),
        name="prepare",
    )(wanted, src_pts, cluster, src_cent, src_mass, *tgt)


def coarse_kernel(n_src, n_tgt, stored, *refs):
    given_src = refs[:n_src]
    given_tgt = refs[n_src : n_src + n_tgt]
    f_out, g_out, kernel, mass, dual, sums, all_src, all_tgt, arrived, *ahead = refs[n_src + n_tgt :]
    src = [all_src.at[n] for n in range(n_src)]
    tgt = [all_tgt.at[n] for n in range(n_tgt)]
    copies = [
        pltpu.make_async_copy(given.at[pl.ds(TGT_AT, 2 * F + 8)], held, arrived.at[n])
        for n, (given, held) in enumerate(zip(given_tgt, tgt))
    ]
    copies += [
        pltpu.make_async_copy(given, held, arrived.at[n_tgt + n])
        for n, (given, held) in enumerate(zip(given_src, src))
    ]
    for copy in copies:
        copy.start()
    for copy in copies:
        copy.wait()
    ks, kt = f_out.shape[1], g_out.shape[1]
    wide_src = src[0].shape[0] // (F + 1)
    piece = wide_src * LANES
    tiles = kt // LANES
    y = jnp.concatenate(
        [ref[F * e : F * e + F, :] for ref in tgt for e in range(2)], 1
    )
    at = 2 * F
    b = jnp.concatenate([ref[at + e : at + e + 1, :] for ref in tgt for e in range(2)], 1)
    right = pack_right(y, jnp.log2(b) - SCALE * square_norm(y))
    ones = jnp.ones((F, LANES), jnp.bfloat16)
    zero = jnp.zeros((8, kt), jnp.float32)
    high = jnp.full((8, LANES), jnp.inf, jnp.float32)

    def wide(values):
        return jnp.tile(values, (1, tiles))

    def over_sources(size, body, carry):
        for s in range(n_src):

            def chunk(k, carry, s=s):
                rows = pl.ds(pl.multiple_of(s * piece + k * size, size), size)
                x, values = source_columns(src[s], wide_src, k, size // LANES)
                left = pack_left(x, -SCALE * square_norm(x))
                return body(values, rows, left, carry)

            carry = lax.fori_loop(0, piece // size, chunk, carry)
        return carry

    def over_rows(size, body, carry):
        def chunk(k, carry):
            return body(pl.ds(pl.multiple_of(k * size, size), size), carry)

        return lax.fori_loop(0, ks // size, chunk, carry)

    def weigh(e, weighted, rows, carry):
        total, least = carry
        row_sum = jnp.broadcast_to(jnp.sum(weighted, 1, keepdims=True), (e.shape[0], LANES))
        sums[rows, :] = row_sum
        weight = mass[rows, :] / row_sum
        return total + fold(e * wide(weight), jnp.add), jnp.minimum(least, fold(row_sum, jnp.minimum))

    def close(total, least):
        total = jnp.sum(total, 0, keepdims=True)
        small = jnp.minimum(jnp.min(total), jnp.min(least)) < LOW
        return b / total, small.astype(jnp.int32)

    def spread_mass(values, rows):
        mass[rows, :] = contract(constant_rows(values, 0, None), ones)

    def begin_rows(z, rows, carry):
        top = jnp.max(z, 1, keepdims=True)
        dual[rows, :] = jnp.broadcast_to(-top, (z.shape[0], LANES))
        e = jnp.exp2(z - top)
        if stored:
            kernel[rows, :] = e
        return weigh(e, e, rows, carry)

    def begin(values, rows, left, carry):
        spread_mass(values, rows)
        return begin_rows(contract(left, right), rows, carry)

    if stored:
        def products(s, out):
            rows = slice(s * piece, (s + 1) * piece)
            x, values = source_columns(src[s], wide_src, 0, wide_src)
            out[...] = contract(pack_left(x, -SCALE * square_norm(x)), right)
            spread_mass(values, rows)

        products(0, ahead[0])
        carry = (zero, high)
        for s in range(n_src):
            if s + 1 < n_src:
                products(s + 1, ahead[(s + 1) % 2])
            carry = begin_rows(ahead[s % 2][...], slice(s * piece, (s + 1) * piece), carry)
    else:
        carry = over_sources(ROWS, begin, (zero, high))
    scale, small = close(*carry)
    base = jnp.zeros((1, kt), jnp.float32)

    def rescue(base, scale):
        def rebase(rows, carry):
            dual[rows, :] = dual[rows, :] - jnp.log2(sums[rows, :])
            return carry

        over_rows(ROWS, rebase, 0)

        def tops(_, rows, left, top):
            return jnp.maximum(top, fold(contract(left, right) + wide(dual[rows, :]), jnp.maximum))

        top = jnp.max(over_sources(ROWS, tops, zero - jnp.inf), 0, keepdims=True)

        def step(_, rows, left, total):
            e = jnp.exp2(contract(left, right) + wide(dual[rows, :]) - top)
            return total + fold(e * wide(mass[rows, :]), jnp.add)

        total = jnp.sum(over_sources(ROWS, step, zero), 0, keepdims=True)
        over_rows(ROWS, unit, 0)
        return jnp.log2(b) - (top + jnp.log2(total)), jnp.ones_like(scale)

    def unit(rows, carry):
        sums[rows, :] = jnp.ones((ROWS, LANES), jnp.float32)
        return carry

    base, scale = lax.cond(small > 0, rescue, lambda base, scale: (base, scale), base, scale)

    def renew(base, scale):
        base = base + jnp.log2(scale)

        def step(_, rows, left, carry):
            f = dual[rows, :] - jnp.log2(sums[rows, :])
            dual[rows, :] = f
            e = jnp.exp2(contract(left, right) + wide(f) + base)
            if stored:
                kernel[rows, :] = e
            return weigh(e, e, rows, carry)

        scale, small = close(*over_sources(ROWS, step, (zero, high)))
        return base, scale, small

    def reuse(base, scale):
        def step(rows, carry):
            e = kernel[rows, :]
            return weigh(e, e * scale, rows, carry)

        scale, small = close(*over_rows(ROWS_TURN, step, (zero, high)))
        return base, scale, small

    def turn(_, state):
        base, scale, small = state
        if not stored:
            return renew(base, scale)
        return lax.cond(small > 0, renew, reuse, base, scale)

    base, scale, small = lax.fori_loop(1, ITERS, turn, (base, scale, small))
    g_out[...] = (base + jnp.log2(scale)) * (1.0 / SCALE)
    diagonal = lax.broadcasted_iota(jnp.int32, (LANES, LANES), 0) == lax.broadcasted_iota(
        jnp.int32, (LANES, LANES), 1
    )

    def to_lanes(k, carry):
        span = pl.ds(pl.multiple_of(k * LANES, LANES), LANES)
        f = dual[span, :] - jnp.log2(sums[span, :])
        f_out[:, span] = jnp.sum(jnp.where(diagonal, f, 0.0), 0, keepdims=True) * (1.0 / SCALE)
        return carry

    lax.fori_loop(0, ks // LANES, to_lanes, 0)

def coarse_duals(src, tgt):
    ks = sum(part.shape[0] // (F + 1) * LANES for part in src)
    kt = sum(2 * part.shape[1] for part in tgt)
    stored = ks * kt * 4 <= 16 * MIB
    return pl.pallas_call(
        functools.partial(coarse_kernel, len(src), len(tgt), stored),
        out_shape=(
            jax.ShapeDtypeStruct((1, ks), jnp.float32),
            jax.ShapeDtypeStruct((1, kt), jnp.float32),
        ),
        in_specs=[VMEM] * (len(src) + len(tgt)),
        out_specs=(VMEM, VMEM),
        scratch_shapes=[
            pltpu.VMEM((ks, kt) if stored else (8, LANES), jnp.float32),
        ]
        + [pltpu.VMEM((ks, LANES), jnp.float32)] * 3
        + [
            pltpu.VMEM((len(src),) + src[0].shape, jnp.float32),
            pltpu.VMEM((len(tgt), 2 * F + 8, LANES), jnp.float32),
            pltpu.SemaphoreType.DMA((len(src) + len(tgt),)),
        ]
        + [pltpu.VMEM((ks // len(src), kt) if stored else (8, LANES), jnp.float32)] * 2,
        compiler_params=pltpu.CompilerParams(vmem_limit_bytes=36 * MIB),
        cost_estimate=pl.CostEstimate(
            flops=40 * ks * kt, bytes_accessed=4 * 24 * (ks + kt), transcendentals=9 * ks * kt
        ),
        name="coarse",
    )(*src, *tgt)


def look_up(table_ref, index):
    low = index & (LANES - 1)
    high = index >> 7
    out = jnp.zeros(index.shape, jnp.float32)
    for h in range(table_ref.shape[1] // LANES):
        row = jnp.broadcast_to(table_ref[0:1, h * LANES : (h + 1) * LANES], index.shape)
        out = jnp.where(high == h, jnp.take_along_axis(row, low, axis=1), out)
    return out


def fine_kernel(n_stacks, slots_each, stride, where_ref, *refs):
    stacks = refs[:n_stacks]
    points_a, points_b, cluster_a, cluster_b, f_table, g_table = refs[n_stacks : n_stacks + 6]
    partial_out, kept = refs[n_stacks + 6 : n_stacks + 8]
    bundle, slot_rows, start_g, packed, col_sum, col_top, codes, arrived, slots, count = refs[
        n_stacks + 8 : n_stacks + 18
    ]
    order_t, order_block, order_from, order_span = refs[n_stacks + 18 :]
    senders = bundle.shape[0]
    depth = senders // n_stacks
    blocks = 2 * TB_DEV
    sums_out = kept
    start_g_at = 3 * blocks
    start_f_at = start_g_at + 2 * TB_DEV
    me, core, src_flip, tgt_flip = (where_ref[k] for k in range(4))

    def copy_of(n, first, rows, to, sem):
        source = stacks[n].at[:, pl.ds(first, rows), :]
        return pltpu.make_async_copy(source, to.at[pl.ds(n * depth, depth)], arrived.at[sem])

    early = [copy_of(n, SLOT_AT, 8, slot_rows, n) for n in range(n_stacks)]
    late = [copy_of(n, 0, SLOT_AT, bundle, n_stacks + n) for n in range(n_stacks)]
    for copy in early + late:
        copy.start()

    for side, cluster in enumerate((cluster_a, cluster_b)):
        for k in range(2 * TB_DEV // 8):
            index = cluster[8 * k : 8 * k + 8, :] ^ tgt_flip
            at = 2 * TB_DEV * side + 8 * k
            start_g[at : at + 8, :] = look_up(g_table, index)
    kept[start_g_at:start_f_at, :] = start_g[0 : 2 * TB_DEV, :]
    for t in range(blocks + 1):
        count[t] = 0
    for copy in early:
        copy.wait()

    at = me * 2 * stride

    def slot_row(n, carry):
        codes[pl.ds(n, 1), :] = slot_rows[n, pl.ds(at // LANES, 1), :].astype(jnp.int32)
        return carry

    lax.fori_loop(0, senders, slot_row, 0, unroll=BLOCKS)
    codes[...] = pltpu.roll(codes[...], (LANES - at % LANES) % LANES, 1)
    to_scalars = pltpu.make_async_copy(codes, slots, arrived.at[2 * n_stacks])
    to_scalars.start()

    for side, points in enumerate((points_a, points_b)):

        def pack_target(t, carry, side=side, points=points):
            y = points[:, pl.ds(pl.multiple_of(t * BLK, BLK), BLK)]
            row = 2 * (side * TB_DEV + t)
            g = jnp.concatenate([start_g[pl.ds(row, 1), :], start_g[pl.ds(row + 1, 1), :]], 1)
            rows = pack_right(y, SCALE * (g - square_norm(y)))
            rows = jnp.concatenate([rows, jnp.zeros((LANES - KDIM, BLK), jnp.bfloat16)], 0)
            packed[side * TB_DEV + t] = jnp.transpose(rows.astype(jnp.float32)).astype(jnp.bfloat16)
            col_sum[side * TB_DEV + t] = jnp.zeros((BLK, LANES), jnp.float32)
            return carry

        lax.fori_loop(0, TB_DEV, pack_target, 0, unroll=BLOCKS)
    packed[blocks] = jnp.zeros((BLK, LANES), jnp.bfloat16)
    col_sum[blocks] = jnp.zeros((BLK, LANES), jnp.float32)
    to_scalars.wait()

    each = 2 * slots_each
    total = senders * each
    unroll = math.gcd(PAIRS, total)

    def place(d, carry):
        used, unused = carry
        for rest in range(each):
            owner, s = divmod(rest, slots_each)
            code = slots[d, owner * stride + s]
            valid = code > 0
            t = jnp.where(valid, (code - 1) % TB_DEV + TB_DEV * (owner ^ core), blocks)
            n = jnp.where(valid, used, unused)
            order_t[n] = t
            order_block[n] = jnp.where(valid, (code - 1) // TB_DEV, 0)
            order_from[n] = d
            order_span[n] = rest * BLK
            count[t] = count[t] + 1
            step = valid.astype(jnp.int32)
            used, unused = used + step, unused - (1 - step)
        return used, unused

    used, _ = lax.fori_loop(0, senders, place, (jnp.int32(0), jnp.int32(total - 1)))
    for copy in late:
        copy.wait()
    index = bundle[0, 2 * LANES : SLOT_AT, :].astype(jnp.int32) ^ src_flip
    for half in range(2):
        rows = slice(8 * half, 8 * half + 8)
        at = start_f_at + 8 * half
        kept[at : at + 8, :] = look_up(f_table, index[rows])

    def cluster_rows(n):
        at = 2 * LANES + 2 * order_block[n]
        return [bundle[order_from[n], pl.ds(at + k, 1), :] for k in range(2)]

    def starts(ps):
        out = []
        for n in range(0, len(ps), 4):
            rows = jnp.concatenate([r for p in ps[n:n+4] for r in cluster_rows(p)], 0)
            f = look_up(f_table, rows.astype(jnp.int32) ^ src_flip)
            for m in range(len(ps[n:n+4])):
                out.append(jnp.concatenate([f[2*m:2*m+1], f[2*m+1:2*m+2]], 1))
        return out

    def product(p, f):
        t, block, d = order_t[p], order_block[p], order_from[p]
        tile = [[bundle[d, pl.ds(pl.multiple_of(half * LANES + 16 * block + 8 * k, 8), 8), :] for k in range(2)] for half in range(2)]
        x = jnp.concatenate([jnp.concatenate(row, 1) for row in tile], 0)
        left = pack_left(x, SCALE * (f - square_norm(x)))
        left = jnp.concatenate([left, jnp.zeros((LANES - KDIM, BLK), jnp.bfloat16)], 0)
        z = jnp.dot(packed[t], left, preferred_element_type=jnp.float32)
        return t, d, SCALE * f, z

    def put(p, d, value):
        span = pl.ds(pl.multiple_of(order_span[p], BLK), BLK)
        partial_out[me ^ d, :, span] = value

    def pair(p, f, least, most):
        t, d, f, z = product(p, f)
        e = jnp.exp2(z)
        row = fold(e, jnp.add)
        col_sum[t] = col_sum[t] + (e[:, :LANES] + e[:, LANES:])
        row = jnp.sum(row, 0, keepdims=True)
        put(p, d, jnp.log2(row) - f)
        return jnp.minimum(least, row), jnp.maximum(most, row)

    def pairs(n, carry):
        ps = [unroll * n + u for u in range(unroll)]
        fs = starts(ps)
        for u in range(unroll):
            carry = pair(ps[u], fs[u], *carry)
        return carry

    def lanes(t, carry):
        least, most = carry
        halves = []
        for k in range(2):
            block = jnp.transpose(col_sum[t, k * LANES : (k + 1) * LANES, :])
            halves.append(jnp.sum(block, 0, keepdims=True))
        s = jnp.concatenate(halves, 0)
        sums_out[pl.ds(pl.multiple_of(2 * t, 2), 2), :] = jnp.log2(s)
        sums_out[pl.ds(2 * blocks + t, 1), :] = jnp.full((1, LANES), count[t].astype(jnp.float32))
        return jnp.minimum(least, jnp.where(count[t] > 0, s, LARGE)), jnp.maximum(most, s)

    least = jnp.full((1, BLK), LARGE, jnp.float32)
    most = jnp.zeros((1, BLK), jnp.float32)
    least, most = lax.fori_loop(0, (used + unroll - 1) // unroll, pairs, (least, most))
    low = jnp.full((2, LANES), LARGE, jnp.float32)
    high = jnp.zeros((2, LANES), jnp.float32)
    low, high = lax.fori_loop(0, blocks, lanes, (low, high), unroll=BLOCKS)
    smallest = jnp.minimum(jnp.min(least), jnp.min(low))
    largest = jnp.maximum(jnp.max(most), jnp.max(high))
    fits = (smallest >= SMALL) & (largest <= LARGE)

    @pl.when(jnp.logical_not(fits))
    def _():
        def fill(t, carry):
            col_sum[t] = jnp.zeros((BLK, LANES), jnp.float32)
            col_top[t] = jnp.full((BLK, LANES), -1e30, jnp.float32)
            return carry

        lax.fori_loop(0, blocks + 1, fill, 0)

        def pair(n, carry):
            p = n
            t, d, f, z = product(p, starts([p])[0])
            top = jnp.max(z, 0, keepdims=True)
            put(p, d, top + jnp.log2(jnp.sum(jnp.exp2(z - top), 0, keepdims=True)) - f)
            a, b = z[:, :LANES], z[:, LANES:]
            old = col_top[t]
            new = jnp.maximum(old, jnp.maximum(a, b))
            col_sum[t] = col_sum[t] * jnp.exp2(old - new) + (jnp.exp2(a - new) + jnp.exp2(b - new))
            col_top[t] = new
            return carry

        lax.fori_loop(0, used, pair, 0)

        def lanes(t, carry):
            for k in range(2):
                rows = slice(k * LANES, (k + 1) * LANES)
                top = jnp.transpose(col_top[t, rows, :])
                most = jnp.max(top, 0, keepdims=True)
                s = jnp.sum(jnp.transpose(col_sum[t, rows, :]) * jnp.exp2(top - most), 0, keepdims=True)
                sums_out[pl.ds(2 * t + k, 1), :] = most + jnp.log2(s)
            return carry

        lax.fori_loop(0, blocks, lanes, 0)


def fine_update(where, stacks, points, clusters, f_table, g_table, slots_each, stride):
    senders = sum(stack.shape[0] for stack in stacks)
    blocks = 2 * TB_DEV
    return pl.pallas_call(
        functools.partial(fine_kernel, len(stacks), slots_each, stride),
        out_shape=(
            jax.ShapeDtypeStruct((senders, 1, 2 * slots_each * BLK), jnp.float32),
            jax.ShapeDtypeStruct((3 * blocks + 2 * TB_DEV + F, LANES), jnp.float32),
        ),
        in_specs=[SMEM] + [pl.BlockSpec(memory_space=pl.ANY)] * len(stacks) + [VMEM] * 6,
        out_specs=(VMEM, VMEM),
        scratch_shapes=[
            pltpu.VMEM((senders, SLOT_AT, LANES), jnp.float32),
            pltpu.VMEM((senders, 8, LANES), jnp.float32),
            pltpu.VMEM((2 * blocks, LANES), jnp.float32),
            pltpu.VMEM((blocks + 1, BLK, LANES), jnp.bfloat16),
            pltpu.VMEM((blocks + 1, BLK, LANES), jnp.float32),
            pltpu.VMEM((blocks + 1, BLK, LANES), jnp.float32),
            pltpu.VMEM((senders, LANES), jnp.int32),
            pltpu.SemaphoreType.DMA((2 * len(stacks) + 1,)),
            pltpu.SMEM((senders, LANES), jnp.int32),
            pltpu.SMEM((blocks + 1,), jnp.int32),
        ]
        + [pltpu.SMEM((senders * 2 * slots_each,), jnp.int32)] * 4,
        compiler_params=pltpu.CompilerParams(vmem_limit_bytes=(28 + senders // 8) * MIB),
        name="fine",
    )(where, *stacks, *points, *clusters, f_table, g_table)


def finish_kernel(place_ref, own, other, partial, fine_f_out, fine_g_out, gathered):
    rows = 2 * TB_DEV
    a, b = own[0:rows, :], other[rows : 2 * rows, :]
    top = jnp.maximum(a, b)
    lse = top + jnp.log2(jnp.exp2(a - top) + jnp.exp2(b - top))
    counts = 2 * rows
    g = own[3 * rows : 4 * rows, :]
    named = own[counts : counts + TB_DEV, :] + other[counts + TB_DEV : counts + 2 * TB_DEV, :]
    logs = EPS * jnp.log(named * float(BLK))
    base = g - (lse * (1.0 / SCALE) - g)
    for t in range(TB_DEV):
        span = slice(2 * t, 2 * t + 2)
        fine_g_out[span, :] = 0.5 * (base[span, :] + logs[t : t + 1, :])
    for block in range(SB_DEV):
        for k in range(SUPP):
            n = block * SUPP + k
            span = pl.ds(pl.multiple_of(place_ref[1, n], BLK), BLK)
            gathered[k, block : block + 1, :] = partial[place_ref[0, n], :, span]
    values = gathered[...]
    top = jnp.max(values, 0)
    lse = top + jnp.log2(jnp.sum(jnp.exp2(values - top[None]), 0))
    term = EPS * math.log(float(SUPP * BLK)) - lse * (1.0 / SCALE)
    for block in range(SB_DEV):
        for k in range(2):
            row = slice(2 * block + k, 2 * block + k + 1)
            piece = term[block : block + 1, k * LANES : (k + 1) * LANES]
            start_f = own[8 * TB_DEV + 2 * block + k : 8 * TB_DEV + 2 * block + k + 1, :]
            fine_f_out[row, :] = 0.5 * (start_f + piece)


def finish(places, own, other, partial):
    return pl.pallas_call(
        finish_kernel,
        out_shape=(
            jax.ShapeDtypeStruct((F, LANES), jnp.float32),
            jax.ShapeDtypeStruct((2 * TB_DEV, LANES), jnp.float32),
        ),
        in_specs=[SMEM] + [VMEM] * 3,
        out_specs=(VMEM, VMEM),
        scratch_shapes=[pltpu.VMEM((SUPP, SB_DEV, BLK), jnp.float32)],
        name="finish",
    )(places, own, other, partial)


def exchange(x, axis, flip):
    count = lax.axis_size(axis)
    return lax.ppermute(x, axis, [(i, i ^ flip) for i in range(count)])


def on_device(
    src_cent, tgt_cent, src_mass, tgt_mass, src_pts, tgt_pts, src_cluster, tgt_cluster, support
):
    n_row, n_chip, n_core = (lax.axis_size(axis) for axis in AXES)
    devices = n_row * n_chip * n_core
    row, chip, core = (lax.axis_index(axis) for axis in AXES)

    flat_mass = tgt_mass.reshape(-1, LANES)
    tgt = [tgt_cent, flat_mass, exchange(tgt_cent, "core", 1), exchange(flat_mass, "core", 1)]

    tgt_cluster = tgt_cluster.reshape(2 * TB_DEV, LANES)
    requests_each = SB_DEV * SUPP
    slots_each = requests_each // devices + 1
    stride = 1 << (slots_each - 1).bit_length()
    bundle, src_own, places = prepare(
        support.reshape(1, requests_each),
        src_pts,
        src_cluster.reshape(F, LANES),
        src_cent,
        src_mass.reshape(-1, LANES),
        tgt,
        devices,
        slots_each,
        stride,
    )
    along = [bundle] + [exchange(bundle, "chip", k) for k in range(1, n_chip)]
    src_all = [src_own] + [exchange(src_own, "row", k) for k in range(1, 3)]
    src_own, src_all[1] = lax.optimization_barrier((src_own, src_all[1]))
    src_all += [exchange(src_own, "row", k) for k in range(3, n_row)]
    stack = jnp.stack([part[:TGT_AT] for part in along])
    src_all, along, stack = lax.optimization_barrier((src_all, along, stack))
    stacks = [stack] + [exchange(stack, "row", k) for k in range(1, n_row)]
    f_table, g_table = coarse_duals(src_all, along)
    tgt_pts, tgt_cluster, f_table, g_table = lax.optimization_barrier(
        (tgt_pts, tgt_cluster, f_table, g_table)
    )
    points = [tgt_pts, exchange(tgt_pts, "core", 1)]
    clusters = [tgt_cluster, exchange(tgt_cluster, "core", 1)]
    coarse_f = f_table[0, : src_cent.shape[1]]
    coarse_g = g_table[0, : tgt_cent.shape[1]]

    col = chip * n_core + core
    where = [row * n_chip + chip, core, row * src_cent.shape[1], col * tgt_cent.shape[1]]
    partial, kept = fine_update(
        jnp.stack(where).astype(jnp.int32),
        stacks,
        points,
        clusters,
        f_table,
        g_table,
        slots_each,
        stride,
    )
    returned = lax.all_to_all(partial, CHIPS, split_axis=0, concat_axis=0, tiled=True)
    other = exchange(kept, "core", 1)
    fine_f, fine_g = finish(places, kept, other, returned)
    return coarse_f, coarse_g, fine_f.reshape(-1), fine_g.reshape(-1)


def solution(mesh):
    n_row, n_col = mesh.devices.shape
    cores = jax.sharding.Mesh(mesh.devices.reshape(n_row, n_col // 2, 2), AXES)
    col = CHIPS[1:] + AXES[2:]
    in_specs = (
        P(None, "row"),
        P(None, col),
        P("row"),
        P(col),
        P(None, AXES),
        P(None, AXES),
        P(AXES),
        P(AXES),
        P(AXES, None),
    )
    out_specs = (P("row"), P(col), P(AXES), P(AXES))
    return jax.shard_map(
        on_device, mesh=cores, in_specs=in_specs, out_specs=out_specs, check_vma=False
    )
```

```python
import functools
import math

import jax
import jax.numpy as jnp
from jax import lax
from jax.experimental import pallas as pl
from jax.experimental.pallas import tpu as pltpu
from jax.sharding import PartitionSpec as P

F = 16
BLK = 256
SUPP = 16
ITERS = 8
SB_DEV = 8
TB_DEV = 32
EPS = 0.1

SCALE = math.log2(math.e) / EPS
KDIM = 7 * F
LANES = 128
ROWS = 256
ROWS_PRODUCT = 1024
ROWS_BEGIN = 1024
ROWS_TURN = 1024
PAIRS = 32
BLOCKS = 16
LOW = 2.0**-30
SMALL = 2.0**-80
LARGE = 2.0**100
MIB = 1024 * 1024
SLOT_AT = 2 * LANES + F
TGT_AT = SLOT_AT + 8
AXES = ("row", "chip", "core")
CHIPS = ("row", "chip")

VMEM = pl.BlockSpec(memory_space=pltpu.VMEM)
SMEM = pl.BlockSpec(memory_space=pltpu.SMEM)
CONTRACT_FIRST = (((0,), (0,)), ((), ()))


def split3(x):
    first = x.astype(jnp.bfloat16)
    rest = x - first.astype(jnp.float32)
    second = rest.astype(jnp.bfloat16)
    rest = rest - second.astype(jnp.float32)
    return first, second, rest.astype(jnp.bfloat16)


def constant_rows(values, at, ones_at):
    width = values.shape[1]
    parts = split3(jnp.broadcast_to(values, (F, width)))
    row = lax.broadcasted_iota(jnp.int32, (F, width), 0)
    rows = jnp.zeros((F, width), jnp.float32)
    for k, part in enumerate(parts):
        rows = jnp.where(row == at + k, part.astype(jnp.float32), rows)
    if ones_at is not None:
        rows = jnp.where((row >= ones_at) & (row < ones_at + 3), 1.0, rows)
    return rows.astype(jnp.bfloat16)


def pack_left(x, constant):
    a, b, c = split3(x * (2.0 * SCALE))
    return jnp.concatenate([a, a, b, b, a, c, constant_rows(constant, 0, 3)], 0)


def pack_right(y, constant):
    a, b, c = split3(y)
    return jnp.concatenate([a, b, a, b, c, a, constant_rows(constant, 3, 0)], 0)


def contract(left, right):
    return lax.dot_general(left, right, CONTRACT_FIRST, preferred_element_type=jnp.float32)


def square_norm(x):
    return jnp.sum(x * x, 0, keepdims=True)


def fold(values, combine):
    out = values[0:8]
    for k in range(1, values.shape[0] // 8):
        out = combine(out, values[8 * k : 8 * k + 8])
    return out


def source_columns(ref, count, k, n):
    halves = [
        jnp.concatenate(
            [
                ref[pl.ds(pl.multiple_of(8 * (half * count + k * n + i), 8), 8), :]
                for i in range(n)
            ],
            1,
        )
        for half in range(2)
    ]
    values = [ref[pl.ds(F * count + k * n + i, 1), :] for i in range(n)]
    return jnp.concatenate(halves, 0), jnp.concatenate(values, 1)


def to_tiles(ref, out):
    count = ref.shape[1] // LANES
    for half in range(2):
        for i in range(count):
            at = 8 * (half * count + i)
            out[at : at + 8, :] = ref[8 * half : 8 * half + 8, i * LANES : (i + 1) * LANES]


def prepare_kernel(
    rows, slots_each, stride, wanted, src_pts, cluster, src_cent, src_mass, tgt_a, mass_a, tgt_b, mass_b,
    bundle, src_own, places,
):
    shape = (LANES, LANES)
    down = lax.broadcasted_iota(jnp.int32, shape, 0)
    across = lax.broadcasted_iota(jnp.int32, shape, 1)
    block_bits = TB_DEV.bit_length() - 1
    entry = wanted[...]
    owners = entry >> block_bits

    def turned(values):
        return jnp.transpose(jnp.broadcast_to(values.astype(jnp.float32), shape))

    same = turned(owners) == jnp.broadcast_to(owners.astype(jnp.float32), shape)
    earlier = jnp.where(same & (down < across), 1.0, 0.0)
    occurs = jnp.sum(earlier, 0, keepdims=True).astype(jnp.int32)
    number = lax.broadcasted_iota(jnp.int32, entry.shape, 1)
    codes = number // SUPP * TB_DEV + (entry & (TB_DEV - 1)) + 1
    filled, codes = turned(owners * stride + occurs), turned(codes)
    places[0:1, :] = owners >> 1
    places[1:2, :] = ((owners & 1) * slots_each + occurs) * BLK
    bundle[SLOT_AT:TGT_AT, :] = jnp.zeros((TGT_AT - SLOT_AT, LANES), jnp.float32)
    for k in range(rows):
        here = filled == (across + k * LANES).astype(jnp.float32)
        bundle[SLOT_AT + k : SLOT_AT + k + 1, :] = jnp.sum(
            jnp.where(here, codes, 0.0), 0, keepdims=True
        )
    to_tiles(src_cent, src_own)
    src_own[F * src_mass.shape[0] :, :] = src_mass[...]
    to_tiles(src_pts, bundle)
    bundle[2 * LANES : SLOT_AT, :] = cluster[...].astype(jnp.float32)
    bundle[TGT_AT : TGT_AT + F, :] = tgt_a[...]
    bundle[TGT_AT + F : TGT_AT + 2 * F, :] = tgt_b[...]
    masses = jnp.concatenate([mass_a[...], mass_b[...], jnp.ones((6, LANES), jnp.float32)], 0)
    bundle[TGT_AT + 2 * F :, :] = masses


def prepare(wanted, src_pts, cluster, src_cent, src_mass, tgt, devices, slots_each, stride):
    return pl.pallas_call(
        functools.partial(prepare_kernel, devices * stride // LANES, slots_each, stride),
        out_shape=(
            jax.ShapeDtypeStruct((TGT_AT + 2 * F + 8, LANES), jnp.float32),
            jax.ShapeDtypeStruct(((F + 1) * src_mass.shape[0], LANES), jnp.float32),
            jax.ShapeDtypeStruct((2, LANES), jnp.int32),
        ),
        in_specs=[VMEM] * 9,
        out_specs=(VMEM, VMEM, VMEM),
        name="prepare",
    )(wanted, src_pts, cluster, src_cent, src_mass, *tgt)


def coarse_kernel(n_src, n_tgt, stored, *refs):
    given_src = refs[:n_src]
    given_tgt = refs[n_src : n_src + n_tgt]
    f_out, g_out, kernel, mass, dual, sums, all_src, all_tgt, arrived, *ahead = refs[n_src + n_tgt :]
    src = [all_src.at[n] for n in range(n_src)]
    tgt = [all_tgt.at[n] for n in range(n_tgt)]
    copies = [
        pltpu.make_async_copy(given.at[pl.ds(TGT_AT, 2 * F + 8)], held, arrived.at[n])
        for n, (given, held) in enumerate(zip(given_tgt, tgt))
    ]
    copies += [
        pltpu.make_async_copy(given, held, arrived.at[n_tgt + n])
        for n, (given, held) in enumerate(zip(given_src, src))
    ]
    for copy in copies:
        copy.start()
    for copy in copies:
        copy.wait()
    ks, kt = f_out.shape[1], g_out.shape[1]
    wide_src = src[0].shape[0] // (F + 1)
    piece = wide_src * LANES
    tiles = kt // LANES
    y = jnp.concatenate(
        [ref[F * e : F * e + F, :] for ref in tgt for e in range(2)], 1
    )
    at = 2 * F
    b = jnp.concatenate([ref[at + e : at + e + 1, :] for ref in tgt for e in range(2)], 1)
    right = pack_right(y, jnp.log2(b) - SCALE * square_norm(y))
    ones = jnp.ones((F, LANES), jnp.bfloat16)
    zero = jnp.zeros((8, kt), jnp.float32)
    high = jnp.full((8, LANES), jnp.inf, jnp.float32)

    def wide(values):
        return jnp.tile(values, (1, tiles))

    def over_sources(size, body, carry):
        for s in range(n_src):

            def chunk(k, carry, s=s):
                rows = pl.ds(pl.multiple_of(s * piece + k * size, size), size)
                x, values = source_columns(src[s], wide_src, k, size // LANES)
                left = pack_left(x, -SCALE * square_norm(x))
                return body(values, rows, left, carry)

            carry = lax.fori_loop(0, piece // size, chunk, carry)
        return carry

    def over_rows(size, body, carry):
        def chunk(k, carry):
            return body(pl.ds(pl.multiple_of(k * size, size), size), carry)

        return lax.fori_loop(0, ks // size, chunk, carry)

    def weigh(e, weighted, rows, carry):
        total, least = carry
        row_sum = jnp.broadcast_to(jnp.sum(weighted, 1, keepdims=True), (e.shape[0], LANES))
        sums[rows, :] = row_sum
        weight = mass[rows, :] / row_sum
        return total + fold(e * wide(weight), jnp.add), jnp.minimum(least, fold(row_sum, jnp.minimum))

    def close(total, least):
        total = jnp.sum(total, 0, keepdims=True)
        small = jnp.minimum(jnp.min(total), jnp.min(least)) < LOW
        return b / total, small.astype(jnp.int32)

    def spread_mass(values, rows):
        mass[rows, :] = contract(constant_rows(values, 0, None), ones)

    def begin_rows(z, rows, carry):
        top = jnp.max(z, 1, keepdims=True)
        dual[rows, :] = jnp.broadcast_to(-top, (z.shape[0], LANES))
        e = jnp.exp2(z - top)
        if stored:
            kernel[rows, :] = e
        return weigh(e, e, rows, carry)

    def begin(values, rows, left, carry):
        spread_mass(values, rows)
        return begin_rows(contract(left, right), rows, carry)

    if stored:
        def products(s, out):
            rows = slice(s * piece, (s + 1) * piece)
            x, values = source_columns(src[s], wide_src, 0, wide_src)
            out[...] = contract(pack_left(x, -SCALE * square_norm(x)), right)
            spread_mass(values, rows)

        products(0, ahead[0])
        carry = (zero, high)
        for s in range(n_src):
            if s + 1 < n_src:
                products(s + 1, ahead[(s + 1) % 2])
            carry = begin_rows(ahead[s % 2][...], slice(s * piece, (s + 1) * piece), carry)
    else:
        carry = over_sources(ROWS, begin, (zero, high))
    scale, small = close(*carry)
    base = jnp.zeros((1, kt), jnp.float32)

    def rescue(base, scale):
        def rebase(rows, carry):
            dual[rows, :] = dual[rows, :] - jnp.log2(sums[rows, :])
            return carry

        over_rows(ROWS, rebase, 0)

        def tops(_, rows, left, top):
            return jnp.maximum(top, fold(contract(left, right) + wide(dual[rows, :]), jnp.maximum))

        top = jnp.max(over_sources(ROWS, tops, zero - jnp.inf), 0, keepdims=True)

        def step(_, rows, left, total):
            e = jnp.exp2(contract(left, right) + wide(dual[rows, :]) - top)
            return total + fold(e * wide(mass[rows, :]), jnp.add)

        total = jnp.sum(over_sources(ROWS, step, zero), 0, keepdims=True)
        over_rows(ROWS, unit, 0)
        return jnp.log2(b) - (top + jnp.log2(total)), jnp.ones_like(scale)

    def unit(rows, carry):
        sums[rows, :] = jnp.ones((ROWS, LANES), jnp.float32)
        return carry

    base, scale = lax.cond(small > 0, rescue, lambda base, scale: (base, scale), base, scale)

    def renew(base, scale):
        base = base + jnp.log2(scale)

        def step(_, rows, left, carry):
            f = dual[rows, :] - jnp.log2(sums[rows, :])
            dual[rows, :] = f
            e = jnp.exp2(contract(left, right) + wide(f) + base)
            if stored:
                kernel[rows, :] = e
            return weigh(e, e, rows, carry)

        scale, small = close(*over_sources(ROWS, step, (zero, high)))
        return base, scale, small

    def reuse(base, scale):
        def step(rows, carry):
            e = kernel[rows, :]
            return weigh(e, e * scale, rows, carry)

        scale, small = close(*over_rows(ROWS_TURN, step, (zero, high)))
        return base, scale, small

    def turn(_, state):
        base, scale, small = state
        if not stored:
            return renew(base, scale)
        return lax.cond(small > 0, renew, reuse, base, scale)

    base, scale, small = lax.fori_loop(1, ITERS, turn, (base, scale, small))
    g_out[...] = (base + jnp.log2(scale)) * (1.0 / SCALE)
    diagonal = lax.broadcasted_iota(jnp.int32, (LANES, LANES), 0) == lax.broadcasted_iota(
        jnp.int32, (LANES, LANES), 1
    )

    def to_lanes(k, carry):
        span = pl.ds(pl.multiple_of(k * LANES, LANES), LANES)
        f = dual[span, :] - jnp.log2(sums[span, :])
        f_out[:, span] = jnp.sum(jnp.where(diagonal, f, 0.0), 0, keepdims=True) * (1.0 / SCALE)
        return carry

    lax.fori_loop(0, ks // LANES, to_lanes, 0, unroll=8)

def coarse_duals(src, tgt):
    ks = sum(part.shape[0] // (F + 1) * LANES for part in src)
    kt = sum(2 * part.shape[1] for part in tgt)
    stored = ks * kt * 4 <= 16 * MIB
    return pl.pallas_call(
        functools.partial(coarse_kernel, len(src), len(tgt), stored),
        out_shape=(
            jax.ShapeDtypeStruct((1, ks), jnp.float32),
            jax.ShapeDtypeStruct((1, kt), jnp.float32),
        ),
        in_specs=[VMEM] * (len(src) + len(tgt)),
        out_specs=(VMEM, VMEM),
        scratch_shapes=[
            pltpu.VMEM((ks, kt) if stored else (8, LANES), jnp.float32),
        ]
        + [pltpu.VMEM((ks, LANES), jnp.float32)] * 3
        + [
            pltpu.VMEM((len(src),) + src[0].shape, jnp.float32),
            pltpu.VMEM((len(tgt), 2 * F + 8, LANES), jnp.float32),
            pltpu.SemaphoreType.DMA((len(src) + len(tgt),)),
        ]
        + [pltpu.VMEM((ks // len(src), kt) if stored else (8, LANES), jnp.float32)] * 2,
        compiler_params=pltpu.CompilerParams(vmem_limit_bytes=36 * MIB),
        cost_estimate=pl.CostEstimate(
            flops=40 * ks * kt, bytes_accessed=4 * 24 * (ks + kt), transcendentals=9 * ks * kt
        ),
        name="coarse",
    )(*src, *tgt)


def look_up(table_ref, index):
    low = index & (LANES - 1)
    high = index >> 7
    out = jnp.zeros(index.shape, jnp.float32)
    for h in range(table_ref.shape[1] // LANES):
        row = jnp.broadcast_to(table_ref[0:1, h * LANES : (h + 1) * LANES], index.shape)
        out = jnp.where(high == h, jnp.take_along_axis(row, low, axis=1), out)
    return out


def fine_kernel(n_stacks, slots_each, stride, where_ref, *refs):
    stacks = refs[:n_stacks]
    points_a, points_b, cluster_a, cluster_b, f_table, g_table = refs[n_stacks : n_stacks + 6]
    partial_out, kept = refs[n_stacks + 6 : n_stacks + 8]
    bundle, slot_rows, start_g, packed, col_sum, col_top, codes, arrived, slots, count = refs[
        n_stacks + 8 : n_stacks + 18
    ]
    order_t, order_block, order_from, order_span = refs[n_stacks + 18 :]
    senders = bundle.shape[0]
    depth = senders // n_stacks
    blocks = 2 * TB_DEV
    sums_out = kept
    start_g_at = 3 * blocks
    start_f_at = start_g_at + 2 * TB_DEV
    me, core, src_flip, tgt_flip = (where_ref[k] for k in range(4))

    def copy_of(n, first, rows, to, sem):
        source = stacks[n].at[:, pl.ds(first, rows), :]
        return pltpu.make_async_copy(source, to.at[pl.ds(n * depth, depth)], arrived.at[sem])

    early = [copy_of(n, SLOT_AT, 8, slot_rows, n) for n in range(n_stacks)]
    late = [copy_of(n, 0, SLOT_AT, bundle, n_stacks + n) for n in range(n_stacks)]
    for copy in early + late:
        copy.start()

    for side, cluster in enumerate((cluster_a, cluster_b)):
        for k in range(2 * TB_DEV // 8):
            index = cluster[8 * k : 8 * k + 8, :] ^ tgt_flip
            at = 2 * TB_DEV * side + 8 * k
            start_g[at : at + 8, :] = look_up(g_table, index)
    kept[start_g_at:start_f_at, :] = start_g[0 : 2 * TB_DEV, :]
    for t in range(blocks + 1):
        count[t] = 0
    for copy in early:
        copy.wait()

    at = me * 2 * stride

    def slot_row(n, carry):
        codes[pl.ds(n, 1), :] = slot_rows[n, pl.ds(at // LANES, 1), :].astype(jnp.int32)
        return carry

    lax.fori_loop(0, senders, slot_row, 0, unroll=BLOCKS)
    codes[...] = pltpu.roll(codes[...], (LANES - at % LANES) % LANES, 1)
    to_scalars = pltpu.make_async_copy(codes, slots, arrived.at[2 * n_stacks])
    to_scalars.start()

    for side, points in enumerate((points_a, points_b)):

        def pack_target(t, carry, side=side, points=points):
            y = points[:, pl.ds(pl.multiple_of(t * BLK, BLK), BLK)]
            row = 2 * (side * TB_DEV + t)
            g = jnp.concatenate([start_g[pl.ds(row, 1), :], start_g[pl.ds(row + 1, 1), :]], 1)
            rows = pack_right(y, SCALE * (g - square_norm(y)))
            rows = jnp.concatenate([rows, jnp.zeros((LANES - KDIM, BLK), jnp.bfloat16)], 0)
            packed[side * TB_DEV + t] = jnp.transpose(rows.astype(jnp.float32)).astype(jnp.bfloat16)
            col_sum[side * TB_DEV + t] = jnp.zeros((BLK, LANES), jnp.float32)
            return carry

        lax.fori_loop(0, TB_DEV, pack_target, 0, unroll=BLOCKS)
    packed[blocks] = jnp.zeros((BLK, LANES), jnp.bfloat16)
    col_sum[blocks] = jnp.zeros((BLK, LANES), jnp.float32)
    to_scalars.wait()

    each = 2 * slots_each
    total = senders * each
    unroll = math.gcd(PAIRS, total)

    def place(d, carry):
        used, unused = carry
        for rest in range(each):
            owner, s = divmod(rest, slots_each)
            code = slots[d, owner * stride + s]
            valid = code > 0
            t = jnp.where(valid, (code - 1) % TB_DEV + TB_DEV * (owner ^ core), blocks)
            n = jnp.where(valid, used, unused)
            order_t[n] = t
            order_block[n] = jnp.where(valid, (code - 1) // TB_DEV, 0)
            order_from[n] = d
            order_span[n] = rest * BLK
            count[t] = count[t] + 1
            step = valid.astype(jnp.int32)
            used, unused = used + step, unused - (1 - step)
        return used, unused

    used, _ = lax.fori_loop(0, senders, place, (jnp.int32(0), jnp.int32(total - 1)), unroll=4)
    for copy in late:
        copy.wait()
    index = bundle[0, 2 * LANES : SLOT_AT, :].astype(jnp.int32) ^ src_flip
    for half in range(2):
        rows = slice(8 * half, 8 * half + 8)
        at = start_f_at + 8 * half
        kept[at : at + 8, :] = look_up(f_table, index[rows])

    def cluster_rows(n):
        at = 2 * LANES + 2 * order_block[n]
        return [bundle[order_from[n], pl.ds(at + k, 1), :] for k in range(2)]

    def starts(ps):
        out = []
        for n in range(0, len(ps), 4):
            rows = jnp.concatenate([r for p in ps[n:n+4] for r in cluster_rows(p)], 0)
            f = look_up(f_table, rows.astype(jnp.int32) ^ src_flip)
            for m in range(len(ps[n:n+4])):
                out.append(jnp.concatenate([f[2*m:2*m+1], f[2*m+1:2*m+2]], 1))
        return out

    def product(p, f):
        t, block, d = order_t[p], order_block[p], order_from[p]
        tile = [[bundle[d, pl.ds(pl.multiple_of(half * LANES + 16 * block + 8 * k, 8), 8), :] for k in range(2)] for half in range(2)]
        x = jnp.concatenate([jnp.concatenate(row, 1) for row in tile], 0)
        left = pack_left(x, SCALE * (f - square_norm(x)))
        left = jnp.concatenate([left, jnp.zeros((LANES - KDIM, BLK), jnp.bfloat16)], 0)
        z = jnp.dot(packed[t], left, preferred_element_type=jnp.float32)
        return t, d, SCALE * f, z

    def put(p, d, value):
        span = pl.ds(pl.multiple_of(order_span[p], BLK), BLK)
        partial_out[me ^ d, :, span] = value

    def pair(p, f, least, most):
        t, d, f, z = product(p, f)
        e = jnp.exp2(z)
        row = fold(e, jnp.add)
        col_sum[t] = col_sum[t] + (e[:, :LANES] + e[:, LANES:])
        row = jnp.sum(row, 0, keepdims=True)
        put(p, d, jnp.log2(row) - f)
        return jnp.minimum(least, row), jnp.maximum(most, row)

    def pairs(n, carry):
        ps = [unroll * n + u for u in range(unroll)]
        fs = starts(ps)
        for u in range(unroll):
            carry = pair(ps[u], fs[u], *carry)
        return carry

    def lanes(t, carry):
        least, most = carry
        halves = []
        for k in range(2):
            block = jnp.transpose(col_sum[t, k * LANES : (k + 1) * LANES, :])
            halves.append(jnp.sum(block, 0, keepdims=True))
        s = jnp.concatenate(halves, 0)
        sums_out[pl.ds(pl.multiple_of(2 * t, 2), 2), :] = jnp.log2(s)
        sums_out[pl.ds(2 * blocks + t, 1), :] = jnp.full((1, LANES), count[t].astype(jnp.float32))
        return jnp.minimum(least, jnp.where(count[t] > 0, s, LARGE)), jnp.maximum(most, s)

    least = jnp.full((1, BLK), LARGE, jnp.float32)
    most = jnp.zeros((1, BLK), jnp.float32)
    least, most = lax.fori_loop(0, (used + unroll - 1) // unroll, pairs, (least, most))
    low = jnp.full((2, LANES), LARGE, jnp.float32)
    high = jnp.zeros((2, LANES), jnp.float32)
    low, high = lax.fori_loop(0, blocks, lanes, (low, high), unroll=BLOCKS)
    smallest = jnp.minimum(jnp.min(least), jnp.min(low))
    largest = jnp.maximum(jnp.max(most), jnp.max(high))
    fits = (smallest >= SMALL) & (largest <= LARGE)

    @pl.when(jnp.logical_not(fits))
    def _():
        def fill(t, carry):
            col_sum[t] = jnp.zeros((BLK, LANES), jnp.float32)
            col_top[t] = jnp.full((BLK, LANES), -1e30, jnp.float32)
            return carry

        lax.fori_loop(0, blocks + 1, fill, 0)

        def pair(n, carry):
            p = n
            t, d, f, z = product(p, starts([p])[0])
            top = jnp.max(z, 0, keepdims=True)
            put(p, d, top + jnp.log2(jnp.sum(jnp.exp2(z - top), 0, keepdims=True)) - f)
            a, b = z[:, :LANES], z[:, LANES:]
            old = col_top[t]
            new = jnp.maximum(old, jnp.maximum(a, b))
            col_sum[t] = col_sum[t] * jnp.exp2(old - new) + (jnp.exp2(a - new) + jnp.exp2(b - new))
            col_top[t] = new
            return carry

        lax.fori_loop(0, used, pair, 0)

        def lanes(t, carry):
            for k in range(2):
                rows = slice(k * LANES, (k + 1) * LANES)
                top = jnp.transpose(col_top[t, rows, :])
                most = jnp.max(top, 0, keepdims=True)
                s = jnp.sum(jnp.transpose(col_sum[t, rows, :]) * jnp.exp2(top - most), 0, keepdims=True)
                sums_out[pl.ds(2 * t + k, 1), :] = most + jnp.log2(s)
            return carry

        lax.fori_loop(0, blocks, lanes, 0)


def fine_update(where, stacks, points, clusters, f_table, g_table, slots_each, stride):
    senders = sum(stack.shape[0] for stack in stacks)
    blocks = 2 * TB_DEV
    return pl.pallas_call(
        functools.partial(fine_kernel, len(stacks), slots_each, stride),
        out_shape=(
            jax.ShapeDtypeStruct((senders, 1, 2 * slots_each * BLK), jnp.float32),
            jax.ShapeDtypeStruct((3 * blocks + 2 * TB_DEV + F, LANES), jnp.float32),
        ),
        in_specs=[SMEM] + [pl.BlockSpec(memory_space=pl.ANY)] * len(stacks) + [VMEM] * 6,
        out_specs=(VMEM, VMEM),
        scratch_shapes=[
            pltpu.VMEM((senders, SLOT_AT, LANES), jnp.float32),
            pltpu.VMEM((senders, 8, LANES), jnp.float32),
            pltpu.VMEM((2 * blocks, LANES), jnp.float32),
            pltpu.VMEM((blocks + 1, BLK, LANES), jnp.bfloat16),
            pltpu.VMEM((blocks + 1, BLK, LANES), jnp.float32),
            pltpu.VMEM((blocks + 1, BLK, LANES), jnp.float32),
            pltpu.VMEM((senders, LANES), jnp.int32),
            pltpu.SemaphoreType.DMA((2 * len(stacks) + 1,)),
            pltpu.SMEM((senders, LANES), jnp.int32),
            pltpu.SMEM((blocks + 1,), jnp.int32),
        ]
        + [pltpu.SMEM((senders * 2 * slots_each,), jnp.int32)] * 4,
        compiler_params=pltpu.CompilerParams(vmem_limit_bytes=(28 + senders // 8) * MIB),
        name="fine",
    )(where, *stacks, *points, *clusters, f_table, g_table)


def finish_kernel(place_ref, own, other, partial, fine_f_out, fine_g_out, gathered):
    rows = 2 * TB_DEV
    a, b = own[0:rows, :], other[rows : 2 * rows, :]
    top = jnp.maximum(a, b)
    lse = top + jnp.log2(jnp.exp2(a - top) + jnp.exp2(b - top))
    counts = 2 * rows
    g = own[3 * rows : 4 * rows, :]
    named = own[counts : counts + TB_DEV, :] + other[counts + TB_DEV : counts + 2 * TB_DEV, :]
    logs = EPS * jnp.log(named * float(BLK))
    base = g - (lse * (1.0 / SCALE) - g)
    for t in range(TB_DEV):
        span = slice(2 * t, 2 * t + 2)
        fine_g_out[span, :] = 0.5 * (base[span, :] + logs[t : t + 1, :])
    for block in range(SB_DEV):
        for k in range(SUPP):
            n = block * SUPP + k
            span = pl.ds(pl.multiple_of(place_ref[1, n], BLK), BLK)
            gathered[k, block : block + 1, :] = partial[place_ref[0, n], :, span]
    values = gathered[...]
    top = jnp.max(values, 0)
    lse = top + jnp.log2(jnp.sum(jnp.exp2(values - top[None]), 0))
    term = EPS * math.log(float(SUPP * BLK)) - lse * (1.0 / SCALE)
    for block in range(SB_DEV):
        for k in range(2):
            row = slice(2 * block + k, 2 * block + k + 1)
            piece = term[block : block + 1, k * LANES : (k + 1) * LANES]
            start_f = own[8 * TB_DEV + 2 * block + k : 8 * TB_DEV + 2 * block + k + 1, :]
            fine_f_out[row, :] = 0.5 * (start_f + piece)


def finish(places, own, other, partial):
    return pl.pallas_call(
        finish_kernel,
        out_shape=(
            jax.ShapeDtypeStruct((F, LANES), jnp.float32),
            jax.ShapeDtypeStruct((2 * TB_DEV, LANES), jnp.float32),
        ),
        in_specs=[SMEM] + [VMEM] * 3,
        out_specs=(VMEM, VMEM),
        scratch_shapes=[pltpu.VMEM((SUPP, SB_DEV, BLK), jnp.float32)],
        name="finish",
    )(places, own, other, partial)


def exchange(x, axis, flip):
    count = lax.axis_size(axis)
    return lax.ppermute(x, axis, [(i, i ^ flip) for i in range(count)])


def on_device(
    src_cent, tgt_cent, src_mass, tgt_mass, src_pts, tgt_pts, src_cluster, tgt_cluster, support
):
    n_row, n_chip, n_core = (lax.axis_size(axis) for axis in AXES)
    devices = n_row * n_chip * n_core
    row, chip, core = (lax.axis_index(axis) for axis in AXES)

    flat_mass = tgt_mass.reshape(-1, LANES)
    tgt = [tgt_cent, flat_mass, exchange(tgt_cent, "core", 1), exchange(flat_mass, "core", 1)]

    tgt_cluster = tgt_cluster.reshape(2 * TB_DEV, LANES)
    requests_each = SB_DEV * SUPP
    slots_each = requests_each // devices + 1
    stride = 1 << (slots_each - 1).bit_length()
    bundle, src_own, places = prepare(
        support.reshape(1, requests_each),
        src_pts,
        src_cluster.reshape(F, LANES),
        src_cent,
        src_mass.reshape(-1, LANES),
        tgt,
        devices,
        slots_each,
        stride,
    )
    along = [bundle] + [exchange(bundle, "chip", k) for k in range(1, n_chip)]
    src_all = [src_own] + [exchange(src_own, "row", k) for k in range(1, 3)]
    src_own, src_all[1] = lax.optimization_barrier((src_own, src_all[1]))
    src_all += [exchange(src_own, "row", k) for k in range(3, n_row)]
    stack = jnp.stack([part[:TGT_AT] for part in along])
    src_all, along, stack = lax.optimization_barrier((src_all, along, stack))
    stacks = [stack] + [exchange(stack, "row", k) for k in range(1, n_row)]
    f_table, g_table = coarse_duals(src_all, along)
    tgt_pts, tgt_cluster, f_table, g_table = lax.optimization_barrier(
        (tgt_pts, tgt_cluster, f_table, g_table)
    )
    points = [tgt_pts, exchange(tgt_pts, "core", 1)]
    clusters = [tgt_cluster, exchange(tgt_cluster, "core", 1)]
    coarse_f = f_table[0, : src_cent.shape[1]]
    coarse_g = g_table[0, : tgt_cent.shape[1]]

    col = chip * n_core + core
    where = [row * n_chip + chip, core, row * src_cent.shape[1], col * tgt_cent.shape[1]]
    partial, kept = fine_update(
        jnp.stack(where).astype(jnp.int32),
        stacks,
        points,
        clusters,
        f_table,
        g_table,
        slots_each,
        stride,
    )
    returned = lax.all_to_all(partial, CHIPS, split_axis=0, concat_axis=0, tiled=True)
    other = exchange(kept, "core", 1)
    fine_f, fine_g = finish(places, kept, other, returned)
    return coarse_f, coarse_g, fine_f.reshape(-1), fine_g.reshape(-1)


def solution(mesh):
    n_row, n_col = mesh.devices.shape
    cores = jax.sharding.Mesh(mesh.devices.reshape(n_row, n_col // 2, 2), AXES)
    col = CHIPS[1:] + AXES[2:]
    in_specs = (
        P(None, "row"),
        P(None, col),
        P("row"),
        P(col),
        P(None, AXES),
        P(None, AXES),
        P(AXES),
        P(AXES),
        P(AXES, None),
    )
    out_specs = (P("row"), P(col), P(AXES), P(AXES))
    return jax.shard_map(
        on_device, mesh=cores, in_specs=in_specs, out_specs=out_specs, check_vma=False
    )
```
